32 devices in a mesh: sec: 4 (over z), blk: 8 (over y, x, core).
Axes of the slice: x: 2, y: 2, z: 4, core: 2. Of those that a mesh axis runs over, the one named last changes fastest.
Arguments:
- wavefunction: bfloat16 [4, 96, 128, 128], P('sec', 'blk')
- left_env: bfloat16 [4, 20, 96, 128, 128], P('sec', None, 'blk')
- right_env: bfloat16 [4, 20, 96, 128, 128], P('sec', None, 'blk')
- row_offset: int32 [4, 12], P('sec'), may hold values from 0 to 7, as said below
- sector_dims: int32 [4, 96, 2], P('sec', 'blk'), may hold values from 64 to 128
- trunc_ranks: int32 [4, 96], P('sec', 'blk'), may hold values from 32 to 128
Outputs:
- state_new: bfloat16 [4, 96, 128, 128], P('sec', 'blk')
- hstate_new: bfloat16 [4, 96, 128, 128], P('sec', 'blk')
- energy: float32 [4], P('sec')
- next_left: bfloat16 [4, 20, 96, 128, 128], P('sec', None, 'blk')
The draws below stay inside these ranges and needn't reach their ends.
Inputs may be any that keep to these rules, and one draw needn't show every extreme that they name: The sector with up-charge u and down-charge e is stored in slot u of device (e + row_offset[u]) mod 8; in every section the offsets of some two adjacent up-charges differ by 8 / 2 modulo 8.
All inputs are finite; a program needn't handle non-finite values.
Results may differ from the reference program's by a relative error of at most 0.0067.
Values may be sent and summed in bfloat16 or wider, within the bound.
No kernel may reach another device: no remote copies, remote signals or barrier semaphores. Data moves between devices by JAX's collectives and lax.ppermute only.
A program may use at most 128 MiB of HBM per device.

```python
import math
import jax
import jax.numpy as jnp

SB = 128
NW = 20
Q_DEV = 12
NSEC = 4
NQ = 96
N_BLK = 8


def draw_wavefunction(key, part):
    key_block, key_row, key_col, key_base = jax.random.split(key, 4)
    slots = jnp.arange(NQ, dtype=jnp.int32)
    device = (slots // Q_DEV).astype(jnp.float32)
    rising = 1.0 + 2.0 * device / float(max(N_BLK - 1, 1))
    block_scale = jnp.exp(jax.random.uniform(key_block, (NSEC, NQ, 1, 1), jnp.float32) * math.log(10.0))
    block_scale = block_scale * rising[None, :, None, None]
    row_scale = jnp.exp(jax.random.uniform(key_row, (NSEC, NQ, SB, 1), jnp.float32) * math.log(3.0))
    col_scale = jnp.exp(jax.random.uniform(key_col, (NSEC, NQ, 1, SB), jnp.float32) * math.log(3.0))
    base = jax.random.normal(key_base, (NSEC, NQ, SB, SB), jnp.float32)
    return (base * block_scale * row_scale * col_scale).astype(jnp.bfloat16)


def environment_draw(key):
    key_noise, key_diag = jax.random.split(key, 2)
    slots = jnp.arange(NQ, dtype=jnp.int32)
    device = (slots // Q_DEV).astype(jnp.float32) / float(max(N_BLK - 1, 1))
    noise = jax.random.normal(key_noise, (NSEC, NW, NQ, SB, SB), jnp.float32)
    rising = 0.5 + device
    noise = noise / math.sqrt(float(SB))
    jitter = jax.random.uniform(key_diag, (NSEC, NW, NQ, 1, 1), jnp.float32, 0.8, 1.25)
    channel_on = (jnp.arange(NW, dtype=jnp.int32) % 5 == 0).astype(jnp.float32)
    lines = jnp.arange(SB, dtype=jnp.int32)
    identity = (lines[:, None] == lines[None, :]).astype(jnp.float32)
    diag = channel_on[None, :, None, None, None] * rising[None, None, :, None, None] * jitter * identity[None, None, None, :, :]
    return (noise + diag).astype(jnp.bfloat16)


def draw_left_env(key, part):
    return environment_draw(jax.random.fold_in(key, 31))


def draw_right_env(key, part):
    return environment_draw(jax.random.fold_in(key, 37))


def draw_row_offset(key, part):
    key_first, key_step, key_place = jax.random.split(jax.random.fold_in(key, 17), 3)
    first = jax.random.randint(key_first, (NSEC, 1), 0, N_BLK, dtype=jnp.int32)
    steps = jax.random.randint(key_step, (NSEC, Q_DEV - 1), 0, N_BLK, dtype=jnp.int32)
    place = jax.random.randint(key_place, (NSEC, 1), 0, Q_DEV - 1, dtype=jnp.int32)
    columns = jnp.arange(Q_DEV - 1, dtype=jnp.int32)[None, :]
    steps = jnp.where(columns == place, jnp.int32(N_BLK // 2), steps)
    offsets = jnp.concatenate([first, first + jnp.cumsum(steps, axis=1, dtype=jnp.int32)], axis=1)
    return (offsets % N_BLK).astype(jnp.int32)


def touch_ends(entries, own_key, least, largest):
    index_at = [jax.random.randint(jax.random.fold_in(own_key, axis), (), 0, length) for axis, length in enumerate(entries.shape)]
    longest = entries.shape.index(max(entries.shape))
    beside = index_at[:longest] + [(index_at[longest] + 1) % entries.shape[longest]] + index_at[longest + 1:]
    return entries.at[tuple(index_at)].set(least).at[tuple(beside)].set(largest)


def setup_inputs(seed: int = 0) -> dict:
    key_list = jax.random.split(jax.random.key(seed), 7)
    return {
        "wavefunction": draw_wavefunction(jax.random.fold_in(key_list[6], 71), 0),
        "left_env": draw_left_env(jax.random.fold_in(key_list[6], 71), 0),
        "right_env": draw_right_env(jax.random.fold_in(key_list[6], 71), 0),
        "row_offset": draw_row_offset(jax.random.fold_in(key_list[6], 71), 0),
        "sector_dims": touch_ends(jax.random.randint(key_list[4], (NSEC, NQ, 2), SB // 2, SB + 1), jax.random.fold_in(key_list[4], 1), SB // 2, SB).astype(jnp.int32),
        "trunc_ranks": touch_ends(jax.random.randint(key_list[5], (NSEC, NQ), SB // 4, SB + 1), jax.random.fold_in(key_list[5], 1), SB // 4, SB).astype(jnp.int32),
    }


def source_slots(offsets):
    slots = jnp.arange(NQ, dtype=jnp.int32)
    device = slots // Q_DEV
    up_val = slots % Q_DEV
    own_off = jnp.take(offsets, up_val)
    prev_off = jnp.take(offsets, (up_val - 1) % Q_DEV)
    next_off = jnp.take(offsets, (up_val + 1) % Q_DEV)
    down_val = (device - own_off) % N_BLK
    row_lo = jnp.clip(up_val - 1, 0, Q_DEV - 1)
    row_hi = jnp.clip(up_val + 1, 0, Q_DEV - 1)
    sources = [slots, (down_val + prev_off) % N_BLK * Q_DEV + row_lo, (down_val + next_off) % N_BLK * Q_DEV + row_hi, (device - 1) % N_BLK * Q_DEV + up_val, (device + 1) % N_BLK * Q_DEV + up_val]
    exists = [slots >= 0, up_val >= 1, up_val <= Q_DEV - 2, down_val >= 1, down_val <= N_BLK - 2]
    return ([s.astype(jnp.int32) for s in sources], exists)

def picked_blocks(state, sources, exists):
    result = []
    for ctype in range(5):
        taken = jnp.take(state, sources[ctype], axis=0)
        result.append(jnp.where(exists[ctype][:, None, None], taken, jnp.zeros_like(taken)))
    return result

def apply_ham(state, lenv, renv, sources, exists, mask):
    blocks = picked_blocks(state, sources, exists)
    total = jnp.zeros(state.shape, jnp.float32)
    for ctype in range(5):
        inner = jnp.einsum('wtab,tbc->wtac', lenv[ctype::5].astype(jnp.float32), blocks[ctype].astype(jnp.float32)).astype(jnp.bfloat16)
        total = total + jnp.einsum('wtac,wtdc->tad', inner.astype(jnp.float32), renv[ctype::5].astype(jnp.float32))
    return total * mask

def env_update(kept, lenv, sources, exists):
    blocks = picked_blocks(kept, sources, exists)
    parts = []
    for ctype in range(5):
        inner = jnp.einsum('wtab,tbc->wtac', lenv[ctype::5].astype(jnp.float32), blocks[ctype].astype(jnp.float32)).astype(jnp.bfloat16)
        parts.append(jnp.einsum('tba,wtbc->wtac', kept.astype(jnp.float32), inner.astype(jnp.float32)).astype(jnp.bfloat16))
    stacked = jnp.stack(parts, axis=1)
    return stacked.reshape((NW, NQ, SB, SB))

def reference(wavefunction, left_env, right_env, row_offset, sector_dims, trunc_ranks):
    cells = float(NQ * SB * SB)
    lines = jnp.arange(SB, dtype=jnp.int32)
    states, hstates, energies, updates = ([], [], [], [])
    for section in range(NSEC):
        sources, exists = source_slots(row_offset[section])
        dims = sector_dims[section]
        mask_on = (lines[None, :, None] < dims[:, 0][:, None, None]) & (lines[None, None, :] < dims[:, 1][:, None, None])
        mask = mask_on.astype(jnp.float32)
        lenv = left_env[section]
        renv = right_env[section]
        start = wavefunction[section]
        vzero = jnp.where(mask_on, start, jnp.zeros_like(start))
        hzero = apply_ham(vzero, lenv, renv, sources, exists, mask)
        vzero_f = vzero.astype(jnp.float32)
        nzero = jnp.sum(vzero_f * vzero_f)
        pzero = jnp.sum(vzero_f * hzero)
        scale = jnp.sqrt(cells / nzero)
        uzero = vzero_f * scale
        huzero = hzero * scale
        a_zero = pzero / nzero
        resid = huzero - a_zero * uzero
        beta = jnp.sqrt(jnp.sum(resid * resid) / cells + 1e-06)
        vone = (resid / beta).astype(jnp.bfloat16)
        hone = apply_ham(vone, lenv, renv, sources, exists, mask)
        a_one = jnp.sum(vone.astype(jnp.float32) * hone) / cells
        half_gap = (a_zero - a_one) / 2.0
        ritz = (a_zero + a_one) / 2.0 - jnp.sqrt(half_gap * half_gap + beta * beta)
        gap_val = ritz - a_zero
        length = jnp.sqrt(beta * beta + gap_val * gap_val)
        xcoef = beta / length
        ycoef = gap_val / length
        state_new = (xcoef * uzero + ycoef * vone.astype(jnp.float32)).astype(jnp.bfloat16)
        hstate_new = (xcoef * huzero + ycoef * hone).astype(jnp.bfloat16)
        kept_on = lines[None, None, :] < trunc_ranks[section][:, None, None]
        kept = jnp.where(kept_on, state_new, jnp.zeros_like(state_new))
        updates.append(env_update(kept, lenv, sources, exists))
        states.append(state_new)
        hstates.append(hstate_new)
        energies.append(ritz)
    next_left = jnp.stack([left_env[0]] + updates[:-1], axis=0)
    return (jnp.stack(states, 0), jnp.stack(hstates, 0), jnp.stack(energies, 0).astype(jnp.float32), next_left)
```

```python
import functools

import jax
import jax.numpy as jnp
from jax import lax
from jax.experimental import pallas as pl
from jax.experimental.pallas import tpu as pltpu
from jax.sharding import PartitionSpec as P

GROUPS = 5
EARLY = (1, 2)
LATE = (0, 3, 4)
EXTRA = 16
SLACK = 128
VMEM = 56 * 1024 * 1024
F32 = jnp.float32
BF16 = jnp.bfloat16


def params():
    return pltpu.CompilerParams(vmem_limit_bytes=VMEM)


def exchange(value, bit):
    length = lax.axis_size("blk")
    return lax.ppermute(value, "blk", [(i, i ^ bit) for i in range(length)])


def onward(value):
    length = lax.axis_size("sec")
    return lax.ppermute(value, "sec", [(i, i + 1) for i in range(length - 1)])


def gathered(value):
    nblk = lax.axis_size("blk")
    if nblk == 8:
        rows = value.shape[0]
        half = rows // 2 // 16 * 16
        four, two, one = exchange(value, 4), exchange(value, 2), exchange(value, 1)
        six_a, six_b = exchange(two[:half], 4), exchange(four[half:], 2)
        three, five = exchange(two, 1), exchange(four, 1)
        seven_a, seven_b = exchange(six_a, 1), exchange(six_b, 1)
        return [
            (value, 0, 0), (one, 1, 0), (two, 2, 0), (three, 3, 0), (four, 4, 0), (five, 5, 0),
            (six_a, 6, 0), (six_b, 6, half), (seven_a, 7, 0), (seven_b, 7, half),
        ]
    held = {0: value}
    bit = 1
    while bit < nblk:
        held.update({place | bit: exchange(rows, bit) for place, rows in list(held.items())})
        bit *= 2
    return [(held[place], place, 0) for place in range(nblk)]


def extras_of(pieces, nblk, body):
    found = [None] * nblk
    for rows, place, first in pieces:
        if first + rows.shape[0] == body + EXTRA:
            found[place] = rows[rows.shape[0] - EXTRA :]
    return jnp.stack(found)


def load_pieces(places, refs, scratch, sem):
    copies = []
    for (place, first), ref in zip(places, refs):
        copies.append(
            pltpu.make_async_copy(ref, scratch.at[place, pl.ds(first, ref.shape[0])], sem.at[len(copies)])
        )
    for copy in copies:
        copy.start()
    return copies


def block_of(scratch, entry, count, width):
    place = entry // count
    slot = entry - place * count
    return scratch[place, pl.ds(pl.multiple_of(slot * width, width), width), :]


def ham_sum(x, lref, rref):
    kinds = lref.shape[0] // GROUPS
    zero = jnp.zeros_like(x[0])
    width = zero.shape[0]
    total = jnp.zeros((width, width), F32)
    flip = (((1,), (1,)), ((), ()))
    for c0, c1 in ((0, 1), (2, 3)):
        both = jnp.concatenate(
            [jnp.concatenate([x[c0], zero], 1), jnp.concatenate([zero, x[c1]], 1)], 0
        )
        left = jnp.concatenate(
            [jnp.concatenate([lref[GROUPS * k + c0, 0], lref[GROUPS * k + c1, 0]], 1) for k in range(kinds)], 0
        )
        inner = jnp.dot(left, both, preferred_element_type=F32).astype(BF16)
        for k in range(kinds):
            right = jnp.concatenate([rref[GROUPS * k + c0, 0], rref[GROUPS * k + c1, 0]], 1)
            total += lax.dot_general(
                inner[width * k : width * (k + 1)], right, flip, preferred_element_type=F32
            )
    left = jnp.concatenate([lref[GROUPS * k + 4, 0] for k in range(kinds)], 0)
    inner = jnp.dot(left, x[4], preferred_element_type=F32).astype(BF16)
    inner = jnp.concatenate([inner[width * k : width * (k + 1)] for k in range(kinds)], 1)
    right = jnp.concatenate([rref[GROUPS * k + 4, 0] for k in range(kinds)], 1)
    return total + lax.dot_general(inner, right, flip, preferred_element_type=F32)


def inside(rows, cols, shape):
    row = lax.broadcasted_iota(jnp.int32, shape, 0)
    col = lax.broadcasted_iota(jnp.int32, shape, 1)
    return (row < rows) & (col < cols)


def total_of(value):
    return jnp.sum(jnp.sum(value, axis=0, keepdims=True), axis=1, keepdims=True)


def first_kernel(places, count, idx, there, dims, *refs):
    pieces = refs[: len(places)]
    lref, rref, href, payload, held, ext, sem = refs[len(places) :]
    t = pl.program_id(0)
    width = href.shape[1]

    @pl.when(t == 0)
    def _():
        copies = load_pieces(places, pieces, held, sem)
        ext[...] = jnp.zeros_like(ext)
        for copy in copies:
            copy.wait()

    x = []
    for c in range(GROUPS):
        block = block_of(held, idx[c, t], count, width)
        x.append(jnp.where(there[c, t] > 0, block, jnp.zeros_like(block)))
    total = ham_sum(x, lref, rref)
    h = jnp.where(inside(dims[t, 0], dims[t, 1], (width, width)), total, 0.0)
    href[0] = h
    v = x[0].astype(F32)
    norm, num = total_of(v * v), total_of(v * h)
    alpha = jnp.where(norm > 1e-30, num / jnp.maximum(norm, 1e-30), 0.0).astype(BF16).astype(F32)
    payload[pl.ds(pl.multiple_of(t * width, width), width), :] = (h - alpha * v).astype(BF16)
    row = lax.broadcasted_iota(jnp.int32, ext.shape, 0)
    lane = lax.broadcasted_iota(jnp.int32, ext.shape, 1)
    now = jnp.where(row == t, alpha, ext[...])
    now = now + jnp.where(row == count, norm, 0.0) + jnp.where(row == count + 1, num, 0.0)
    ext[...] = now

    @pl.when(t == count - 1)
    def _():
        high = now.astype(BF16).astype(F32)
        rest = now - high
        mid = rest.astype(BF16).astype(F32)
        low = rest - mid
        split = jnp.where(lane == 0, high, jnp.where(lane == 1, mid, jnp.where(lane == 2, low, 0.0)))
        payload[pl.ds(count * width, EXTRA), :] = jnp.where(row < count, now, split).astype(BF16)


def second_kernel(places, count, cells, idx, there, dims, *refs):
    n = len(places)
    vpieces, rpieces = refs[:n], refs[n : 2 * n]
    lref, rref, gref, sums, vsrc, wsrc, vheld, rheld, ext, vsem, rsem = refs[2 * n :]
    t = pl.program_id(0)
    width = gref.shape[1]
    nblk = vheld.shape[0]
    srow = lax.broadcasted_iota(jnp.int32, sums.shape, 0)

    @pl.when(t == 0)
    def _():
        copies = load_pieces(places, vpieces, vheld, vsem) + load_pieces(places, rpieces, rheld, rsem)
        for copy in copies:
            copy.wait()
        both = jnp.zeros((EXTRA, 128), F32)
        for place in range(nblk):
            part = rheld[place, pl.ds(count * width, EXTRA), :].astype(F32)
            ext[pl.ds(place * EXTRA, EXTRA), :] = part
            both = both + part
        both = jnp.sum(both, axis=1, keepdims=True)
        norm, num = both[count : count + 1], both[count + 1 : count + 2]
        sums[...] = jnp.where(srow == 2, num / norm, jnp.where(srow == 3, jnp.sqrt(cells / norm), 0.0))

    a_zero, scale = sums[2:3, :], sums[3:4, :]
    x = []
    squares = None
    for c in range(GROUPS):
        entry = idx[c, t]
        on = there[c, t] > 0
        place = entry // count
        v = block_of(vheld, entry, count, width)
        r = block_of(rheld, entry, count, width).astype(F32)
        alpha = ext[pl.ds(place * EXTRA + (entry - place * count), 1), :]
        w = scale * (r + (alpha - a_zero) * v.astype(F32))
        if c == 0:
            squares = total_of(w * w)
        w = jnp.where(on, w, 0.0).astype(BF16)
        x.append(w)
        if c in LATE:
            vsrc[LATE.index(c), 0] = jnp.where(on, v, jnp.zeros_like(v))
            wsrc[LATE.index(c), 0] = w
    total = ham_sum(x, lref, rref)
    g = jnp.where(inside(dims[t, 0], dims[t, 1], (width, width)), total, 0.0)
    gref[0] = g
    num = total_of(x[0].astype(F32) * g)
    sums[...] += jnp.where(srow == 0, squares, jnp.where(srow == 1, num, 0.0))


def pack_kernel(caps, src_caps, starts, coefs, vsrc, wsrc, lref, out, acc):
    t = pl.program_id(0)
    width = vsrc.shape[2]
    kinds = lref.shape[0]
    lane = lax.broadcasted_iota(jnp.int32, (width, width), 1)
    kept = []
    for i, c in enumerate(LATE):
        state = (coefs[0] * vsrc[i, 0].astype(F32) + coefs[1] * wsrc[i, 0].astype(F32)).astype(BF16)
        kept.append(jnp.where(lane < src_caps[c, t], state, jnp.zeros_like(state)))
    own = jnp.where(lane < caps[t], kept[0].astype(F32), 0.0).T.astype(BF16)
    at = jnp.int32(0)
    for i, c in enumerate(LATE):
        left = jnp.concatenate([lref[k, c, 0] for k in range(kinds)], 0)
        inner = jnp.dot(left, kept[i], preferred_element_type=F32).astype(BF16)
        inner = jnp.concatenate([inner[width * k : width * (k + 1)] for k in range(kinds)], 1)
        update = jnp.dot(own, inner, preferred_element_type=F32)
        for k in range(kinds):
            tile = at // width
            lead = at - tile * width
            turned = pltpu.roll(update[:, width * k : width * (k + 1)], lead, 1)
            acc[tile] = jnp.where(lane >= lead, turned, acc[tile])
            acc[tile + 1] = turned
            at = at + src_caps[c, t]
    high = (caps[t] + 15) // 16 * 16

    def flush(tile, carry):
        first = pl.multiple_of(starts[t] + tile * high, 16)
        out[pl.ds(first, width), :] = acc[tile].astype(BF16)
        return carry

    lax.fori_loop(0, (at + width - 1) // width, flush, 0)


def unpack_kernel(caps, src_caps, starts, first_sec, packed, lenv, so_far, out):
    del so_far
    t, g = pl.program_id(0), pl.program_id(1)
    width = out.shape[3]
    kinds = out.shape[0]

    @pl.when(first_sec[0] == 1)
    def _():
        out[...] = lenv[...]

    @pl.when(first_sec[0] == 0)
    def _():
        lane = lax.broadcasted_iota(jnp.int32, (width, width), 1)
        caps_g = [src_caps[c, t] for c in LATE]
        mine = caps_g[-1]
        at = jnp.int32(0)
        for i in range(len(LATE) - 1):
            mine = jnp.where(g == i, caps_g[i], mine)
            at = at + jnp.where(g > i, kinds * caps_g[i], 0)
        high = (caps[t] + 15) // 16 * 16
        valid = inside(caps[t], mine, (width, width))
        for k in range(kinds):
            tile = jnp.where(mine > 0, at // width, 0)
            lead = at - at // width * width
            low = packed[pl.ds(pl.multiple_of(starts[t] + tile * high, 16), width), :]
            upper = packed[pl.ds(pl.multiple_of(starts[t] + (tile + 1) * high, 16), width), :]
            both = jnp.where(lane >= lead, low.astype(F32), upper.astype(F32))
            both = pltpu.roll(both, width - lead, 1)
            out[k, 0, 0] = jnp.where(valid, both, 0.0).astype(BF16)
            at = at + mine


def early_kernel(places, count, idx, there, first_sec, *refs):
    pieces = refs[: len(places)]
    one, two, lenv, out, held, sem = refs[len(places) :]
    t, g = pl.program_id(0), pl.program_id(1)
    width = out.shape[3]
    kinds = out.shape[0]

    @pl.when((t == 0) & (g == 0))
    def _():
        for copy in load_pieces(places, pieces, held, sem):
            copy.wait()

    @pl.when(first_sec[0] == 1)
    def _():
        out[...] = lenv[...]

    for i, c in enumerate(EARLY):
        here = there[c, t] > 0

        @pl.when((first_sec[0] == 0) & (g == i) & jnp.logical_not(here))
        def _():
            out[...] = jnp.zeros_like(out)

        @pl.when((first_sec[0] == 0) & (g == i) & here)
        def _():
            sent = (one, two)[i]
            own = block_of(held, idx[0, t], count, width).astype(F32).T.astype(BF16)
            kept = block_of(held, idx[c, t], count, width)
            left = jnp.concatenate([sent[k, 0] for k in range(kinds)], 0)
            inner = jnp.dot(left, kept, preferred_element_type=F32).astype(BF16)
            inner = jnp.concatenate([inner[width * k : width * (k + 1)] for k in range(kinds)], 1)
            update = jnp.dot(own, inner, preferred_element_type=F32).astype(BF16)
            for k in range(kinds):
                out[k, 0, 0] = update[:, width * k : width * (k + 1)]


def whole(shape):
    return pl.BlockSpec(shape, lambda *a: (0,) * len(shape))


def shards(wavefunction, left_env, right_env, row_offset, sector_dims, trunc_ranks):
    start, lenv, renv = wavefunction[0], left_env[0], right_env[0]
    offsets, dims, ranks = row_offset[0], sector_dims[0], trunc_ranks[0]
    count, width = start.shape[0], start.shape[1]
    channels = lenv.shape[0]
    kinds = channels // GROUPS
    nblk, device = lax.axis_size("blk"), lax.axis_index("blk")
    body = count * width
    cells = float(count * nblk * width * width)
    lines = jnp.arange(width, dtype=jnp.int32)
    first_sec = jnp.reshape((lax.axis_index("sec") == 0).astype(jnp.int32), (1,))
    by_group = lenv.reshape((kinds, GROUPS, count, width, width))

    up_val = jnp.arange(count, dtype=jnp.int32)
    down_val = (device - offsets) % nblk
    holders = jnp.stack(
        [
            jnp.broadcast_to(device, (count,)),
            (down_val + jnp.roll(offsets, 1)) % nblk,
            (down_val + jnp.roll(offsets, -1)) % nblk,
            jnp.broadcast_to((device - 1) % nblk, (count,)),
            jnp.broadcast_to((device + 1) % nblk, (count,)),
        ]
    )
    slots = jnp.stack(
        [up_val, jnp.maximum(up_val - 1, 0), jnp.minimum(up_val + 1, count - 1), up_val, up_val]
    )
    there = jnp.stack(
        [up_val >= 0, up_val >= 1, up_val <= count - 2, down_val >= 1, down_val <= nblk - 2]
    ).astype(jnp.int32)
    idx = ((holders ^ device) * count + slots).astype(jnp.int32)

    mask_on = (lines[None, :, None] < dims[:, 0][:, None, None]) & (
        lines[None, None, :] < dims[:, 1][:, None, None]
    )
    vzero = jnp.where(mask_on, start, jnp.zeros_like(start))
    caps = jnp.minimum(dims[:, 1], ranks)
    meta = jnp.zeros((EXTRA, width), BF16).at[0, :count].set(caps.astype(BF16))
    vpieces = gathered(jnp.concatenate([vzero.reshape((body, width)), meta]))
    sent_one = onward(by_group[:, 1, 1:])
    sent_two = onward(by_group[:, 2, : count - 1])
    places = tuple((place, first) for _, place, first in vpieces)
    n = len(places)
    anywhere = pl.BlockSpec(memory_space=pl.ANY)
    env = pl.BlockSpec((channels, 1, width, width), lambda t, *s: (0, t, 0, 0))
    slot_block = pl.BlockSpec((1, width, width), lambda t, *s: (t, 0, 0))
    held = pltpu.VMEM((nblk, body + EXTRA, width), BF16)
    ham_cost = pl.CostEstimate(
        flops=4 * channels * count * width**3,
        bytes_accessed=4 * channels * count * width**2 + 8 * body * width,
        transcendentals=0,
    )

    hzero, rpay = pl.pallas_call(
        functools.partial(first_kernel, places, count),
        grid_spec=pltpu.PrefetchScalarGridSpec(
            num_scalar_prefetch=3,
            grid=(count,),
            in_specs=[anywhere] * n + [env, env],
            out_specs=[slot_block, whole((body + EXTRA, width))],
            scratch_shapes=[held, pltpu.VMEM((EXTRA, 128), F32), pltpu.SemaphoreType.DMA((n,))],
        ),
        out_shape=[
            jax.ShapeDtypeStruct((count, width, width), F32),
            jax.ShapeDtypeStruct((body + EXTRA, width), BF16),
        ],
        compiler_params=params(),
        cost_estimate=ham_cost,
        name="ham_first",
    )(idx, there, dims, *[rows for rows, _, _ in vpieces], lenv, renv)

    rpieces = gathered(rpay)
    late_block = pl.BlockSpec((len(LATE), 1, width, width), lambda t, *s: (0, t, 0, 0))
    late_shape = jax.ShapeDtypeStruct((len(LATE), count, width, width), BF16)
    gone, sums, vsrc, wsrc = pl.pallas_call(
        functools.partial(second_kernel, places, count, cells),
        grid_spec=pltpu.PrefetchScalarGridSpec(
            num_scalar_prefetch=3,
            grid=(count,),
            in_specs=[anywhere] * (2 * n) + [env, env],
            out_specs=[slot_block, whole((8, 128)), late_block, late_block],
            scratch_shapes=[
                held,
                held,
                pltpu.VMEM((nblk * EXTRA, 128), F32),
                pltpu.SemaphoreType.DMA((n,)),
                pltpu.SemaphoreType.DMA((n,)),
            ],
        ),
        out_shape=[
            jax.ShapeDtypeStruct((count, width, width), F32),
            jax.ShapeDtypeStruct((8, 128), F32),
            late_shape,
            late_shape,
        ],
        compiler_params=params(),
        cost_estimate=ham_cost,
        name="ham_second",
    )(idx, there, dims, *[rows for rows, _, _ in vpieces], *[rows for rows, _, _ in rpieces], lenv, renv)

    all_caps = extras_of(vpieces, nblk, body)[:, 0, :count].astype(jnp.int32).reshape((-1,))
    src_caps = jnp.where(there > 0, jnp.take(all_caps, idx), 0).astype(jnp.int32)

    def layout(caps, src_caps):
        high = (caps + 15) // 16 * 16
        wide = (kinds * sum(src_caps[c] for c in LATE) + width - 1) // width
        ends = jnp.cumsum(high * wide)
        return ends - high * wide, ends[-1]

    starts, rows_used = layout(caps, src_caps)

    parts = lax.all_gather(
        jnp.where(jnp.arange(8)[:, None] == 4, rows_used.astype(F32), sums), "blk", axis=0
    )
    squares, num = jnp.sum(parts[:, 0, 0]) / cells, jnp.sum(parts[:, 1, 0]) / cells
    a_zero, scale = sums[2, 0], sums[3, 0]
    beta = jnp.sqrt(squares + 1e-06)
    a_one = num / (beta * beta)
    half_gap = (a_zero - a_one) / 2.0
    ritz = (a_zero + a_one) / 2.0 - jnp.sqrt(half_gap * half_gap + beta * beta)
    gap_val = ritz - a_zero
    length = jnp.sqrt(beta * beta + gap_val * gap_val)
    from_v, from_w = beta / length * scale, gap_val / length / beta
    state_new = (from_v * vzero.astype(F32) + from_w * wsrc[0].astype(F32)).astype(BF16)
    hstate_new = (from_v * hzero + from_w * gone).astype(BF16)
    kept = jnp.where(lines[None, None, :] < ranks[:, None, None], state_new, jnp.zeros_like(state_new))

    facts = jnp.concatenate([caps[None], src_caps, idx], axis=0).astype(BF16)
    facts = jnp.zeros((EXTRA, width), BF16).at[: facts.shape[0], :count].set(facts)
    passed = onward(jnp.concatenate([kept.reshape((body, width)), facts]))
    facts = passed[body:, :count].astype(jnp.int32)
    prev_caps, prev_src, prev_idx = facts[0], facts[1 : 1 + GROUPS], facts[1 + GROUPS : 1 + 2 * GROUPS]
    prev_starts, _ = layout(prev_caps, prev_src)

    tiles = kinds * len(LATE)
    most = count * tiles * width + SLACK
    coefs = jnp.stack([from_v, from_w])
    by_slot = pl.BlockSpec((kinds, GROUPS, 1, width, width), lambda t, *s: (0, 0, t, 0, 0))
    packed = pl.pallas_call(
        pack_kernel,
        grid_spec=pltpu.PrefetchScalarGridSpec(
            num_scalar_prefetch=3,
            grid=(count,),
            in_specs=[pl.BlockSpec(memory_space=pltpu.SMEM), late_block, late_block, by_slot],
            out_specs=whole((most, width)),
            scratch_shapes=[pltpu.VMEM((tiles + 2, width, width), F32)],
        ),
        out_shape=jax.ShapeDtypeStruct((most, width), BF16),
        compiler_params=params(),
        cost_estimate=pl.CostEstimate(
            flops=4 * tiles * count * width**3, bytes_accessed=4 * channels * count * width**2, transcendentals=0
        ),
        name="pack_update",
    )(caps, src_caps, starts, coefs, vsrc, wsrc, by_group)

    length = lax.axis_size("sec")
    needed = jnp.where(lax.axis_index("sec") == length - 1, 0.0, jnp.max(parts[:, 4, 0]))
    shift = 1
    while shift < length:
        turn = [(i, (i + shift) % length) for i in range(length)]
        needed = jnp.maximum(needed, lax.ppermute(jnp.full((8, 128), needed), "sec", turn)[0, 0])
        shift *= 2

    def env_block(pick):
        return pl.BlockSpec(
            (kinds, 1, 1, width, width), lambda t, g, *s: (0, pick(g), t, 0, 0)
        )

    def env_if_first(pick):
        return pl.BlockSpec(
            (kinds, 1, 1, width, width),
            lambda t, g, *s: (0, pick(g) * s[-1][0], t * s[-1][0], 0, 0),
        )

    def early_at(g):
        return g + EARLY[0]

    def late_at(g):
        return jnp.where(g == 0, LATE[0], g + LATE[1] - 1)

    out_shape = jax.ShapeDtypeStruct(by_group.shape, BF16)

    def finish(rows):
        def branch(packed, passed, sent_one, sent_two, prev_caps, prev_src, prev_idx, prev_starts, by_group):
            arrived = onward(packed[:rows])
            kpieces = gathered(passed)
            so_far = pl.pallas_call(
                functools.partial(early_kernel, places, count),
                grid_spec=pltpu.PrefetchScalarGridSpec(
                    num_scalar_prefetch=3,
                    grid=(count, len(EARLY)),
                    in_specs=[anywhere] * n
                    + [
                        pl.BlockSpec((kinds, 1, width, width), lambda t, g, *s: (0, jnp.maximum(t - 1, 0), 0, 0)),
                        pl.BlockSpec((kinds, 1, width, width), lambda t, g, *s: (0, jnp.minimum(t, count - 2), 0, 0)),
                        env_if_first(early_at),
                    ],
                    out_specs=env_block(early_at),
                    scratch_shapes=[held, pltpu.SemaphoreType.DMA((n,))],
                ),
                out_shape=out_shape,
                compiler_params=params(),
                cost_estimate=pl.CostEstimate(
                    flops=4 * kinds * len(EARLY) * count * width**3,
                    bytes_accessed=4 * kinds * len(EARLY) * count * width**2,
                    transcendentals=0,
                ),
                name="early_update",
            )(prev_idx, prev_src, first_sec, *[r for r, _, _ in kpieces], sent_one, sent_two, by_group)
            return pl.pallas_call(
                unpack_kernel,
                grid_spec=pltpu.PrefetchScalarGridSpec(
                    num_scalar_prefetch=4,
                    grid=(count, len(LATE)),
                    in_specs=[whole((rows, width)), env_if_first(late_at), anywhere],
                    out_specs=env_block(late_at),
                ),
                out_shape=out_shape,
                input_output_aliases={6: 0},
                compiler_params=params(),
                name="unpack_update",
            )(prev_caps, prev_src, prev_starts, first_sec, arrived, by_group, so_far)

        return branch

    sizes = [most * part // 16 // 16 * 16 for part in (5, 6, 7, 8, 10, 13)] + [most]
    tier = sum((needed + SLACK > size).astype(jnp.int32) for size in sizes[:-1])
    next_left = lax.switch(
        tier,
        [finish(size) for size in sizes],
        packed, passed, sent_one, sent_two, prev_caps, prev_src, prev_idx, prev_starts, by_group,
    )
    next_left = next_left.reshape((channels, count, width, width))
    return (state_new[None], hstate_new[None], jnp.reshape(ritz, (1,)), next_left[None])


def solution(mesh):
    placed = (
        P("sec", "blk", None, None),
        P("sec", None, "blk", None, None),
        P("sec", None, "blk", None, None),
        P("sec", None),
        P("sec", "blk", None),
        P("sec", "blk"),
    )
    return jax.shard_map(
        shards,
        mesh=mesh,
        in_specs=placed,
        out_specs=(
            P("sec", "blk", None, None),
            P("sec", "blk", None, None),
            P("sec"),
            P("sec", None, "blk", None, None),
        ),
        check_vma=False,
    )
```

```python
import functools

import jax
import jax.numpy as jnp
from jax import lax
from jax.experimental import pallas as pl
from jax.experimental.pallas import tpu as pltpu
from jax.sharding import PartitionSpec as P

GROUPS = 5
EARLY = (1, 2)
LATE = (0, 3, 4)
EXTRA = 16
SLACK = 128
VMEM = 32 * 1024 * 1024
F32 = jnp.float32
BF16 = jnp.bfloat16


def params():
    return pltpu.CompilerParams(vmem_limit_bytes=VMEM)


def exchange(value, bit):
    length = lax.axis_size("blk")
    return lax.ppermute(value, "blk", [(i, i ^ bit) for i in range(length)])


def onward(value):
    length = lax.axis_size("sec")
    return lax.ppermute(value, "sec", [(i, i + 1) for i in range(length - 1)])


def gathered(value):
    nblk = lax.axis_size("blk")
    if nblk == 8:
        rows = value.shape[0]
        half = rows // 2 // 16 * 16
        four, two, one = exchange(value, 4), exchange(value, 2), exchange(value, 1)
        six_a, six_b = exchange(two[:half], 4), exchange(four[half:], 2)
        three, five = exchange(two, 1), exchange(four, 1)
        seven_a, seven_b = exchange(six_a, 1), exchange(six_b, 1)
        return [
            (value, 0, 0), (one, 1, 0), (two, 2, 0), (three, 3, 0), (four, 4, 0), (five, 5, 0),
            (six_a, 6, 0), (six_b, 6, half), (seven_a, 7, 0), (seven_b, 7, half),
        ]
    held = {0: value}
    bit = 1
    while bit < nblk:
        held.update({place | bit: exchange(rows, bit) for place, rows in list(held.items())})
        bit *= 2
    return [(held[place], place, 0) for place in range(nblk)]


def extras_of(pieces, nblk, body):
    found = [None] * nblk
    for rows, place, first in pieces:
        if first + rows.shape[0] == body + EXTRA:
            found[place] = rows[rows.shape[0] - EXTRA :]
    return jnp.stack(found)


def load_pieces(places, refs, scratch, sem):
    copies = []
    for (place, first), ref in zip(places, refs):
        copies.append(
            pltpu.make_async_copy(ref, scratch.at[place, pl.ds(first, ref.shape[0])], sem.at[len(copies)])
        )
    for copy in copies:
        copy.start()
    return copies


def block_of(scratch, entry, count, width):
    place = entry // count
    slot = entry - place * count
    return scratch[place, pl.ds(pl.multiple_of(slot * width, width), width), :]


def ham_sum(x, t, lref, rref):
    kinds = lref.shape[0] // GROUPS
    zero = jnp.zeros_like(x[0])
    width = zero.shape[0]
    inner = [None] * lref.shape[0]
    for c0, c1 in ((0, 1), (2, 3)):
        both = jnp.concatenate(
            [jnp.concatenate([x[c0], zero], 1), jnp.concatenate([zero, x[c1]], 1)], 0
        )
        left = jnp.concatenate(
            [
                jnp.concatenate([lref[GROUPS * k + c0, t], lref[GROUPS * k + c1, t]], 1)
                for k in range(kinds)
            ],
            0,
        )
        pair = jnp.dot(left, both, preferred_element_type=F32).astype(BF16)
        for k in range(kinds):
            inner[GROUPS * k + c0] = pair[width * k : width * (k + 1), :width]
            inner[GROUPS * k + c1] = pair[width * k : width * (k + 1), width:]
    left = jnp.concatenate([lref[GROUPS * k + 4, t] for k in range(kinds)], 0)
    last = jnp.dot(left, x[4], preferred_element_type=F32).astype(BF16)
    for k in range(kinds):
        inner[GROUPS * k + 4] = last[width * k : width * (k + 1)]
    right = jnp.concatenate([rref[w, t] for w in range(lref.shape[0])], 1)
    return lax.dot_general(
        jnp.concatenate(inner, 1), right, (((1,), (1,)), ((), ())), preferred_element_type=F32
    )


def over_slots(count, body):
    per = max(p for p in (1, 2, 3, 4) if count % p == 0)

    def step(i, carry):
        for p in range(per):
            body(i * per + p)
        return carry

    lax.fori_loop(0, count // per, step, 0)


def inside(rows, cols, shape):
    row = lax.broadcasted_iota(jnp.int32, shape, 0)
    col = lax.broadcasted_iota(jnp.int32, shape, 1)
    return (row < rows) & (col < cols)


def total_of(value):
    return jnp.sum(jnp.sum(value, axis=0, keepdims=True), axis=1, keepdims=True)


def first_kernel(places, count, idx, there, dims, *refs):
    pieces = refs[: len(places)]
    lref, rref, href, payload, held, ext, sem = refs[len(places) :]
    width = href.shape[1]
    copies = load_pieces(places, pieces, held, sem)
    ext[...] = jnp.zeros_like(ext)
    for copy in copies:
        copy.wait()
    row = lax.broadcasted_iota(jnp.int32, ext.shape, 0)
    lane = lax.broadcasted_iota(jnp.int32, ext.shape, 1)

    def slot(t):
        x = []
        for c in range(GROUPS):
            block = block_of(held, idx[c, t], count, width)
            x.append(jnp.where(there[c, t] > 0, block, jnp.zeros_like(block)))
        h = jnp.where(inside(dims[t, 0], dims[t, 1], (width, width)), ham_sum(x, t, lref, rref), 0.0)
        href[t] = h
        v = x[0].astype(F32)
        norm, num = total_of(v * v), total_of(v * h)
        alpha = jnp.where(norm > 1e-30, num / jnp.maximum(norm, 1e-30), 0.0).astype(BF16).astype(F32)
        payload[pl.ds(pl.multiple_of(t * width, width), width), :] = (h - alpha * v).astype(BF16)
        now = jnp.where(row == t, alpha, ext[...])
        ext[...] = now + jnp.where(row == count, norm, 0.0) + jnp.where(row == count + 1, num, 0.0)

    over_slots(count, slot)
    now = ext[...]
    high = now.astype(BF16).astype(F32)
    rest = now - high
    mid = rest.astype(BF16).astype(F32)
    low = rest - mid
    split = jnp.where(lane == 0, high, jnp.where(lane == 1, mid, jnp.where(lane == 2, low, 0.0)))
    payload[pl.ds(count * width, EXTRA), :] = jnp.where(row < count, now, split).astype(BF16)


def second_kernel(places, count, cells, idx, there, dims, *refs):
    n = len(places)
    vpieces, rpieces = refs[:n], refs[n : 2 * n]
    lref, rref, gref, sums, vsrc, wsrc, vheld, rheld, ext, vsem, rsem = refs[2 * n :]
    width = gref.shape[1]
    nblk = vheld.shape[0]
    srow = lax.broadcasted_iota(jnp.int32, sums.shape, 0)
    for copy in load_pieces(places, vpieces, vheld, vsem) + load_pieces(places, rpieces, rheld, rsem):
        copy.wait()
    both = jnp.zeros((EXTRA, 128), F32)
    for place in range(nblk):
        part = rheld[place, pl.ds(count * width, EXTRA), :].astype(F32)
        ext[pl.ds(place * EXTRA, EXTRA), :] = part
        both = both + part
    both = jnp.sum(both, axis=1, keepdims=True)
    norm, num = both[count : count + 1], both[count + 1 : count + 2]
    sums[...] = jnp.where(srow == 2, num / norm, jnp.where(srow == 3, jnp.sqrt(cells / norm), 0.0))
    a_zero, scale = sums[2:3, :], sums[3:4, :]

    def slot(t):
        x = []
        squares = None
        for c in range(GROUPS):
            entry = idx[c, t]
            on = there[c, t] > 0
            place = entry // count
            v = block_of(vheld, entry, count, width)
            r = block_of(rheld, entry, count, width).astype(F32)
            alpha = ext[pl.ds(place * EXTRA + (entry - place * count), 1), :]
            w = scale * (r + (alpha - a_zero) * v.astype(F32))
            if c == 0:
                squares = total_of(w * w)
            w = jnp.where(on, w, 0.0).astype(BF16)
            x.append(w)
            if c in LATE:
                vsrc[LATE.index(c), t] = jnp.where(on, v, jnp.zeros_like(v))
                wsrc[LATE.index(c), t] = w
        g = jnp.where(inside(dims[t, 0], dims[t, 1], (width, width)), ham_sum(x, t, lref, rref), 0.0)
        gref[t] = g
        num = total_of(x[0].astype(F32) * g)
        sums[...] += jnp.where(srow == 0, squares, jnp.where(srow == 1, num, 0.0))

    over_slots(count, slot)


def ritz_kernel(count, cells, ranks, parts, vsrc, wsrc, facts, passed, coefs):
    width = vsrc.shape[2]
    both = parts[0]
    for i in range(1, parts.shape[0]):
        both = both + parts[i]
    squares, num = both[0:1, :] / cells, both[1:2, :] / cells
    a_zero, scale = parts[0, 2:3, :], parts[0, 3:4, :]
    beta = jnp.sqrt(squares + 1e-06)
    a_one = num / (beta * beta)
    half_gap = (a_zero - a_one) / 2.0
    ritz = (a_zero + a_one) / 2.0 - jnp.sqrt(half_gap * half_gap + beta * beta)
    gap_val = ritz - a_zero
    length = jnp.sqrt(beta * beta + gap_val * gap_val)
    from_v, from_w = beta / length * scale, gap_val / length / beta
    row = lax.broadcasted_iota(jnp.int32, coefs.shape, 0)
    coefs[...] = jnp.where(row == 0, from_v, jnp.where(row == 1, from_w, ritz))
    lane = lax.broadcasted_iota(jnp.int32, (width, width), 1)
    passed[pl.ds(count * width, EXTRA), :] = facts[...]

    def slot(t):
        state = from_v * vsrc[0, t].astype(F32) + from_w * wsrc[0, t].astype(F32)
        kept = jnp.where(lane < ranks[t], state, 0.0).astype(BF16)
        passed[pl.ds(pl.multiple_of(t * width, width), width), :] = kept

    over_slots(count, slot)


def pack_kernel(count, caps, src_caps, starts, coefs, vsrc, wsrc, lref, out, *accs):
    width = vsrc.shape[2]
    kinds = lref.shape[0] // GROUPS
    lane = lax.broadcasted_iota(jnp.int32, (width, width), 1)
    from_v, from_w = coefs[0:1, :], coefs[1:2, :]

    def slot(t, acc):
        kept = []
        for i, c in enumerate(LATE):
            state = from_v * vsrc[i, t].astype(F32) + from_w * wsrc[i, t].astype(F32)
            kept.append(jnp.where(lane < src_caps[c, t], state, 0.0))
        own = kept[0].T.astype(BF16)
        at = jnp.int32(0)
        for i, c in enumerate(LATE):
            left = jnp.concatenate([lref[GROUPS * k + c, t] for k in range(kinds)], 0)
            inner = jnp.dot(left, kept[i].astype(BF16), preferred_element_type=F32).astype(BF16)
            inner = jnp.concatenate([inner[width * k : width * (k + 1)] for k in range(kinds)], 1)
            update = jnp.dot(own, inner, preferred_element_type=F32)
            for k in range(kinds):
                tile = at // width
                lead = at - tile * width
                turned = pltpu.roll(update[:, width * k : width * (k + 1)], lead, 1)
                acc[tile] = jnp.where(lane >= lead, turned, acc[tile])
                acc[tile + 1] = turned
                at = at + src_caps[c, t]
        return (at + width - 1) // width

    def step(i, carry):
        used = [slot(i * len(accs) + p, acc) for p, acc in enumerate(accs)]
        for p, acc in enumerate(accs):
            t = i * len(accs) + p
            high = (caps[t] + 15) // 16 * 16

            def flush(tile, c, t=t, acc=acc, high=high):
                first = jnp.minimum(starts[t] + tile * high, out.shape[0] - width)
                out[pl.ds(pl.multiple_of(first, 16), width), :] = acc[tile].astype(BF16)
                return c

            lax.fori_loop(0, used[p], flush, 0)
        return carry

    lax.fori_loop(0, count // len(accs), step, 0)


def unpack_kernel(count, caps, src_caps, starts, first_sec, packed, lenv, so_far, out, made, sem):
    del so_far
    width = packed.shape[1]
    kinds = made.shape[0]

    @pl.when(first_sec[0] == 1)
    def _():
        copies = [
            pltpu.make_async_copy(lenv.at[GROUPS * k + c], out.at[k, c], sem.at[len(LATE) * k + i])
            for i, c in enumerate(LATE)
            for k in range(kinds)
        ]
        for copy in copies:
            copy.start()
        for copy in copies:
            copy.wait()

    @pl.when(first_sec[0] == 0)
    def _():
        lane = lax.broadcasted_iota(jnp.int32, (width, width), 1)
        copies = []

        def slot(t):
            high = (caps[t] + 15) // 16 * 16
            at = jnp.int32(0)
            for i, c in enumerate(LATE):
                mine = src_caps[c, t]
                valid = inside(caps[t], mine, (width, width))
                for k in range(kinds):
                    tile = jnp.where(mine > 0, at // width, 0)
                    lead = at - at // width * width
                    low = packed[pl.ds(pl.multiple_of(starts[t] + tile * high, 16), width), :]
                    upper = packed[pl.ds(pl.multiple_of(starts[t] + (tile + 1) * high, 16), width), :]
                    both = jnp.where(lane >= lead, low.astype(F32), upper.astype(F32))
                    both = pltpu.roll(both, width - lead, 1)
                    made[k, i, t] = jnp.where(valid, both, 0.0).astype(BF16)
                    at = at + mine

        def sent_off(first, many):
            for i, c in enumerate(LATE):
                span = pl.ds(first, many)
                copies.append(
                    pltpu.make_async_copy(made.at[:, i, span], out.at[:, c, span], sem.at[len(copies)])
                )
                copies[-1].start()

        per = max(p for p in (1, 2, 3, 4) if count % p == 0)
        for first in range(0, count, per):

            def pair(i, carry, first=first):
                for p in range(per // 2 if per % 2 == 0 else per):
                    slot(first + i * (per // 2 if per % 2 == 0 else per) + p)
                return carry

            lax.fori_loop(0, 2 if per % 2 == 0 else 1, pair, 0)
            sent_off(first, per)
        for copy in copies:
            copy.wait()


def early_kernel(places, count, idx, there, first_sec, *refs):
    pieces = refs[: len(places)]
    one, two, lenv, out, held, made, sem, out_sem = refs[len(places) :]
    width = one.shape[2]
    kinds = one.shape[0]

    @pl.when(first_sec[0] == 1)
    def _():
        copies = [
            pltpu.make_async_copy(lenv.at[GROUPS * k + c], out.at[k, c], out_sem.at[len(EARLY) * k + i])
            for i, c in enumerate(EARLY)
            for k in range(kinds)
        ]
        for copy in copies:
            copy.start()
        for copy in copies:
            copy.wait()

    @pl.when(first_sec[0] == 0)
    def _():
        for copy in load_pieces(places, pieces, held, sem):
            copy.wait()
        copies = []

        def slot(t):
            own = block_of(held, idx[0, t], count, width).astype(F32).T.astype(BF16)
            for i, c in enumerate(EARLY):
                sent = (one, two)[i]
                at = jnp.clip(t - 1 + i, 0, count - 2)
                kept = block_of(held, idx[c, t], count, width)
                kept = jnp.where(there[c, t] > 0, kept, jnp.zeros_like(kept))
                left = jnp.concatenate([sent[k, at] for k in range(kinds)], 0)
                inner = jnp.dot(left, kept, preferred_element_type=F32).astype(BF16)
                inner = jnp.concatenate([inner[width * k : width * (k + 1)] for k in range(kinds)], 1)
                update = jnp.dot(own, inner, preferred_element_type=F32).astype(BF16)
                for k in range(kinds):
                    made[k, i, t] = update[:, width * k : width * (k + 1)]

        per = max(p for p in (1, 2, 3, 4) if count % p == 0)
        for first in range(0, count, per):
            for p in range(per):
                slot(first + p)
            for i, c in enumerate(EARLY):
                span = pl.ds(first, per)
                copies.append(
                    pltpu.make_async_copy(made.at[:, i, span], out.at[:, c, span], out_sem.at[len(copies)])
                )
                copies[-1].start()
        for copy in copies:
            copy.wait()


def shards(wavefunction, left_env, right_env, row_offset, sector_dims, trunc_ranks):
    start, lenv, renv = wavefunction[0], left_env[0], right_env[0]
    offsets, dims, ranks = row_offset[0], sector_dims[0], trunc_ranks[0]
    count, width = start.shape[0], start.shape[1]
    channels = lenv.shape[0]
    kinds = channels // GROUPS
    nblk, device = lax.axis_size("blk"), lax.axis_index("blk")
    body = count * width
    cells = float(count * nblk * width * width)
    lines = jnp.arange(width, dtype=jnp.int32)
    first_sec = jnp.reshape((lax.axis_index("sec") == 0).astype(jnp.int32), (1,))
    by_group = lenv.reshape((kinds, GROUPS, count, width, width))
    near_left = pltpu.with_memory_space_constraint(lenv, pltpu.VMEM)
    near_right = pltpu.with_memory_space_constraint(renv, pltpu.VMEM)

    up_val = jnp.arange(count, dtype=jnp.int32)

    def sources(holder):
        down_val = (holder - offsets) % nblk
        holders = [
            jnp.broadcast_to(holder, (count,)),
            (down_val + jnp.roll(offsets, 1)) % nblk,
            (down_val + jnp.roll(offsets, -1)) % nblk,
            jnp.broadcast_to((holder - 1) % nblk, (count,)),
            jnp.broadcast_to((holder + 1) % nblk, (count,)),
        ]
        slots = [up_val, jnp.maximum(up_val - 1, 0), jnp.minimum(up_val + 1, count - 1), up_val, up_val]
        there = [up_val >= 0, up_val >= 1, up_val <= count - 2, down_val >= 1, down_val <= nblk - 2]
        idx = (jnp.stack(holders) ^ device) * count + jnp.stack(slots)
        return idx.astype(jnp.int32), jnp.stack(there).astype(jnp.int32)

    idx, there = sources(device)

    mask_on = (lines[None, :, None] < dims[:, 0][:, None, None]) & (
        lines[None, None, :] < dims[:, 1][:, None, None]
    )
    vzero = jnp.where(mask_on, start, jnp.zeros_like(start))
    caps = jnp.minimum(dims[:, 1], ranks)
    meta = jnp.zeros((EXTRA, width), BF16).at[0, :count].set(caps.astype(BF16))
    vpieces = gathered(jnp.concatenate([vzero.reshape((body, width)), meta]))
    sent_one = onward(by_group[:, 1, 1:])
    sent_two = onward(by_group[:, 2, : count - 1])
    places = tuple((place, first) for _, place, first in vpieces)
    n = len(places)
    anywhere = pl.BlockSpec(memory_space=pl.ANY)
    near = pl.BlockSpec(memory_space=pltpu.VMEM)
    scalars = pl.BlockSpec(memory_space=pltpu.SMEM)
    held = pltpu.VMEM((nblk, body + EXTRA, width), BF16)
    wide_shape = jax.ShapeDtypeStruct((count, width, width), F32)
    pay_shape = jax.ShapeDtypeStruct((body + EXTRA, width), BF16)
    row_shape = jax.ShapeDtypeStruct((8, 128), F32)
    late_shape = jax.ShapeDtypeStruct((len(LATE), count, width, width), BF16)
    cheap = pl.CostEstimate(flops=1, bytes_accessed=1, transcendentals=0)

    def call(kernel, name, in_specs, out_specs, out_shape, scratch=(), aliases=None):
        return pl.pallas_call(
            kernel,
            in_specs=in_specs,
            out_specs=out_specs,
            out_shape=out_shape,
            scratch_shapes=list(scratch),
            input_output_aliases=aliases or {},
            compiler_params=params(),
            cost_estimate=cheap,
            name=name,
        )

    hzero, rpay = call(
        functools.partial(first_kernel, places, count),
        "ham_first",
        [scalars] * 3 + [anywhere] * n + [near] * 2,
        [near] * 2,
        [wide_shape, pay_shape],
        [held, pltpu.VMEM((EXTRA, 128), F32), pltpu.SemaphoreType.DMA((n,))],
    )(idx, there, dims, *[rows for rows, _, _ in vpieces], near_left, near_right)

    rpieces = gathered(rpay)
    gone, sums, vsrc, wsrc = call(
        functools.partial(second_kernel, places, count, cells),
        "ham_second",
        [scalars] * 3 + [anywhere] * (2 * n) + [near] * 2,
        [near] * 4,
        [wide_shape, row_shape, late_shape, late_shape],
        [
            held,
            held,
            pltpu.VMEM((nblk * EXTRA, 128), F32),
            pltpu.SemaphoreType.DMA((n,)),
            pltpu.SemaphoreType.DMA((n,)),
        ],
    )(
        idx, there, dims, *[rows for rows, _, _ in vpieces], *[rows for rows, _, _ in rpieces],
        near_left, near_right,
    )

    all_caps = extras_of(vpieces, nblk, body)[:, 0, :count].astype(jnp.int32).reshape((-1,))

    def layout(caps, src_caps):
        high = (caps + 15) // 16 * 16
        wide = (kinds * sum(src_caps[c] for c in LATE) + width - 1) // width
        ends = jnp.cumsum(high * wide)
        return ends - high * wide, ends[-1]

    def used_by(holder):
        entries, on = sources(holder)
        found = jnp.where(on > 0, jnp.take(all_caps, entries), 0).astype(jnp.int32)
        return found, *layout(found[0], found)

    src_caps, starts, _ = used_by(device)
    needed = jnp.max(jax.vmap(lambda holder: used_by(holder)[2])(jnp.arange(nblk, dtype=jnp.int32)))
    length = lax.axis_size("sec")
    needed = jnp.where(lax.axis_index("sec") == length - 1, 0, needed).astype(F32)
    needed, sums = lax.optimization_barrier((needed, sums))
    needed = jnp.full((8, 128), needed)
    most_needed = needed
    for shift in range(1, length):
        turn = [(i, (i + shift) % length) for i in range(length)]
        most_needed = jnp.maximum(most_needed, lax.ppermute(needed, "sec", turn))
    most_needed = most_needed[0, 0].astype(jnp.int32)

    parts = lax.all_gather(sums, "blk", axis=0)
    facts = jnp.concatenate([caps[None], src_caps, idx], axis=0).astype(BF16)
    facts = jnp.zeros((EXTRA, width), BF16).at[: facts.shape[0], :count].set(facts)

    tiles = kinds * len(LATE)
    most = count * tiles * width + SLACK
    out_shape = jax.ShapeDtypeStruct(by_group.shape, BF16)
    accs = [pltpu.VMEM((tiles + 2, width, width), F32)] * max(p for p in (1, 2, 3) if count % p == 0)

    def finish(rows):
        def branch(parts, hzero, gone, vsrc, wsrc, near_left, sent_one, sent_two):
            passed, coefs = call(
                functools.partial(ritz_kernel, count, cells),
                "ritz",
                [scalars] + [near] * 4,
                [near] * 2,
                [pay_shape, row_shape],
            )(ranks, parts, vsrc, wsrc, facts)
            passed = onward(passed)
            packed = call(
                functools.partial(pack_kernel, count),
                "pack_update",
                [scalars] * 3 + [near] * 4,
                near,
                jax.ShapeDtypeStruct((rows, width), BF16),
                accs,
            )(caps, src_caps, starts, coefs, vsrc, wsrc, near_left)
            arrived = onward(packed)
            from_v, from_w, ritz = coefs[0, 0], coefs[1, 0], coefs[2, 0]
            state_new = (from_v * vsrc[0].astype(F32) + from_w * wsrc[0].astype(F32)).astype(BF16)
            hstate_new = (from_v * hzero + from_w * gone).astype(BF16)
            kpieces = gathered(passed)
            facts_in = passed[body:, :count].astype(jnp.int32)
            prev_caps, prev_src, prev_idx = facts_in[0], facts_in[1 : 1 + GROUPS], facts_in[1 + GROUPS : 1 + 2 * GROUPS]
            prev_starts, _ = layout(prev_caps, prev_src)
            so_far = call(
                functools.partial(early_kernel, places, count),
                "early_update",
                [scalars] * 3 + [anywhere] * n + [near] * 2 + [anywhere],
                anywhere,
                out_shape,
                [
                    held,
                    pltpu.VMEM((kinds, len(EARLY), count, width, width), BF16),
                    pltpu.SemaphoreType.DMA((n,)),
                    pltpu.SemaphoreType.DMA((len(EARLY) * count,)),
                ],
            )(prev_idx, prev_src, first_sec, *[r for r, _, _ in kpieces], sent_one, sent_two, lenv)
            next_left = call(
                functools.partial(unpack_kernel, count),
                "unpack_update",
                [scalars] * 4 + [near] + [anywhere] * 2,
                anywhere,
                out_shape,
                [
                    pltpu.VMEM((kinds, len(LATE), count, width, width), BF16),
                    pltpu.SemaphoreType.DMA((len(LATE) * count,)),
                ],
                {6: 0},
            )(prev_caps, prev_src, prev_starts, first_sec, arrived, lenv, so_far)
            return state_new, hstate_new, ritz, next_left

        return branch

    sizes = [most * part // 32 // 16 * 16 for part in (8, 9, 10, 11, 12, 13, 14, 15, 16, 18, 20, 24)] + [most]
    tier = sum((most_needed + SLACK > size).astype(jnp.int32) for size in sizes[:-1])
    state_new, hstate_new, ritz, next_left = lax.switch(
        tier,
        [finish(size) for size in sizes],
        parts, hzero, gone, vsrc, wsrc, near_left, sent_one, sent_two,
    )
    next_left = next_left.reshape((channels, count, width, width))
    return (state_new[None], hstate_new[None], jnp.reshape(ritz, (1,)), next_left[None])


def solution(mesh):
    placed = (
        P("sec", "blk", None, None),
        P("sec", None, "blk", None, None),
        P("sec", None, "blk", None, None),
        P("sec", None),
        P("sec", "blk", None),
        P("sec", "blk"),
    )
    return jax.shard_map(
        shards,
        mesh=mesh,
        in_specs=placed,
        out_specs=(
            P("sec", "blk", None, None),
            P("sec", "blk", None, None),
            P("sec"),
            P("sec", None, "blk", None, None),
        ),
        check_vma=False,
    )
```

```python
import functools

import jax
import jax.numpy as jnp
from jax import lax
from jax.experimental import pallas as pl
from jax.experimental.pallas import tpu as pltpu
from jax.sharding import PartitionSpec as P

GROUPS = 5
EXTRA = 16
SLACK = 128
HAM_STEP = 4
PACK_STEP = 2
UNPACK_STEP = 2
EARLY_STEP = 1
VMEM = 40 * 1024 * 1024
F32 = jnp.float32
BF16 = jnp.bfloat16


def params():
    return pltpu.CompilerParams(vmem_limit_bytes=VMEM)


def shares(kinds):
    first = tuple((c, 0, 1) for c in range(GROUPS))
    then = ((0, 1, kinds), (1, 1, 2))
    return first, then, ((1, 2, kinds), (2, 1, kinds), (3, 1, kinds), (4, 1, kinds))


def exchange(value, bit):
    length = lax.axis_size("blk")
    return lax.ppermute(value, "blk", [(i, i ^ bit) for i in range(length)])


def onward(value):
    length = lax.axis_size("sec")
    return lax.ppermute(value, "sec", [(i, i + 1) for i in range(length - 1)])


def in_hbm(value):
    return pltpu.with_memory_space_constraint(value, pltpu.HBM)


def gathered(value):
    nblk = lax.axis_size("blk")
    if nblk == 8:
        rows = value.shape[0]
        half = rows // 2 // 16 * 16
        four, two, one = exchange(value, 4), exchange(value, 2), exchange(value, 1)
        six_a, six_b = exchange(two[:half], 4), exchange(four[half:], 2)
        three, five = exchange(two, 1), exchange(four, 1)
        seven_a, seven_b = exchange(six_a, 1), exchange(six_b, 1)
        return [
            (value, 0, 0), (one, 1, 0), (two, 2, 0), (three, 3, 0), (four, 4, 0), (five, 5, 0),
            (six_a, 6, 0), (six_b, 6, half), (seven_a, 7, 0), (seven_b, 7, half),
        ]
    held = {0: value}
    bit = 1
    while bit < nblk:
        held.update({place | bit: exchange(rows, bit) for place, rows in list(held.items())})
        bit *= 2
    return [(held[place], place, 0) for place in range(nblk)]


def extras_of(pieces, nblk, body):
    found = [None] * nblk
    for rows, place, first in pieces:
        if first + rows.shape[0] == body + EXTRA:
            found[place] = rows[rows.shape[0] - EXTRA :]
    return jnp.stack(found)


def start_pieces(places, refs, scratch, sem):
    copies = []
    for (place, first), ref in zip(places, refs):
        copies.append(
            pltpu.make_async_copy(ref, scratch.at[place, pl.ds(first, ref.shape[0])], sem.at[len(copies)])
        )
        copies[-1].start()
    return copies


def source_of(c, t, offsets, device, count, nblk):
    mine = device[0]
    down = (mine - offsets[t]) & (nblk - 1)
    if c == 0:
        return 0, t, None
    if c in (1, 2):
        slot = jnp.maximum(t - 1, 0) if c == 1 else jnp.minimum(t + 1, count - 1)
        holder = (down + offsets[slot]) & (nblk - 1)
        return holder ^ mine, slot, (t >= 1) if c == 1 else (t <= count - 2)
    if c == 3:
        return ((mine - 1) & (nblk - 1)) ^ mine, t, down >= 1
    return ((mine + 1) & (nblk - 1)) ^ mine, t, down <= nblk - 2


def block_of(scratch, place, slot, width):
    return scratch[place, pl.ds(pl.multiple_of(slot * width, width), width), :]


def only(on, block):
    return block if on is None else jnp.where(on, block, jnp.zeros_like(block))


def ham_sum(x, t, lref, rref):
    kinds = lref.shape[0] // GROUPS
    zero = jnp.zeros_like(x[0])
    width = zero.shape[0]
    inner = [None] * lref.shape[0]
    for c0, c1 in ((0, 1), (2, 3)):
        both = jnp.concatenate(
            [jnp.concatenate([x[c0], zero], 1), jnp.concatenate([zero, x[c1]], 1)], 0
        )
        left = jnp.concatenate(
            [
                jnp.concatenate([lref[GROUPS * k + c0, t], lref[GROUPS * k + c1, t]], 1)
                for k in range(kinds)
            ],
            0,
        )
        pair = jnp.dot(left, both, preferred_element_type=F32).astype(BF16)
        for k in range(kinds):
            inner[GROUPS * k + c0] = pair[width * k : width * (k + 1), :width]
            inner[GROUPS * k + c1] = pair[width * k : width * (k + 1), width:]
    left = jnp.concatenate([lref[GROUPS * k + 4, t] for k in range(kinds)], 0)
    last = jnp.dot(left, x[4], preferred_element_type=F32).astype(BF16)
    for k in range(kinds):
        inner[GROUPS * k + 4] = last[width * k : width * (k + 1)]
    right = jnp.concatenate([rref[w, t] for w in range(lref.shape[0])], 1)
    return lax.dot_general(
        jnp.concatenate(inner, 1), right, (((1,), (1,)), ((), ())), preferred_element_type=F32
    )


def step_of(count, most):
    return max(p for p in range(1, most + 1) if count % p == 0)


def over_slots(count, body, most, before=None, after=None):
    per = step_of(count, most)

    def step(i, carry):
        if before is not None:
            before(i)
        for p in range(per):
            body(i * per + p)
        if after is not None:
            after(i)
        return carry

    lax.fori_loop(0, count // per, step, 0)


def env_copies(envs, count, i):
    per = step_of(count, HAM_STEP)
    span = pl.ds(i * per, per)
    return [pltpu.make_async_copy(far.at[:, span], near.at[:, span], sem.at[i]) for far, near, sem in envs]


def bring_in(envs, count, copies):
    for copy in env_copies(envs, count, 0):
        copy.start()
    for copy in copies:
        copy.wait()
    for i in range(1, count // step_of(count, HAM_STEP)):
        for copy in env_copies(envs, count, i):
            copy.start()


def arrival(envs, count):
    def before(i):
        for copy in env_copies(envs, count, i):
            copy.wait()

    return before


def inside(rows, cols, shape):
    row = lax.broadcasted_iota(jnp.int32, shape, 0)
    col = lax.broadcasted_iota(jnp.int32, shape, 1)
    return (row < rows) & (col < cols)


def total_of(value):
    return jnp.sum(jnp.sum(value, axis=0, keepdims=True), axis=1, keepdims=True)


def first_kernel(places, count, then, offsets, device, dims, *refs):
    pieces = refs[: len(places)]
    lfar, rfar, href, payload, sent, held, lref, rref, ext, sem, lsem, rsem, out_sem = refs[len(places) :]
    width = href.shape[1]
    nblk = held.shape[0]
    envs = ((lfar, lref, lsem), (rfar, rref, rsem))
    channels = [GROUPS * k + c for c, low, end in then for k in range(low, end)]
    outgoing = [pltpu.make_async_copy(lref.at[w], sent.at[i], out_sem.at[i]) for i, w in enumerate(channels)]
    ext[...] = jnp.zeros_like(ext)
    bring_in(envs, count, start_pieces(places, pieces, held, sem))
    row = lax.broadcasted_iota(jnp.int32, ext.shape, 0)
    lane = lax.broadcasted_iota(jnp.int32, ext.shape, 1)

    def slot(t):
        x = []
        for c in range(GROUPS):
            place, at, on = source_of(c, t, offsets, device, count, nblk)
            x.append(only(on, block_of(held, place, at, width)))
        h = jnp.where(inside(dims[t, 0], dims[t, 1], (width, width)), ham_sum(x, t, lref, rref), 0.0)
        href[t] = h
        v = x[0].astype(F32)
        norm, num = total_of(v * v), total_of(v * h)
        alpha = jnp.where(norm > 1e-30, num / jnp.maximum(norm, 1e-30), 0.0).astype(BF16).astype(F32)
        payload[pl.ds(pl.multiple_of(t * width, width), width), :] = (h - alpha * v).astype(BF16)
        now = jnp.where(row == t, alpha, ext[...])
        ext[...] = now + jnp.where(row == count, norm, 0.0) + jnp.where(row == count + 1, num, 0.0)

    def before(i):
        arrival(envs, count)(i)

        @pl.when(i == count // step_of(count, HAM_STEP) - 1)
        def _():
            for copy in outgoing:
                copy.start()

    over_slots(count, slot, HAM_STEP, before)
    now = ext[...]
    high = now.astype(BF16).astype(F32)
    rest = now - high
    mid = rest.astype(BF16).astype(F32)
    low = rest - mid
    split = jnp.where(lane == 0, high, jnp.where(lane == 1, mid, jnp.where(lane == 2, low, 0.0)))
    payload[pl.ds(count * width, EXTRA), :] = jnp.where(row < count, now, split).astype(BF16)
    for copy in outgoing:
        copy.wait()


def second_kernel(places, count, cells, used, offsets, device, dims, *refs):
    n = len(places)
    vpieces, rpieces = refs[:n], refs[n : 2 * n]
    lfar, rfar, gref, sums, vsrc, wsrc, vheld, rheld, lref, rref, ext, vsem, hsem, lsem, rsem = refs[2 * n :]
    width = gref.shape[1]
    nblk = vheld.shape[0]
    srow = lax.broadcasted_iota(jnp.int32, sums.shape, 0)
    envs = ((lfar, lref, lsem), (rfar, rref, rsem))
    copies = start_pieces(places, rpieces, rheld, hsem) + start_pieces(places, vpieces, vheld, vsem)
    bring_in(envs, count, copies)
    both = jnp.zeros((EXTRA, 128), F32)
    for place in range(nblk):
        part = rheld[place, pl.ds(count * width, EXTRA), :].astype(F32)
        ext[pl.ds(place * EXTRA, EXTRA), :] = part
        both = both + part
    both = jnp.sum(both, axis=1, keepdims=True)
    norm, num = both[count : count + 1], both[count + 1 : count + 2]
    sums[...] = jnp.where(srow == 2, num / norm, jnp.where(srow == 3, jnp.sqrt(cells / norm), 0.0))
    a_zero, scale = sums[2:3, :], sums[3:4, :]

    def slot(t):
        x = []
        squares = None
        for c in range(GROUPS):
            place, at, on = source_of(c, t, offsets, device, count, nblk)
            v = only(on, block_of(vheld, place, at, width))
            r = block_of(rheld, place, at, width).astype(F32)
            alpha = ext[pl.ds(place * EXTRA + at, 1), :]
            w = scale * (r + (alpha - a_zero) * v.astype(F32))
            if c == 0:
                squares = total_of(w * w)
            w = only(on, w).astype(BF16)
            x.append(w)
            if c in used:
                vsrc[used.index(c), t] = v
                wsrc[used.index(c), t] = w
        g = jnp.where(inside(dims[t, 0], dims[t, 1], (width, width)), ham_sum(x, t, lref, rref), 0.0)
        gref[t] = g
        num = total_of(x[0].astype(F32) * g)
        sums[...] += jnp.where(srow == 0, squares, jnp.where(srow == 1, num, 0.0))

    over_slots(count, slot, HAM_STEP, arrival(envs, count))


def ritz_kernel(count, cells, ranks, parts, vsrc, wsrc, facts, passed, coefs):
    width = vsrc.shape[2]
    both = parts[0]
    for i in range(1, parts.shape[0]):
        both = both + parts[i]
    squares, num = both[0:1, :] / cells, both[1:2, :] / cells
    a_zero, scale = parts[0, 2:3, :], parts[0, 3:4, :]
    beta = jnp.sqrt(squares + 1e-06)
    a_one = num / (beta * beta)
    half_gap = (a_zero - a_one) / 2.0
    ritz = (a_zero + a_one) / 2.0 - jnp.sqrt(half_gap * half_gap + beta * beta)
    gap_val = ritz - a_zero
    length = jnp.sqrt(beta * beta + gap_val * gap_val)
    from_v, from_w = beta / length * scale, gap_val / length / beta
    row = lax.broadcasted_iota(jnp.int32, coefs.shape, 0)
    coefs[...] = jnp.where(row == 0, from_v, jnp.where(row == 1, from_w, ritz))
    lane = lax.broadcasted_iota(jnp.int32, (width, width), 1)
    passed[pl.ds(count * width, EXTRA), :] = facts[...]

    def slot(t):
        state = from_v * vsrc[0, t].astype(F32) + from_w * wsrc[0, t].astype(F32)
        kept = jnp.where(lane < ranks[t], state, 0.0).astype(BF16)
        passed[pl.ds(pl.multiple_of(t * width, width), width), :] = kept

    over_slots(count, slot, 2)


def stacked(blocks):
    width = blocks.shape[1]
    return jnp.concatenate([blocks[width * k : width * (k + 1)] for k in range(blocks.shape[0] // width)], 1)


def pack_kernel(count, late, used, caps, src_caps, starts, coefs, vsrc, wsrc, far, out, lref, accs, sem):
    width = vsrc.shape[2]
    per = accs.shape[0]
    lane = lax.broadcasted_iota(jnp.int32, (width, width), 1)
    from_v, from_w = coefs[0:1, :], coefs[1:2, :]

    def envs(g):
        span, first, copies = pl.ds(g * per, per), 0, []
        for i, (c, low, end) in enumerate(late):
            copies.append(
                pltpu.make_async_copy(
                    far.at[pl.ds(low, end - low), c, span], lref.at[pl.ds(first, end - low), span], sem.at[i, g]
                )
            )
            first += end - low
        return copies

    for g in range(count // per):
        for copy in envs(g):
            copy.start()

    def kept_block(c, t, cap):
        i = used.index(c)
        state = from_v * vsrc[i, t].astype(F32) + from_w * wsrc[i, t].astype(F32)
        return jnp.where(lane < cap, state, 0.0)

    def slot(t, acc):
        own = kept_block(0, t, caps[t]).T.astype(BF16)
        at, first = jnp.int32(0), 0
        for c, low, end in late:
            cap = src_caps[c, t]
            left = jnp.concatenate([lref[first + k, t] for k in range(end - low)], 0)
            inner = jnp.dot(left, kept_block(c, t, cap).astype(BF16), preferred_element_type=F32).astype(BF16)
            update = jnp.dot(own, stacked(inner), preferred_element_type=F32)
            for k in range(end - low):
                tile = at // width
                lead = at - tile * width
                turned = pltpu.roll(update[:, width * k : width * (k + 1)], lead, 1)
                acc[tile] = jnp.where(lane >= lead, turned, acc[tile])
                acc[tile + 1] = turned
                at = at + cap
            first += end - low
        return (at + width - 1) // width

    def step(g, carry):
        for copy in envs(g):
            copy.wait()
        tiles = [slot(g * per + p, accs.at[p]) for p in range(per)]
        for p in range(per):
            t = g * per + p
            high = (caps[t] + 15) // 16 * 16

            def flush(tile, c, t=t, p=p, high=high):
                first = jnp.minimum(starts[t] + tile * high, out.shape[0] - width)
                out[pl.ds(pl.multiple_of(first, 16), width), :] = accs[p, tile].astype(BF16)
                return c

            lax.fori_loop(0, tiles[p], flush, 0)
        return carry

    lax.fori_loop(0, count // per, step, 0)


def made_copies(share, out, made, sem, span, at):
    copies, first = [], 0
    for i, (c, low, end) in enumerate(share):
        copies.append(
            (made.at[pl.ds(first, end - low), span], out.at[pl.ds(low, end - low), c, span], sem.at[len(share) * at + i])
        )
        first += end - low
    return copies


def own_left(share, lenv, out, made, sem, count):
    every = pl.ds(0, count)
    into = [pltpu.make_async_copy(b, a, s) for a, b, s in made_copies(share, lenv, made, sem, every, 0)]
    for copy in into:
        copy.start()
    for copy in into:
        copy.wait()
    back = [pltpu.make_async_copy(a, b, s) for a, b, s in made_copies(share, out, made, sem, every, 0)]
    for copy in back:
        copy.start()
    for copy in back:
        copy.wait()


def send_out(share, out, made, sem, per):
    def after(g):
        for a, b, s in made_copies(share, out, made, sem, pl.ds(g * per, per), g):
            pltpu.make_async_copy(a, b, s).start()

    return after


def wait_out(share, out, made, sem, count, per):
    def wait(g, carry):
        for a, b, s in made_copies(share, out, made, sem, pl.ds(g * per, per), g):
            pltpu.make_async_copy(a, b, s).wait()
        return carry

    lax.fori_loop(0, count // per, wait, 0)


def unpack_kernel(count, late, caps, src_caps, starts, first_sec, packed, lenv, so_far, out, made, sem):
    del so_far
    width = packed.shape[1]

    @pl.when(first_sec[0] == 1)
    def _():
        own_left(late, lenv, out, made, sem, count)

    @pl.when(first_sec[0] == 0)
    def _():
        lane = lax.broadcasted_iota(jnp.int32, (width, width), 1)

        def slot(t):
            high = (caps[t] + 15) // 16 * 16
            at, first = jnp.int32(0), 0
            for c, low, end in late:
                mine = src_caps[c, t]
                valid = inside(caps[t], mine, (width, width))
                for k in range(end - low):
                    tile = jnp.where(mine > 0, at // width, 0)
                    lead = at - at // width * width
                    near = packed[pl.ds(pl.multiple_of(starts[t] + tile * high, 16), width), :]
                    next_one = packed[pl.ds(pl.multiple_of(starts[t] + (tile + 1) * high, 16), width), :]
                    both = jnp.where(lane >= lead, near.astype(F32), next_one.astype(F32))
                    both = pltpu.roll(both, width - lead, 1)
                    made[first + k, t] = jnp.where(valid, both, 0.0).astype(BF16)
                    at = at + mine
                first += end - low

        per = step_of(count, UNPACK_STEP)
        over_slots(count, slot, UNPACK_STEP, None, send_out(late, out, made, sem, per))
        wait_out(late, out, made, sem, count, per)


def early_kernel(places, count, early, offsets, device, first_sec, *refs):
    pieces = refs[: len(places)]
    one, two, lenv, out, held, sent, made, sem, far_sem, out_sem = refs[len(places) :]
    width = made.shape[2]
    nblk = held.shape[0]

    @pl.when(first_sec[0] == 1)
    def _():
        own_left(early, lenv, out, made, out_sem, count)

    @pl.when(first_sec[0] == 0)
    def _():
        copies = start_pieces(places, pieces, held, sem)
        m = one.shape[0]
        copies.append(pltpu.make_async_copy(one, sent.at[pl.ds(0, m)], far_sem.at[0]))
        copies.append(pltpu.make_async_copy(two, sent.at[pl.ds(m, two.shape[0])], far_sem.at[1]))
        for copy in copies[-2:]:
            copy.start()
        for copy in copies:
            copy.wait()

        def slot(t):
            own = block_of(held, 0, t, width).astype(F32).T.astype(BF16)
            first = 0
            for c, low, end in early:
                place, at, on = source_of(c, t, offsets, device, count, nblk)
                kept = only(on, block_of(held, place, at, width))
                left = jnp.concatenate([sent[first + k, t] for k in range(end - low)], 0)
                inner = jnp.dot(left, kept, preferred_element_type=F32).astype(BF16)
                update = jnp.dot(own, stacked(inner), preferred_element_type=F32).astype(BF16)
                for k in range(end - low):
                    made[first + k, t] = update[:, width * k : width * (k + 1)]
                first += end - low

        per = step_of(count, EARLY_STEP)
        over_slots(count, slot, EARLY_STEP, None, send_out(early, out, made, out_sem, per))
        wait_out(early, out, made, out_sem, count, per)


def shards(wavefunction, left_env, right_env, row_offset, sector_dims, trunc_ranks):
    start, lenv, renv = wavefunction[0], left_env[0], right_env[0]
    offsets, dims, ranks = row_offset[0], sector_dims[0], trunc_ranks[0]
    count, width = start.shape[0], start.shape[1]
    channels = lenv.shape[0]
    kinds = channels // GROUPS
    nblk, device = lax.axis_size("blk"), lax.axis_index("blk")
    body = count * width
    cells = float(count * nblk * width * width)
    lines = jnp.arange(width, dtype=jnp.int32)
    first_sec = jnp.reshape((lax.axis_index("sec") == 0).astype(jnp.int32), (1,))
    mine = jnp.reshape(device.astype(jnp.int32), (1,))
    by_group = lenv.reshape((kinds, GROUPS, count, width, width))
    at_once, then, late = shares(kinds)
    early = at_once + then
    used = (0,) + tuple(c for c, _, _ in late)
    n_then, n_late = (sum(end - low for _, low, end in share) for share in (then, late))
    n_early = channels - n_late

    mask_on = (lines[None, :, None] < dims[:, 0][:, None, None]) & (
        lines[None, None, :] < dims[:, 1][:, None, None]
    )
    vzero = jnp.where(mask_on, start, jnp.zeros_like(start))
    caps = jnp.minimum(dims[:, 1], ranks)
    meta = jnp.zeros((EXTRA, width), BF16).at[0, :count].set(caps.astype(BF16))
    vpieces = gathered(jnp.concatenate([vzero.reshape((body, width)), meta]))
    sent_one = onward(lenv[:GROUPS])
    places = tuple((place, first) for _, place, first in vpieces)
    n = len(places)
    vrows = [in_hbm(rows) for rows, _, _ in vpieces]
    anywhere = pl.BlockSpec(memory_space=pl.ANY)
    far = pl.BlockSpec(memory_space=pltpu.HBM)
    near = pl.BlockSpec(memory_space=pltpu.VMEM)
    scalars = pl.BlockSpec(memory_space=pltpu.SMEM)
    held = pltpu.VMEM((nblk, body + EXTRA, width), BF16)
    env = pltpu.VMEM(lenv.shape, BF16)
    wide_shape = jax.ShapeDtypeStruct((count, width, width), F32)
    pay_shape = jax.ShapeDtypeStruct((body + EXTRA, width), BF16)
    row_shape = jax.ShapeDtypeStruct((8, 128), F32)
    used_shape = jax.ShapeDtypeStruct((len(used), count, width, width), BF16)
    steps = count // step_of(count, HAM_STEP)

    def dma(*shape):
        return pltpu.SemaphoreType.DMA(shape)

    def call(kernel, name, in_specs, out_specs, out_shape, scratch=(), aliases=None, moved=1):
        return pl.pallas_call(
            kernel,
            in_specs=in_specs,
            out_specs=out_specs,
            out_shape=out_shape,
            scratch_shapes=list(scratch),
            input_output_aliases=aliases or {},
            compiler_params=params(),
            cost_estimate=pl.CostEstimate(flops=1, bytes_accessed=moved, transcendentals=0),
            name=name,
        )

    hzero, rpay, sent_two = call(
        functools.partial(first_kernel, places, count, then),
        "ham_first",
        [scalars] * 3 + [anywhere] * n + [far] * 2,
        [near, near, far],
        [wide_shape, pay_shape, jax.ShapeDtypeStruct((n_then, count, width, width), BF16)],
        [held, env, env, pltpu.VMEM((EXTRA, 128), F32), dma(n), dma(steps), dma(steps), dma(n_then)],
    )(offsets, mine, dims, *vrows, in_hbm(lenv), in_hbm(renv))

    rpieces = gathered(rpay)
    gone, sums, vsrc, wsrc = call(
        functools.partial(second_kernel, places, count, cells, used),
        "ham_second",
        [scalars] * 3 + [anywhere] * (2 * n) + [far] * 2,
        [near] * 4,
        [wide_shape, row_shape, used_shape, used_shape],
        [
            held, held, env, env, pltpu.VMEM((nblk * EXTRA, 128), F32),
            dma(n), dma(n), dma(steps), dma(steps),
        ],
    )(offsets, mine, dims, *vrows, *[rows for rows, _, _ in rpieces], in_hbm(lenv), in_hbm(renv))

    offsets, caps, hzero = lax.optimization_barrier((offsets, caps, hzero))
    all_caps = extras_of(vpieces, nblk, body)[:, 0, :count].astype(jnp.int32).reshape((-1,))
    up_val = jnp.arange(count, dtype=jnp.int32)

    def layout(caps, src_caps):
        high = (caps + 15) // 16 * 16
        wide = (sum((end - low) * src_caps[c] for c, low, end in late) + width - 1) // width
        ends = jnp.cumsum(high * wide)
        return ends - high * wide, ends[-1]

    def used_by(holder):
        down_val = (holder - offsets) % nblk
        holders = [
            jnp.broadcast_to(holder, (count,)),
            (down_val + jnp.roll(offsets, 1)) % nblk,
            (down_val + jnp.roll(offsets, -1)) % nblk,
            jnp.broadcast_to((holder - 1) % nblk, (count,)),
            jnp.broadcast_to((holder + 1) % nblk, (count,)),
        ]
        slots = [up_val, jnp.maximum(up_val - 1, 0), jnp.minimum(up_val + 1, count - 1), up_val, up_val]
        there = [up_val >= 0, up_val >= 1, up_val <= count - 2, down_val >= 1, down_val <= nblk - 2]
        entries = (jnp.stack(holders) ^ device) * count + jnp.stack(slots)
        match = entries[..., None] == jnp.arange(all_caps.shape[0], dtype=jnp.int32)
        found = jnp.sum(jnp.where(match, all_caps, 0), axis=-1)
        found = jnp.where(jnp.stack(there), found, 0).astype(jnp.int32)
        return found, *layout(found[0], found)

    src_caps, starts, _ = used_by(device)
    needed = jnp.max(jax.vmap(lambda holder: used_by(holder)[2])(jnp.arange(nblk, dtype=jnp.int32)))
    length = lax.axis_size("sec")
    needed = jnp.where(lax.axis_index("sec") == length - 1, 0, needed).astype(F32)
    needed, sums = lax.optimization_barrier((needed, sums))
    needed = jnp.full((8, 128), needed)
    most_needed = needed
    for shift in range(1, length):
        turn = [(i, (i + shift) % length) for i in range(length)]
        most_needed = jnp.maximum(most_needed, lax.ppermute(needed, "sec", turn))
    sent_two = onward(sent_two)
    most_needed = most_needed[0, 0].astype(jnp.int32)

    parts = lax.all_gather(sums, "blk", axis=0)
    facts = jnp.concatenate([caps[None], src_caps, offsets[None]], axis=0).astype(BF16)
    facts = jnp.zeros((EXTRA, width), BF16).at[: facts.shape[0], :count].set(facts)

    most = count * n_late * width + SLACK
    out_shape = jax.ShapeDtypeStruct(by_group.shape, BF16)
    per = step_of(count, PACK_STEP)

    def finish(rows):
        def branch(parts, hzero, gone, vsrc, wsrc, sent_one, sent_two):
            passed, coefs = call(
                functools.partial(ritz_kernel, count, cells),
                "ritz",
                [scalars] + [near] * 4,
                [near] * 2,
                [pay_shape, row_shape],
            )(ranks, parts, vsrc, wsrc, facts)
            passed = onward(passed)
            packed = call(
                functools.partial(pack_kernel, count, late, used),
                "pack_update",
                [scalars] * 3 + [near] * 3 + [far],
                near,
                jax.ShapeDtypeStruct((rows, width), BF16),
                [
                    pltpu.VMEM((n_late, count, width, width), BF16),
                    pltpu.VMEM((per, n_late + 2, width, width), F32),
                    dma(len(late), count // per),
                ],
                moved=20 * 1024 * 1024,
            )(caps, src_caps, starts, coefs, vsrc, wsrc, in_hbm(by_group))
            packed, passed = lax.optimization_barrier((packed, passed))
            arrived = onward(packed)
            kpieces = gathered(passed)
            rows_last, coefs = lax.optimization_barrier((kpieces[-1][0], coefs))
            kpieces[-1] = (rows_last, *kpieces[-1][1:])
            from_v, from_w, ritz = coefs[0, 0], coefs[1, 0], coefs[2, 0]
            state_new = (from_v * vsrc[0].astype(F32) + from_w * wsrc[0].astype(F32)).astype(BF16)
            hstate_new = (from_v * hzero + from_w * gone).astype(BF16)
            facts_in = passed[body:, :count].astype(jnp.int32)
            prev_caps, prev_src, prev_offsets = facts_in[0], facts_in[1 : 1 + GROUPS], facts_in[1 + GROUPS]
            prev_starts, _ = layout(prev_caps, prev_src)
            so_far = call(
                functools.partial(early_kernel, places, count, early),
                "early_update",
                [scalars] * 3 + [anywhere] * n + [far] * 3,
                far,
                out_shape,
                [
                    held,
                    pltpu.VMEM((n_early, count, width, width), BF16),
                    pltpu.VMEM((n_early, count, width, width), BF16),
                    dma(n),
                    dma(2),
                    dma(len(early) * count),
                ],
            )(prev_offsets, mine, first_sec, *[r for r, _, _ in kpieces], in_hbm(sent_one), in_hbm(sent_two), in_hbm(by_group))
            next_left = call(
                functools.partial(unpack_kernel, count, late),
                "unpack_update",
                [scalars] * 4 + [near] + [far] * 2,
                far,
                out_shape,
                [pltpu.VMEM((n_late, count, width, width), BF16), dma(len(late) * count)],
                {6: 0},
            )(prev_caps, prev_src, prev_starts, first_sec, arrived, in_hbm(by_group), in_hbm(so_far))
            return state_new, hstate_new, ritz, next_left

        return branch

    sizes = [most * part // 64 // 16 * 16 for part in (20, 24, 26, 27, 28, 30, 36)] + [most]
    tier = sum((most_needed + SLACK > size).astype(jnp.int32) for size in sizes[:-1])
    state_new, hstate_new, ritz, next_left = lax.switch(
        tier, [finish(size) for size in sizes], parts, hzero, gone, vsrc, wsrc, sent_one, sent_two
    )
    next_left = next_left.reshape((channels, count, width, width))
    return (state_new[None], hstate_new[None], jnp.reshape(ritz, (1,)), next_left[None])


def solution(mesh):
    placed = (
        P("sec", "blk", None, None),
        P("sec", None, "blk", None, None),
        P("sec", None, "blk", None, None),
        P("sec", None),
        P("sec", "blk", None),
        P("sec", "blk"),
    )
    return jax.shard_map(
        shards,
        mesh=mesh,
        in_specs=placed,
        out_specs=(
            P("sec", "blk", None, None),
            P("sec", "blk", None, None),
            P("sec"),
            P("sec", None, "blk", None, None),
        ),
        check_vma=False,
    )
```

```python
import functools

import jax
import jax.numpy as jnp
from jax import lax
from jax.experimental import pallas as pl
from jax.experimental.pallas import tpu as pltpu
from jax.sharding import PartitionSpec as P

GROUPS = 5
EXTRA = 16
SLACK = 128
HAM_STEP = 4
PACK_STEP = 2
UNPACK_STEP = 2
EARLY_STEP = 1
VMEM = 40 * 1024 * 1024
F32 = jnp.float32
BF16 = jnp.bfloat16


def params():
    return pltpu.CompilerParams(vmem_limit_bytes=VMEM)


def shares(kinds):
    first = tuple((c, 0, 1) for c in range(GROUPS))
    then = ((0, 1, kinds),)
    return first, then, ((1, 1, kinds), (2, 1, kinds), (3, 1, kinds), (4, 1, kinds))


def exchange(value, bit):
    length = lax.axis_size("blk")
    return lax.ppermute(value, "blk", [(i, i ^ bit) for i in range(length)])


def onward(value):
    length = lax.axis_size("sec")
    return lax.ppermute(value, "sec", [(i, i + 1) for i in range(length - 1)])


def in_hbm(value):
    return pltpu.with_memory_space_constraint(value, pltpu.HBM)


def gathered(value):
    nblk = lax.axis_size("blk")
    if nblk == 8:
        rows = value.shape[0]
        half = rows // 2 // 16 * 16
        four, two, one = exchange(value, 4), exchange(value, 2), exchange(value, 1)
        six_a, six_b = exchange(two[:half], 4), exchange(four[half:], 2)
        three, five = exchange(two, 1), exchange(four, 1)
        seven_a, seven_b = exchange(six_a, 1), exchange(six_b, 1)
        return [
            (value, 0, 0), (one, 1, 0), (two, 2, 0), (three, 3, 0), (four, 4, 0), (five, 5, 0),
            (six_a, 6, 0), (six_b, 6, half), (seven_a, 7, 0), (seven_b, 7, half),
        ]
    held = {0: value}
    bit = 1
    while bit < nblk:
        held.update({place | bit: exchange(rows, bit) for place, rows in list(held.items())})
        bit *= 2
    return [(held[place], place, 0) for place in range(nblk)]


def start_pieces(places, refs, scratch, sem):
    copies = []
    for (place, first), ref in zip(places, refs):
        copies.append(
            pltpu.make_async_copy(ref, scratch.at[place, pl.ds(first, ref.shape[0])], sem.at[len(copies)])
        )
        copies[-1].start()
    return copies


def source_of(c, t, offsets, device, count, nblk):
    mine = device[0]
    down = (mine - offsets(t)) & (nblk - 1)
    if c == 0:
        return 0, t, None
    if c in (1, 2):
        slot = jnp.maximum(t - 1, 0) if c == 1 else jnp.minimum(t + 1, count - 1)
        holder = (down + offsets(slot)) & (nblk - 1)
        return holder ^ mine, slot, (t >= 1) if c == 1 else (t <= count - 2)
    if c == 3:
        return ((mine - 1) & (nblk - 1)) ^ mine, t, down >= 1
    return ((mine + 1) & (nblk - 1)) ^ mine, t, down <= nblk - 2


def block_of(scratch, place, slot, width):
    return scratch[place, pl.ds(pl.multiple_of(slot * width, width), width), :]


def only(on, block):
    return block if on is None else jnp.where(on, block, jnp.zeros_like(block))


def ham_sum(x, t, lref, rref):
    kinds = lref.shape[0] // GROUPS
    zero = jnp.zeros_like(x[0])
    width = zero.shape[0]
    inner = [None] * lref.shape[0]
    for c0, c1 in ((0, 1), (2, 3)):
        both = jnp.concatenate(
            [jnp.concatenate([x[c0], zero], 1), jnp.concatenate([zero, x[c1]], 1)], 0
        )
        left = jnp.concatenate(
            [
                jnp.concatenate([lref[GROUPS * k + c0, t], lref[GROUPS * k + c1, t]], 1)
                for k in range(kinds)
            ],
            0,
        )
        pair = jnp.dot(left, both, preferred_element_type=F32).astype(BF16)
        for k in range(kinds):
            inner[GROUPS * k + c0] = pair[width * k : width * (k + 1), :width]
            inner[GROUPS * k + c1] = pair[width * k : width * (k + 1), width:]
    left = jnp.concatenate([lref[GROUPS * k + 4, t] for k in range(kinds)], 0)
    last = jnp.dot(left, x[4], preferred_element_type=F32).astype(BF16)
    for k in range(kinds):
        inner[GROUPS * k + 4] = last[width * k : width * (k + 1)]
    right = jnp.concatenate([rref[w, t] for w in range(lref.shape[0])], 1)
    return lax.dot_general(
        jnp.concatenate(inner, 1), right, (((1,), (1,)), ((), ())), preferred_element_type=F32
    )


def step_of(count, most):
    return max(p for p in range(1, most + 1) if count % p == 0)


def over_slots(count, body, most, before=None, after=None):
    per = step_of(count, most)

    def step(i, carry):
        if before is not None:
            before(i)
        for p in range(per):
            body(i * per + p)
        if after is not None:
            after(i)
        return carry

    lax.fori_loop(0, count // per, step, 0)


def env_copies(envs, count, i):
    per = step_of(count, HAM_STEP)
    span = pl.ds(i * per, per)
    return [pltpu.make_async_copy(far.at[:, span], near.at[:, span], sem.at[i]) for far, near, sem in envs]


def bring_in(envs, count, copies):
    for copy in env_copies(envs, count, 0):
        copy.start()
    for copy in copies:
        copy.wait()
    for i in range(1, count // step_of(count, HAM_STEP)):
        for copy in env_copies(envs, count, i):
            copy.start()


def arrival(envs, count):
    def before(i):
        for copy in env_copies(envs, count, i):
            copy.wait()

    return before


def inside(rows, cols, shape):
    row = lax.broadcasted_iota(jnp.int32, shape, 0)
    col = lax.broadcasted_iota(jnp.int32, shape, 1)
    return (row < rows) & (col < cols)


def total_of(value):
    return jnp.sum(jnp.sum(value, axis=0, keepdims=True), axis=1, keepdims=True)


def first_kernel(places, count, then, offsets, device, dims, table, *refs):
    pieces = refs[: len(places)]
    lfar, rfar, href, payload, sent, held, lref, rref, ext, sem, lsem, rsem, out_sem = refs[len(places) :]
    width = href.shape[1]
    nblk = held.shape[0]
    envs = ((lfar, lref, lsem), (rfar, rref, rsem))
    channels = [GROUPS * k + c for c, low, end in then for k in range(low, end)]
    outgoing = [pltpu.make_async_copy(lref.at[w], sent.at[i], out_sem.at[i]) for i, w in enumerate(channels)]
    ext[...] = jnp.zeros_like(ext)
    bring_in(envs, count, start_pieces(places, pieces, held, sem))
    row = lax.broadcasted_iota(jnp.int32, ext.shape, 0)
    lane = lax.broadcasted_iota(jnp.int32, ext.shape, 1)

    def slot(t):
        x = []
        for c in range(GROUPS):
            place, at, on = source_of(c, t, lambda i: offsets[i], device, count, nblk)
            x.append(only(on, block_of(held, place, at, width)))
        h = jnp.where(inside(dims[t, 0], dims[t, 1], (width, width)), ham_sum(x, t, lref, rref), 0.0)
        href[t] = h
        v = x[0].astype(F32)
        norm, num = total_of(v * v), total_of(v * h)
        alpha = jnp.where(norm > 1e-30, num / jnp.maximum(norm, 1e-30), 0.0).astype(BF16).astype(F32)
        payload[pl.ds(pl.multiple_of(t * width, width), width), :] = (h - alpha * v).astype(BF16)
        now = jnp.where(row == t, alpha, ext[...])
        ext[...] = now + jnp.where(row == count, norm, 0.0) + jnp.where(row == count + 1, num, 0.0)

    def before(i):
        arrival(envs, count)(i)

        @pl.when(i == count // step_of(count, HAM_STEP) - 1)
        def _():
            for copy in outgoing:
                copy.start()

    over_slots(count, slot, HAM_STEP, before)
    now = ext[...]
    high = now.astype(BF16).astype(F32)
    rest = now - high
    mid = rest.astype(BF16).astype(F32)
    low = rest - mid
    split = jnp.where(lane == 0, high, jnp.where(lane == 1, mid, jnp.where(lane == 2, low, 0.0)))
    extra = jnp.where(row < count, now, split)
    extra = jnp.where(row == count + 2, table[0:1, :], jnp.where(row == count + 3, table[1:2, :], extra))
    payload[pl.ds(count * width, EXTRA), :] = extra.astype(BF16)
    for copy in outgoing:
        copy.wait()


def layout_of(caps, offsets, device, sec, count, secs, late):
    nblk = caps.shape[0]
    row = lax.broadcasted_iota(jnp.int32, caps.shape, 0)
    lane = lax.broadcasted_iota(jnp.int32, caps.shape, 1)
    sec_of = sum((lane >= count * k).astype(jnp.int32) for k in range(1, secs))
    up = lane - count * sec_of
    down = ((row ^ device) - offsets) & (nblk - 1)

    def by_sector(value):
        rows = [jnp.sum(jnp.where(down == e, value, 0.0), axis=0, keepdims=True) for e in range(nblk)]
        return jnp.concatenate(rows, 0)

    def by_place(value):
        return sum(jnp.where(down == e, value[e : e + 1], 0.0) for e in range(nblk))

    own = by_sector(caps)
    none = jnp.zeros_like(own[:1])
    groups = [
        own,
        jnp.where(up >= 1, pltpu.roll(own, 1, 1), 0.0),
        jnp.where(up <= count - 2, pltpu.roll(own, 127, 1), 0.0),
        jnp.concatenate([none, own[:-1]], 0),
        jnp.concatenate([own[1:], none], 0),
    ]
    wide = sum((end - low) * groups[c] for c, low, end in late)
    used = jnp.floor((own + 15.0) / 16.0) * 16.0 * jnp.floor((wide + 127.0) / 128.0)
    groups = [by_place(value) for value in groups]
    used = by_place(used)
    most = jnp.zeros((1, 1), F32)
    for s in range(secs - 1):
        rows = jnp.sum(jnp.where(sec_of == s, used, 0.0), axis=1, keepdims=True)
        most = jnp.maximum(most, jnp.max(rows, axis=0, keepdims=True))
    line = lax.broadcasted_iota(jnp.int32, (8, 128), 0)
    place = lax.broadcasted_iota(jnp.int32, (8, 128), 1)
    tables = []
    for s in (sec, jnp.maximum(sec - 1, 0)):

        def mine(value, s=s):
            value = jnp.broadcast_to(value[:1], (8, 128))
            return jnp.where(place < count, pltpu.roll(value, (128 - count * s) & 127, 1), 0.0)

        rows = mine(used)
        ends = rows
        for shift in (1, 2, 4, 8):
            ends = ends + jnp.where(place >= shift, pltpu.roll(ends, shift, 1), 0.0)
        lines = [groups[0], *groups, offsets.astype(F32)]
        table = ends - rows
        for i, value in enumerate(lines):
            table = jnp.where(line == i, mine(value), table)
        tables.append(table.astype(jnp.int32))
    return most, tables


def second_kernel(places, count, cells, secs, late, used, offsets, device, dims, *refs):
    n = len(places)
    vpieces, rpieces = refs[:n], refs[n : 2 * n]
    lfar, rfar, gref, sums, tables, vsrc, wsrc, vheld, rheld, lref, rref, ext, vsem, hsem, lsem, rsem = refs[2 * n :]
    width = gref.shape[1]
    nblk = vheld.shape[0]
    srow = lax.broadcasted_iota(jnp.int32, sums.shape, 0)
    envs = ((lfar, lref, lsem), (rfar, rref, rsem))
    copies = start_pieces(places, rpieces, rheld, hsem) + start_pieces(places, vpieces, vheld, vsem)
    bring_in(envs, count, copies)
    both = jnp.zeros((EXTRA, 128), F32)
    caps = []
    for place in range(nblk):
        part = rheld[place, pl.ds(count * width, EXTRA), :].astype(F32)
        ext[pl.ds(place * EXTRA, EXTRA), :] = part
        caps.append(part[count + 2 : count + 3])
        both = both + part
    turns = part[count + 3 : count + 4].astype(jnp.int32)
    most, (table, table_before) = layout_of(
        jnp.concatenate(caps, 0), turns, device[0], device[1], count, secs, late
    )
    tables[0], tables[1] = table, table_before
    both = jnp.sum(both, axis=1, keepdims=True)
    norm, num = both[count : count + 1], both[count + 1 : count + 2]
    firsts = jnp.where(srow == 2, num / norm, jnp.where(srow == 3, jnp.sqrt(cells / norm), 0.0))
    sums[...] = jnp.where(srow == 4, most, firsts)
    a_zero, scale = sums[2:3, :], sums[3:4, :]

    def slot(t):
        x = []
        squares = None
        for c in range(GROUPS):
            place, at, on = source_of(c, t, lambda i: offsets[i], device, count, nblk)
            v = only(on, block_of(vheld, place, at, width))
            r = block_of(rheld, place, at, width).astype(F32)
            alpha = ext[pl.ds(place * EXTRA + at, 1), :]
            w = scale * (r + (alpha - a_zero) * v.astype(F32))
            if c == 0:
                squares = total_of(w * w)
            w = only(on, w).astype(BF16)
            x.append(w)
            if c in used:
                vsrc[used.index(c), t] = v
                wsrc[used.index(c), t] = w
        g = jnp.where(inside(dims[t, 0], dims[t, 1], (width, width)), ham_sum(x, t, lref, rref), 0.0)
        gref[t] = g
        num = total_of(x[0].astype(F32) * g)
        sums[...] += jnp.where(srow == 0, squares, jnp.where(srow == 1, num, 0.0))

    over_slots(count, slot, HAM_STEP, arrival(envs, count))


def ritz_kernel(count, cells, ranks, parts, vsrc, wsrc, passed, coefs):
    width = vsrc.shape[2]
    both = parts[0]
    for i in range(1, parts.shape[0]):
        both = both + parts[i]
    squares, num = both[0:1, :] / cells, both[1:2, :] / cells
    a_zero, scale = parts[0, 2:3, :], parts[0, 3:4, :]
    beta = jnp.sqrt(squares + 1e-06)
    a_one = num / (beta * beta)
    half_gap = (a_zero - a_one) / 2.0
    ritz = (a_zero + a_one) / 2.0 - jnp.sqrt(half_gap * half_gap + beta * beta)
    gap_val = ritz - a_zero
    length = jnp.sqrt(beta * beta + gap_val * gap_val)
    from_v, from_w = beta / length * scale, gap_val / length / beta
    row = lax.broadcasted_iota(jnp.int32, coefs.shape, 0)
    coefs[...] = jnp.where(row == 0, from_v, jnp.where(row == 1, from_w, ritz))
    lane = lax.broadcasted_iota(jnp.int32, (width, width), 1)

    def slot(t):
        state = from_v * vsrc[0, t].astype(F32) + from_w * wsrc[0, t].astype(F32)
        kept = jnp.where(lane < ranks[t], state, 0.0).astype(BF16)
        passed[pl.ds(pl.multiple_of(t * width, width), width), :] = kept

    over_slots(count, slot, 2)


def stacked(blocks):
    width = blocks.shape[1]
    return jnp.concatenate([blocks[width * k : width * (k + 1)] for k in range(blocks.shape[0] // width)], 1)


def pack_kernel(count, late, used, table, coefs, vsrc, wsrc, far, out, lref, accs, sem):
    width = vsrc.shape[2]
    per = accs.shape[0]
    lane = lax.broadcasted_iota(jnp.int32, (width, width), 1)
    from_v, from_w = coefs[0:1, :], coefs[1:2, :]

    def envs(g):
        span, first, copies = pl.ds(g * per, per), 0, []
        for i, (c, low, end) in enumerate(late):
            copies.append(
                pltpu.make_async_copy(
                    far.at[pl.ds(low, end - low), c, span], lref.at[pl.ds(first, end - low), span], sem.at[i, g]
                )
            )
            first += end - low
        return copies

    for g in range(count // per):
        for copy in envs(g):
            copy.start()

    def kept_block(c, t, cap):
        i = used.index(c)
        state = from_v * vsrc[i, t].astype(F32) + from_w * wsrc[i, t].astype(F32)
        return jnp.where(lane < cap, state, 0.0)

    def slot(t, acc):
        own = kept_block(0, t, table[0, t]).T.astype(BF16)
        at, first = jnp.int32(0), 0
        for c, low, end in late:
            cap = table[1 + c, t]
            left = jnp.concatenate([lref[first + k, t] for k in range(end - low)], 0)
            inner = jnp.dot(left, kept_block(c, t, cap).astype(BF16), preferred_element_type=F32).astype(BF16)
            update = jnp.dot(own, stacked(inner), preferred_element_type=F32)
            for k in range(end - low):
                tile = at // width
                lead = at - tile * width
                turned = pltpu.roll(update[:, width * k : width * (k + 1)], lead, 1)
                acc[tile] = jnp.where(lane >= lead, turned, acc[tile])
                acc[tile + 1] = turned
                at = at + cap
            first += end - low
        return (at + width - 1) // width

    def step(g, carry):
        for copy in envs(g):
            copy.wait()
        tiles = [slot(g * per + p, accs.at[p]) for p in range(per)]
        for p in range(per):
            t = g * per + p
            high = (table[0, t] + 15) // 16 * 16

            def flush(tile, c, t=t, p=p, high=high):
                first = jnp.minimum(table[7, t] + tile * high, out.shape[0] - width)
                out[pl.ds(pl.multiple_of(first, 16), width), :] = accs[p, tile].astype(BF16)
                return c

            lax.fori_loop(0, tiles[p], flush, 0)
        return carry

    lax.fori_loop(0, count // per, step, 0)


def made_copies(share, out, made, sem, span, at):
    copies, first = [], 0
    for i, (c, low, end) in enumerate(share):
        copies.append(
            (made.at[pl.ds(first, end - low), span], out.at[pl.ds(low, end - low), c, span], sem.at[len(share) * at + i])
        )
        first += end - low
    return copies


def own_left(share, lenv, out, made, sem, count):
    every = pl.ds(0, count)
    into = [pltpu.make_async_copy(b, a, s) for a, b, s in made_copies(share, lenv, made, sem, every, 0)]
    for copy in into:
        copy.start()
    for copy in into:
        copy.wait()
    back = [pltpu.make_async_copy(a, b, s) for a, b, s in made_copies(share, out, made, sem, every, 0)]
    for copy in back:
        copy.start()
    for copy in back:
        copy.wait()


def send_out(share, out, made, sem, per):
    def after(g):
        for a, b, s in made_copies(share, out, made, sem, pl.ds(g * per, per), g):
            pltpu.make_async_copy(a, b, s).start()

    return after


def wait_out(share, out, made, sem, count, per):
    def wait(g, carry):
        for a, b, s in made_copies(share, out, made, sem, pl.ds(g * per, per), g):
            pltpu.make_async_copy(a, b, s).wait()
        return carry

    lax.fori_loop(0, count // per, wait, 0)


def unpack_kernel(count, late, table, first_sec, packed, lenv, so_far, out, made, sem):
    del so_far
    width = packed.shape[1]

    @pl.when(first_sec[0] == 1)
    def _():
        own_left(late, lenv, out, made, sem, count)

    @pl.when(first_sec[0] == 0)
    def _():
        lane = lax.broadcasted_iota(jnp.int32, (width, width), 1)

        def slot(t):
            high = (table[0, t] + 15) // 16 * 16
            at, first = jnp.int32(0), 0
            for c, low, end in late:
                mine = table[1 + c, t]
                valid = inside(table[0, t], mine, (width, width))
                for k in range(end - low):
                    tile = jnp.where(mine > 0, at // width, 0)
                    lead = at - at // width * width
                    near = packed[pl.ds(pl.multiple_of(table[7, t] + tile * high, 16), width), :]
                    next_one = packed[pl.ds(pl.multiple_of(table[7, t] + (tile + 1) * high, 16), width), :]
                    both = jnp.where(lane >= lead, near.astype(F32), next_one.astype(F32))
                    both = pltpu.roll(both, width - lead, 1)
                    made[first + k, t] = jnp.where(valid, both, 0.0).astype(BF16)
                    at = at + mine
                first += end - low

        per = step_of(count, UNPACK_STEP)
        over_slots(count, slot, UNPACK_STEP, None, send_out(late, out, made, sem, per))
        wait_out(late, out, made, sem, count, per)


def early_kernel(places, count, early, table, device, first_sec, *refs):
    pieces = refs[: len(places)]
    one, two, lenv, out, held, sent, made, sem, far_sem, out_sem = refs[len(places) :]
    width = made.shape[2]
    nblk = held.shape[0]

    @pl.when(first_sec[0] == 1)
    def _():
        own_left(early, lenv, out, made, out_sem, count)

    @pl.when(first_sec[0] == 0)
    def _():
        copies = start_pieces(places, pieces, held, sem)
        m = one.shape[0]
        copies.append(pltpu.make_async_copy(one, sent.at[pl.ds(0, m)], far_sem.at[0]))
        copies.append(pltpu.make_async_copy(two, sent.at[pl.ds(m, two.shape[0])], far_sem.at[1]))
        for copy in copies[-2:]:
            copy.start()
        for copy in copies:
            copy.wait()

        def slot(t):
            own = block_of(held, 0, t, width).astype(F32).T.astype(BF16)
            first = 0
            for c, low, end in early:
                place, at, on = source_of(c, t, lambda i: table[6, i], device, count, nblk)
                kept = only(on, block_of(held, place, at, width))
                left = jnp.concatenate([sent[first + k, t] for k in range(end - low)], 0)
                inner = jnp.dot(left, kept, preferred_element_type=F32).astype(BF16)
                update = jnp.dot(own, stacked(inner), preferred_element_type=F32).astype(BF16)
                for k in range(end - low):
                    made[first + k, t] = update[:, width * k : width * (k + 1)]
                first += end - low

        per = step_of(count, EARLY_STEP)
        over_slots(count, slot, EARLY_STEP, None, send_out(early, out, made, out_sem, per))
        wait_out(early, out, made, out_sem, count, per)


def shards(wavefunction, left_env, right_env, row_offset, sector_dims, trunc_ranks):
    start, lenv, renv = wavefunction[0], left_env[0], right_env[0]
    offsets, dims, ranks = row_offset[0], sector_dims[0], trunc_ranks[0]
    count, width = start.shape[0], start.shape[1]
    channels = lenv.shape[0]
    kinds = channels // GROUPS
    nblk, device = lax.axis_size("blk"), lax.axis_index("blk")
    body = count * width
    cells = float(count * nblk * width * width)
    lines = jnp.arange(width, dtype=jnp.int32)
    first_sec = jnp.reshape((lax.axis_index("sec") == 0).astype(jnp.int32), (1,))
    sec, secs = lax.axis_index("sec"), lax.axis_size("sec")
    mine = jnp.stack([device, sec]).astype(jnp.int32)
    by_group = lenv.reshape((kinds, GROUPS, count, width, width))
    at_once, then, late = shares(kinds)
    early = at_once + then
    used = (0,) + tuple(c for c, _, _ in late if c)
    n_then, n_late = (sum(end - low for _, low, end in share) for share in (then, late))
    n_early = channels - n_late

    mask_on = (lines[None, :, None] < dims[:, 0][:, None, None]) & (
        lines[None, None, :] < dims[:, 1][:, None, None]
    )
    vzero = jnp.where(mask_on, start, jnp.zeros_like(start))
    both = jnp.stack([jnp.minimum(dims[:, 1], ranks), offsets]).astype(F32)
    zero = jnp.zeros((), jnp.int32)
    own_lanes = lax.dynamic_update_slice(jnp.zeros((8, 128), F32), both, (zero, (count * sec).astype(jnp.int32)))
    table = own_lanes
    for shift in range(1, secs):
        table = table + lax.ppermute(own_lanes, "sec", [(i, (i + shift) % secs) for i in range(secs)])
    vpieces = gathered(vzero.reshape((body, width)))
    sent_one, table = lax.optimization_barrier((lenv[: len(at_once)], table))
    sent_one = onward(sent_one)
    places = tuple((place, first) for _, place, first in vpieces)
    n = len(places)
    vrows = [in_hbm(rows) for rows, _, _ in vpieces]
    anywhere = pl.BlockSpec(memory_space=pl.ANY)
    far = pl.BlockSpec(memory_space=pltpu.HBM)
    near = pl.BlockSpec(memory_space=pltpu.VMEM)
    scalars = pl.BlockSpec(memory_space=pltpu.SMEM)
    held = pltpu.VMEM((nblk, body + EXTRA, width), BF16)
    env = pltpu.VMEM(lenv.shape, BF16)
    wide_shape = jax.ShapeDtypeStruct((count, width, width), F32)
    pay_shape = jax.ShapeDtypeStruct((body + EXTRA, width), BF16)
    row_shape = jax.ShapeDtypeStruct((8, 128), F32)
    used_shape = jax.ShapeDtypeStruct((len(used), count, width, width), BF16)
    steps = count // step_of(count, HAM_STEP)

    def dma(*shape):
        return pltpu.SemaphoreType.DMA(shape)

    def call(kernel, name, in_specs, out_specs, out_shape, scratch=(), aliases=None, moved=1):
        return pl.pallas_call(
            kernel,
            in_specs=in_specs,
            out_specs=out_specs,
            out_shape=out_shape,
            scratch_shapes=list(scratch),
            input_output_aliases=aliases or {},
            compiler_params=params(),
            cost_estimate=pl.CostEstimate(flops=1, bytes_accessed=moved, transcendentals=0),
            name=name,
        )

    hzero, rpay, sent_two = call(
        functools.partial(first_kernel, places, count, then),
        "ham_first",
        [scalars] * 3 + [near] + [anywhere] * n + [far] * 2,
        [near, near, far],
        [wide_shape, pay_shape, jax.ShapeDtypeStruct((n_then, count, width, width), BF16)],
        [held, env, env, pltpu.VMEM((EXTRA, 128), F32), dma(n), dma(steps), dma(steps), dma(n_then)],
    )(offsets, mine, dims, table, *vrows, in_hbm(lenv), in_hbm(renv))

    rpieces = gathered(rpay)
    gone, sums, tables, vsrc, wsrc = call(
        functools.partial(second_kernel, places, count, cells, secs, late, used),
        "ham_second",
        [scalars] * 3 + [anywhere] * (2 * n) + [far] * 2,
        [near] * 5,
        [wide_shape, row_shape, jax.ShapeDtypeStruct((2, 8, 128), jnp.int32), used_shape, used_shape],
        [
            held, held, env, env, pltpu.VMEM((nblk * EXTRA, 128), F32),
            dma(n), dma(n), dma(steps), dma(steps),
        ],
    )(offsets, mine, dims, *vrows, *[rows for rows, _, _ in rpieces], in_hbm(lenv), in_hbm(renv))

    sent_two = onward(sent_two)
    parts = lax.all_gather(sums, "blk", axis=0)
    most_needed = sums[4, 0].astype(jnp.int32)
    table, table_before = tables[0], tables[1]

    most = count * n_late * width + SLACK
    out_shape = jax.ShapeDtypeStruct(by_group.shape, BF16)
    per = step_of(count, PACK_STEP)

    def finish(rows):
        def branch(parts, hzero, gone, vsrc, wsrc, sent_one, sent_two, table, table_before):
            passed, coefs = call(
                functools.partial(ritz_kernel, count, cells),
                "ritz",
                [scalars] + [near] * 3,
                [near] * 2,
                [jax.ShapeDtypeStruct((body, width), BF16), row_shape],
            )(ranks, parts, vsrc, wsrc)
            passed = onward(passed)
            packed = call(
                functools.partial(pack_kernel, count, late, used),
                "pack_update",
                [scalars] + [near] * 3 + [far],
                near,
                jax.ShapeDtypeStruct((rows, width), BF16),
                [
                    pltpu.VMEM((n_late, count, width, width), BF16),
                    pltpu.VMEM((per, n_late + 2, width, width), F32),
                    dma(len(late), count // per),
                ],
                moved=20 * 1024 * 1024,
            )(table, coefs, vsrc, wsrc, in_hbm(by_group))
            packed, passed = lax.optimization_barrier((packed, passed))
            arrived = onward(packed)
            kpieces = gathered(passed)
            rows_two, coefs = lax.optimization_barrier((kpieces[2][0], coefs))
            kpieces[2] = (rows_two, *kpieces[2][1:])
            from_v, from_w, ritz = coefs[0, 0], coefs[1, 0], coefs[2, 0]
            state_new = (from_v * vsrc[0].astype(F32) + from_w * wsrc[0].astype(F32)).astype(BF16)
            hstate_new = (from_v * hzero + from_w * gone).astype(BF16)
            so_far = call(
                functools.partial(early_kernel, places, count, early),
                "early_update",
                [scalars] * 3 + [anywhere] * n + [far] * 3,
                far,
                out_shape,
                [
                    held,
                    pltpu.VMEM((n_early, count, width, width), BF16),
                    pltpu.VMEM((n_early, count, width, width), BF16),
                    dma(n),
                    dma(2),
                    dma(len(early) * count),
                ],
            )(table_before, mine, first_sec, *[r for r, _, _ in kpieces], in_hbm(sent_one), in_hbm(sent_two), in_hbm(by_group))
            next_left = call(
                functools.partial(unpack_kernel, count, late),
                "unpack_update",
                [scalars] * 2 + [near] + [far] * 2,
                far,
                out_shape,
                [pltpu.VMEM((n_late, count, width, width), BF16), dma(len(late) * count)],
                {4: 0},
            )(table_before, first_sec, arrived, in_hbm(by_group), in_hbm(so_far))
            return state_new, hstate_new, ritz, next_left

        return branch

    sizes = [most * part // 64 // 16 * 16 for part in (28, 32)] + [most]
    tier = sum((most_needed + SLACK > size).astype(jnp.int32) for size in sizes[:-1])
    state_new, hstate_new, ritz, next_left = lax.switch(
        tier, [finish(size) for size in sizes], parts, hzero, gone, vsrc, wsrc, sent_one, sent_two, table, table_before
    )
    next_left = next_left.reshape((channels, count, width, width))
    return (state_new[None], hstate_new[None], jnp.reshape(ritz, (1,)), next_left[None])


def solution(mesh):
    placed = (
        P("sec", "blk", None, None),
        P("sec", None, "blk", None, None),
        P("sec", None, "blk", None, None),
        P("sec", None),
        P("sec", "blk", None),
        P("sec", "blk"),
    )
    return jax.shard_map(
        shards,
        mesh=mesh,
        in_specs=placed,
        out_specs=(
            P("sec", "blk", None, None),
            P("sec", "blk", None, None),
            P("sec"),
            P("sec", None, "blk", None, None),
        ),
        check_vma=False,
    )
```

```python
import functools

import jax
import jax.numpy as jnp
from jax import lax
from jax.experimental import pallas as pl
from jax.experimental.pallas import tpu as pltpu
from jax.sharding import PartitionSpec as P

GROUPS = 5
EXTRA = 16
SLACK = 128
HAM_STEP = 6
PACK_STEP = 2
UNPACK_STEP = 2
EARLY_STEP = 1
VMEM = 40 * 1024 * 1024
F32 = jnp.float32
BF16 = jnp.bfloat16


def params():
    return pltpu.CompilerParams(vmem_limit_bytes=VMEM)


def shares(kinds):
    first = tuple((c, 0, 1) for c in range(GROUPS))
    then = ((0, 1, kinds),)
    return first, then, ((1, 1, kinds), (2, 1, kinds), (3, 1, kinds), (4, 1, kinds))


def exchange(value, bit):
    length = lax.axis_size("blk")
    return lax.ppermute(value, "blk", [(i, i ^ bit) for i in range(length)])


def onward(value):
    length = lax.axis_size("sec")
    return lax.ppermute(value, "sec", [(i, i + 1) for i in range(length - 1)])


def in_hbm(value):
    return pltpu.with_memory_space_constraint(value, pltpu.HBM)


def gathered(value):
    nblk = lax.axis_size("blk")
    if nblk == 8:
        rows = value.shape[0]
        half = rows // 2 // 16 * 16
        four, two, one = exchange(value, 4), exchange(value, 2), exchange(value, 1)
        six_a, six_b = exchange(two[:half], 4), exchange(four[half:], 2)
        three, five = exchange(two, 1), exchange(four, 1)
        seven_a, seven_b = exchange(six_a, 1), exchange(six_b, 1)
        return [
            (value, 0, 0), (one, 1, 0), (two, 2, 0), (three, 3, 0), (four, 4, 0), (five, 5, 0),
            (six_a, 6, 0), (six_b, 6, half), (seven_a, 7, 0), (seven_b, 7, half),
        ]
    held = {0: value}
    bit = 1
    while bit < nblk:
        held.update({place | bit: exchange(rows, bit) for place, rows in list(held.items())})
        bit *= 2
    return [(held[place], place, 0) for place in range(nblk)]


def start_pieces(places, refs, scratch, sem):
    copies = []
    for (place, first), ref in zip(places, refs):
        copies.append(
            pltpu.make_async_copy(ref, scratch.at[place, pl.ds(first, ref.shape[0])], sem.at[len(copies)])
        )
        copies[-1].start()
    return copies


def source_of(c, t, offsets, device, count, nblk):
    mine = device[0]
    down = (mine - offsets(t)) & (nblk - 1)
    if c == 0:
        return 0, t, None
    if c in (1, 2):
        slot = jnp.maximum(t - 1, 0) if c == 1 else jnp.minimum(t + 1, count - 1)
        holder = (down + offsets(slot)) & (nblk - 1)
        return holder ^ mine, slot, (t >= 1) if c == 1 else (t <= count - 2)
    if c == 3:
        return ((mine - 1) & (nblk - 1)) ^ mine, t, down >= 1
    return ((mine + 1) & (nblk - 1)) ^ mine, t, down <= nblk - 2


def block_of(scratch, place, slot, width):
    return scratch[place, pl.ds(pl.multiple_of(slot * width, width), width), :]


def only(on, block):
    return block if on is None else jnp.where(on, block, jnp.zeros_like(block))


def ham_sum(x, t, lref, rref):
    kinds = lref.shape[0] // GROUPS
    zero = jnp.zeros_like(x[0])
    width = zero.shape[0]
    inner = [None] * lref.shape[0]
    for c0, c1 in ((0, 1), (2, 3)):
        both = jnp.concatenate(
            [jnp.concatenate([x[c0], zero], 1), jnp.concatenate([zero, x[c1]], 1)], 0
        )
        left = jnp.concatenate(
            [
                jnp.concatenate([lref[GROUPS * k + c0, t], lref[GROUPS * k + c1, t]], 1)
                for k in range(kinds)
            ],
            0,
        )
        pair = jnp.dot(left, both, preferred_element_type=F32).astype(BF16)
        for k in range(kinds):
            inner[GROUPS * k + c0] = pair[width * k : width * (k + 1), :width]
            inner[GROUPS * k + c1] = pair[width * k : width * (k + 1), width:]
    left = jnp.concatenate([lref[GROUPS * k + 4, t] for k in range(kinds)], 0)
    last = jnp.dot(left, x[4], preferred_element_type=F32).astype(BF16)
    for k in range(kinds):
        inner[GROUPS * k + 4] = last[width * k : width * (k + 1)]
    right = jnp.concatenate([rref[w, t] for w in range(lref.shape[0])], 1)
    return lax.dot_general(
        jnp.concatenate(inner, 1), right, (((1,), (1,)), ((), ())), preferred_element_type=F32
    )


def step_of(count, most):
    return max(p for p in range(1, most + 1) if count % p == 0)


def over_slots(count, body, most, before=None, after=None):
    per = step_of(count, most)

    def step(i, carry):
        if before is not None:
            before(i)
        for p in range(per):
            body(i * per + p)
        if after is not None:
            after(i)
        return carry

    lax.fori_loop(0, count // per, step, 0)


def env_copies(envs, count, i):
    per = step_of(count, HAM_STEP)
    span = pl.ds(i * per, per)
    return [pltpu.make_async_copy(far.at[:, span], near.at[:, span], sem.at[i]) for far, near, sem in envs]


def bring_in(envs, count, copies):
    for copy in env_copies(envs, count, 0):
        copy.start()
    for copy in copies:
        copy.wait()
    for i in range(1, count // step_of(count, HAM_STEP)):
        for copy in env_copies(envs, count, i):
            copy.start()


def arrival(envs, count):
    def before(i):
        for copy in env_copies(envs, count, i):
            copy.wait()

    return before


def inside(rows, cols, shape):
    row = lax.broadcasted_iota(jnp.int32, shape, 0)
    col = lax.broadcasted_iota(jnp.int32, shape, 1)
    return (row < rows) & (col < cols)


def total_of(value):
    return jnp.sum(jnp.sum(value, axis=0, keepdims=True), axis=1, keepdims=True)


def first_kernel(places, count, then, offsets, device, dims, table, *refs):
    pieces = refs[: len(places)]
    lfar, rfar, href, payload, sent, held, lref, rref, ext, sem, lsem, rsem, out_sem = refs[len(places) :]
    width = href.shape[1]
    nblk = held.shape[0]
    envs = ((lfar, lref, lsem), (rfar, rref, rsem))
    channels = [GROUPS * k + c for c, low, end in then for k in range(low, end)]
    outgoing = [pltpu.make_async_copy(lref.at[w], sent.at[i], out_sem.at[i]) for i, w in enumerate(channels)]
    ext[...] = jnp.zeros_like(ext)
    bring_in(envs, count, start_pieces(places, pieces, held, sem))
    row = lax.broadcasted_iota(jnp.int32, ext.shape, 0)
    lane = lax.broadcasted_iota(jnp.int32, ext.shape, 1)

    def slot(t):
        x = []
        for c in range(GROUPS):
            place, at, on = source_of(c, t, lambda i: offsets[i], device, count, nblk)
            x.append(only(on, block_of(held, place, at, width)))
        h = jnp.where(inside(dims[t, 0], dims[t, 1], (width, width)), ham_sum(x, t, lref, rref), 0.0)
        href[t] = h
        v = x[0].astype(F32)
        norm, num = total_of(v * v), total_of(v * h)
        alpha = jnp.where(norm > 1e-30, num / jnp.maximum(norm, 1e-30), 0.0).astype(BF16).astype(F32)
        payload[pl.ds(pl.multiple_of(t * width, width), width), :] = (h - alpha * v).astype(BF16)
        now = jnp.where(row == t, alpha, ext[...])
        ext[...] = now + jnp.where(row == count, norm, 0.0) + jnp.where(row == count + 1, num, 0.0)

    def before(i):
        arrival(envs, count)(i)

        @pl.when(i == count // step_of(count, HAM_STEP) - 1)
        def _():
            for copy in outgoing:
                copy.start()

    over_slots(count, slot, HAM_STEP, before)
    now = ext[...]
    high = now.astype(BF16).astype(F32)
    rest = now - high
    mid = rest.astype(BF16).astype(F32)
    low = rest - mid
    split = jnp.where(lane == 0, high, jnp.where(lane == 1, mid, jnp.where(lane == 2, low, 0.0)))
    extra = jnp.where(row < count, now, split)
    extra = jnp.where(row == count + 2, table[0:1, :], jnp.where(row == count + 3, table[1:2, :], extra))
    payload[pl.ds(count * width, EXTRA), :] = extra.astype(BF16)
    for copy in outgoing:
        copy.wait()


def layout_of(caps, offsets, device, sec, count, secs, late):
    nblk = caps.shape[0]
    row = lax.broadcasted_iota(jnp.int32, caps.shape, 0)
    lane = lax.broadcasted_iota(jnp.int32, caps.shape, 1)
    sec_of = sum((lane >= count * k).astype(jnp.int32) for k in range(1, secs))
    up = lane - count * sec_of
    down = ((row ^ device) - offsets) & (nblk - 1)

    def by_sector(value):
        rows = [jnp.sum(jnp.where(down == e, value, 0.0), axis=0, keepdims=True) for e in range(nblk)]
        return jnp.concatenate(rows, 0)

    def by_place(value):
        return sum(jnp.where(down == e, value[e : e + 1], 0.0) for e in range(nblk))

    own = by_sector(caps)
    none = jnp.zeros_like(own[:1])
    groups = [
        own,
        jnp.where(up >= 1, pltpu.roll(own, 1, 1), 0.0),
        jnp.where(up <= count - 2, pltpu.roll(own, 127, 1), 0.0),
        jnp.concatenate([none, own[:-1]], 0),
        jnp.concatenate([own[1:], none], 0),
    ]
    wide = sum((end - low) * groups[c] for c, low, end in late)
    used = jnp.floor((own + 15.0) / 16.0) * 16.0 * jnp.floor((wide + 127.0) / 128.0)
    groups = [by_place(value) for value in groups]
    used = by_place(used)
    most = jnp.zeros((1, 1), F32)
    for s in range(secs - 1):
        rows = jnp.sum(jnp.where(sec_of == s, used, 0.0), axis=1, keepdims=True)
        most = jnp.maximum(most, jnp.max(rows, axis=0, keepdims=True))
    line = lax.broadcasted_iota(jnp.int32, (8, 128), 0)
    place = lax.broadcasted_iota(jnp.int32, (8, 128), 1)
    tables = []
    for s in (sec, jnp.maximum(sec - 1, 0)):

        def mine(value, s=s):
            value = jnp.broadcast_to(value[:1], (8, 128))
            return jnp.where(place < count, pltpu.roll(value, (128 - count * s) & 127, 1), 0.0)

        rows = mine(used)
        ends = rows
        for shift in (1, 2, 4, 8):
            ends = ends + jnp.where(place >= shift, pltpu.roll(ends, shift, 1), 0.0)
        lines = [groups[0], *groups, offsets.astype(F32)]
        table = ends - rows
        for i, value in enumerate(lines):
            table = jnp.where(line == i, mine(value), table)
        tables.append(table.astype(jnp.int32))
    return most, tables


def second_kernel(places, count, cells, secs, late, used, offsets, device, dims, *refs):
    n = len(places)
    vpieces, rpieces = refs[:n], refs[n : 2 * n]
    lfar, rfar, gref, sums, tables, vsrc, wsrc, vheld, rheld, lref, rref, ext, vsem, hsem, lsem, rsem = refs[2 * n :]
    width = gref.shape[1]
    nblk = vheld.shape[0]
    srow = lax.broadcasted_iota(jnp.int32, sums.shape, 0)
    envs = ((lfar, lref, lsem), (rfar, rref, rsem))
    copies = start_pieces(places, rpieces, rheld, hsem) + start_pieces(places, vpieces, vheld, vsem)
    bring_in(envs, count, copies)
    both = jnp.zeros((EXTRA, 128), F32)
    caps = []
    for place in range(nblk):
        part = rheld[place, pl.ds(count * width, EXTRA), :].astype(F32)
        ext[pl.ds(place * EXTRA, EXTRA), :] = part
        caps.append(part[count + 2 : count + 3])
        both = both + part
    turns = part[count + 3 : count + 4].astype(jnp.int32)
    most, (table, table_before) = layout_of(
        jnp.concatenate(caps, 0), turns, device[0], device[1], count, secs, late
    )
    tables[0], tables[1] = table, table_before
    both = jnp.sum(both, axis=1, keepdims=True)
    norm, num = both[count : count + 1], both[count + 1 : count + 2]
    firsts = jnp.where(srow == 2, num / norm, jnp.where(srow == 3, jnp.sqrt(cells / norm), 0.0))
    sums[...] = jnp.where(srow == 4, most, firsts)
    a_zero, scale = sums[2:3, :], sums[3:4, :]

    def slot(t):
        x = []
        squares = None
        for c in range(GROUPS):
            place, at, on = source_of(c, t, lambda i: offsets[i], device, count, nblk)
            v = only(on, block_of(vheld, place, at, width))
            r = block_of(rheld, place, at, width).astype(F32)
            alpha = ext[pl.ds(place * EXTRA + at, 1), :]
            w = scale * (r + (alpha - a_zero) * v.astype(F32))
            if c == 0:
                squares = total_of(w * w)
            w = only(on, w).astype(BF16)
            x.append(w)
            if c in used:
                vsrc[used.index(c), t] = v
                wsrc[used.index(c), t] = w
        g = jnp.where(inside(dims[t, 0], dims[t, 1], (width, width)), ham_sum(x, t, lref, rref), 0.0)
        gref[t] = g
        num = total_of(x[0].astype(F32) * g)
        sums[...] += jnp.where(srow == 0, squares, jnp.where(srow == 1, num, 0.0))

    over_slots(count, slot, HAM_STEP, arrival(envs, count))


def ritz_kernel(count, cells, ranks, parts, vsrc, wsrc, passed, coefs):
    width = vsrc.shape[2]
    both = parts[0]
    for i in range(1, parts.shape[0]):
        both = both + parts[i]
    squares, num = both[0:1, :] / cells, both[1:2, :] / cells
    a_zero, scale = parts[0, 2:3, :], parts[0, 3:4, :]
    beta = jnp.sqrt(squares + 1e-06)
    a_one = num / (beta * beta)
    half_gap = (a_zero - a_one) / 2.0
    ritz = (a_zero + a_one) / 2.0 - jnp.sqrt(half_gap * half_gap + beta * beta)
    gap_val = ritz - a_zero
    length = jnp.sqrt(beta * beta + gap_val * gap_val)
    from_v, from_w = beta / length * scale, gap_val / length / beta
    row = lax.broadcasted_iota(jnp.int32, coefs.shape, 0)
    coefs[...] = jnp.where(row == 0, from_v, jnp.where(row == 1, from_w, ritz))
    lane = lax.broadcasted_iota(jnp.int32, (width, width), 1)

    def slot(t):
        state = from_v * vsrc[0, t].astype(F32) + from_w * wsrc[0, t].astype(F32)
        kept = jnp.where(lane < ranks[t], state, 0.0).astype(BF16)
        passed[pl.ds(pl.multiple_of(t * width, width), width), :] = kept

    over_slots(count, slot, 2)


def stacked(blocks):
    width = blocks.shape[1]
    return jnp.concatenate([blocks[width * k : width * (k + 1)] for k in range(blocks.shape[0] // width)], 1)


def pack_kernel(count, late, used, table, coefs, vsrc, wsrc, far, out, lref, accs, sem):
    width = vsrc.shape[2]
    per = accs.shape[0]
    lane = lax.broadcasted_iota(jnp.int32, (width, width), 1)
    from_v, from_w = coefs[0:1, :], coefs[1:2, :]

    def envs(g):
        span, first, copies = pl.ds(g * per, per), 0, []
        for i, (c, low, end) in enumerate(late):
            copies.append(
                pltpu.make_async_copy(
                    far.at[pl.ds(low, end - low), c, span], lref.at[pl.ds(first, end - low), span], sem.at[i, g]
                )
            )
            first += end - low
        return copies

    for g in range(count // per):
        for copy in envs(g):
            copy.start()

    def kept_block(c, t, cap):
        i = used.index(c)
        state = from_v * vsrc[i, t].astype(F32) + from_w * wsrc[i, t].astype(F32)
        return jnp.where(lane < cap, state, 0.0)

    def slot(t, acc):
        own = kept_block(0, t, table[0, t]).T.astype(BF16)
        at, first = jnp.int32(0), 0
        for c, low, end in late:
            cap = table[1 + c, t]
            left = jnp.concatenate([lref[first + k, t] for k in range(end - low)], 0)
            inner = jnp.dot(left, kept_block(c, t, cap).astype(BF16), preferred_element_type=F32).astype(BF16)
            update = jnp.dot(own, stacked(inner), preferred_element_type=F32)
            for k in range(end - low):
                tile = at // width
                lead = at - tile * width
                turned = pltpu.roll(update[:, width * k : width * (k + 1)], lead, 1)
                acc[tile] = jnp.where(lane >= lead, turned, acc[tile])
                acc[tile + 1] = turned
                at = at + cap
            first += end - low
        return (at + width - 1) // width

    def step(g, carry):
        for copy in envs(g):
            copy.wait()
        tiles = [slot(g * per + p, accs.at[p]) for p in range(per)]
        for p in range(per):
            t = g * per + p
            high = (table[0, t] + 15) // 16 * 16

            def flush(tile, c, t=t, p=p, high=high):
                first = jnp.minimum(table[7, t] + tile * high, out.shape[0] - width)
                out[pl.ds(pl.multiple_of(first, 16), width), :] = accs[p, tile].astype(BF16)
                return c

            lax.fori_loop(0, tiles[p], flush, 0)
        return carry

    lax.fori_loop(0, count // per, step, 0)


def made_copies(share, out, made, sem, span, at):
    copies, first = [], 0
    for i, (c, low, end) in enumerate(share):
        copies.append(
            (made.at[pl.ds(first, end - low), span], out.at[pl.ds(low, end - low), c, span], sem.at[len(share) * at + i])
        )
        first += end - low
    return copies


def own_left(share, lenv, out, made, sem, count):
    every = pl.ds(0, count)
    into = [pltpu.make_async_copy(b, a, s) for a, b, s in made_copies(share, lenv, made, sem, every, 0)]
    for copy in into:
        copy.start()
    for copy in into:
        copy.wait()
    back = [pltpu.make_async_copy(a, b, s) for a, b, s in made_copies(share, out, made, sem, every, 0)]
    for copy in back:
        copy.start()
    for copy in back:
        copy.wait()


def send_out(share, out, made, sem, per):
    def after(g):
        for a, b, s in made_copies(share, out, made, sem, pl.ds(g * per, per), g):
            pltpu.make_async_copy(a, b, s).start()

    return after


def wait_out(share, out, made, sem, count, per):
    def wait(g, carry):
        for a, b, s in made_copies(share, out, made, sem, pl.ds(g * per, per), g):
            pltpu.make_async_copy(a, b, s).wait()
        return carry

    lax.fori_loop(0, count // per, wait, 0)


def unpack_kernel(count, late, table, first_sec, packed, lenv, so_far, out, made, sem):
    del so_far
    width = packed.shape[1]

    @pl.when(first_sec[0] == 1)
    def _():
        own_left(late, lenv, out, made, sem, count)

    @pl.when(first_sec[0] == 0)
    def _():
        lane = lax.broadcasted_iota(jnp.int32, (width, width), 1)

        def slot(t):
            high = (table[0, t] + 15) // 16 * 16
            at, first = jnp.int32(0), 0
            for c, low, end in late:
                mine = table[1 + c, t]
                valid = inside(table[0, t], mine, (width, width))
                for k in range(end - low):
                    tile = jnp.where(mine > 0, at // width, 0)
                    lead = at - at // width * width
                    near = packed[pl.ds(pl.multiple_of(table[7, t] + tile * high, 16), width), :]
                    next_one = packed[pl.ds(pl.multiple_of(table[7, t] + (tile + 1) * high, 16), width), :]
                    both = jnp.where(lane >= lead, near.astype(F32), next_one.astype(F32))
                    both = pltpu.roll(both, width - lead, 1)
                    made[first + k, t] = jnp.where(valid, both, 0.0).astype(BF16)
                    at = at + mine
                first += end - low

        per = step_of(count, UNPACK_STEP)
        over_slots(count, slot, UNPACK_STEP, None, send_out(late, out, made, sem, per))
        wait_out(late, out, made, sem, count, per)


def early_kernel(places, count, early, table, device, first_sec, *refs):
    pieces = refs[: len(places)]
    one, two, lenv, out, held, sent, made, sem, far_sem, out_sem = refs[len(places) :]
    width = made.shape[2]
    nblk = held.shape[0]

    @pl.when(first_sec[0] == 1)
    def _():
        own_left(early, lenv, out, made, out_sem, count)

    @pl.when(first_sec[0] == 0)
    def _():
        copies = start_pieces(places, pieces, held, sem)
        m = one.shape[0]
        copies.append(pltpu.make_async_copy(one, sent.at[pl.ds(0, m)], far_sem.at[0]))
        copies.append(pltpu.make_async_copy(two, sent.at[pl.ds(m, two.shape[0])], far_sem.at[1]))
        for copy in copies[-2:]:
            copy.start()
        for copy in copies:
            copy.wait()

        def slot(t):
            own = block_of(held, 0, t, width).astype(F32).T.astype(BF16)
            first = 0
            for c, low, end in early:
                place, at, on = source_of(c, t, lambda i: table[6, i], device, count, nblk)
                kept = only(on, block_of(held, place, at, width))
                left = jnp.concatenate([sent[first + k, t] for k in range(end - low)], 0)
                inner = jnp.dot(left, kept, preferred_element_type=F32).astype(BF16)
                update = jnp.dot(own, stacked(inner), preferred_element_type=F32).astype(BF16)
                for k in range(end - low):
                    made[first + k, t] = update[:, width * k : width * (k + 1)]
                first += end - low

        per = step_of(count, EARLY_STEP)
        over_slots(count, slot, EARLY_STEP, None, send_out(early, out, made, out_sem, per))
        wait_out(early, out, made, out_sem, count, per)


def shards(wavefunction, left_env, right_env, row_offset, sector_dims, trunc_ranks):
    start, lenv, renv = wavefunction[0], left_env[0], right_env[0]
    offsets, dims, ranks = row_offset[0], sector_dims[0], trunc_ranks[0]
    count, width = start.shape[0], start.shape[1]
    channels = lenv.shape[0]
    kinds = channels // GROUPS
    nblk, device = lax.axis_size("blk"), lax.axis_index("blk")
    body = count * width
    cells = float(count * nblk * width * width)
    lines = jnp.arange(width, dtype=jnp.int32)
    first_sec = jnp.reshape((lax.axis_index("sec") == 0).astype(jnp.int32), (1,))
    sec, secs = lax.axis_index("sec"), lax.axis_size("sec")
    mine = jnp.stack([device, sec]).astype(jnp.int32)
    by_group = lenv.reshape((kinds, GROUPS, count, width, width))
    at_once, then, late = shares(kinds)
    early = at_once + then
    used = (0,) + tuple(c for c, _, _ in late if c)
    n_then, n_late = (sum(end - low for _, low, end in share) for share in (then, late))
    n_early = channels - n_late

    mask_on = (lines[None, :, None] < dims[:, 0][:, None, None]) & (
        lines[None, None, :] < dims[:, 1][:, None, None]
    )
    vzero = jnp.where(mask_on, start, jnp.zeros_like(start))
    both = jnp.stack([jnp.minimum(dims[:, 1], ranks), offsets]).astype(F32)
    zero = jnp.zeros((), jnp.int32)
    own_lanes = lax.dynamic_update_slice(jnp.zeros((8, 128), F32), both, (zero, (count * sec).astype(jnp.int32)))
    vpieces = gathered(vzero.reshape((body, width)))
    own_lanes, one = lax.optimization_barrier((own_lanes, vpieces[1][0]))
    vpieces[1] = (one, *vpieces[1][1:])
    table = own_lanes
    for shift in range(1, secs):
        table = table + lax.ppermute(own_lanes, "sec", [(i, (i + shift) % secs) for i in range(secs)])
    sent_one, table = lax.optimization_barrier((lenv[: len(at_once)], table))
    sent_one = onward(sent_one)
    places = tuple((place, first) for _, place, first in vpieces)
    n = len(places)
    vrows = [in_hbm(rows) for rows, _, _ in vpieces]
    anywhere = pl.BlockSpec(memory_space=pl.ANY)
    far = pl.BlockSpec(memory_space=pltpu.HBM)
    near = pl.BlockSpec(memory_space=pltpu.VMEM)
    scalars = pl.BlockSpec(memory_space=pltpu.SMEM)
    held = pltpu.VMEM((nblk, body + EXTRA, width), BF16)
    env = pltpu.VMEM(lenv.shape, BF16)
    wide_shape = jax.ShapeDtypeStruct((count, width, width), F32)
    pay_shape = jax.ShapeDtypeStruct((body + EXTRA, width), BF16)
    row_shape = jax.ShapeDtypeStruct((8, 128), F32)
    used_shape = jax.ShapeDtypeStruct((len(used), count, width, width), BF16)
    steps = count // step_of(count, HAM_STEP)

    def dma(*shape):
        return pltpu.SemaphoreType.DMA(shape)

    def call(kernel, name, in_specs, out_specs, out_shape, scratch=(), aliases=None, moved=1):
        return pl.pallas_call(
            kernel,
            in_specs=in_specs,
            out_specs=out_specs,
            out_shape=out_shape,
            scratch_shapes=list(scratch),
            input_output_aliases=aliases or {},
            compiler_params=params(),
            cost_estimate=pl.CostEstimate(flops=1, bytes_accessed=moved, transcendentals=0),
            name=name,
        )

    hzero, rpay, sent_two = call(
        functools.partial(first_kernel, places, count, then),
        "ham_first",
        [scalars] * 3 + [near] + [anywhere] * n + [far] * 2,
        [near, near, far],
        [wide_shape, pay_shape, jax.ShapeDtypeStruct((n_then, count, width, width), BF16)],
        [held, env, env, pltpu.VMEM((EXTRA, 128), F32), dma(n), dma(steps), dma(steps), dma(n_then)],
    )(offsets, mine, dims, table, *vrows, in_hbm(lenv), in_hbm(renv))

    rpieces = gathered(rpay)
    gone, sums, tables, vsrc, wsrc = call(
        functools.partial(second_kernel, places, count, cells, secs, late, used),
        "ham_second",
        [scalars] * 3 + [anywhere] * (2 * n) + [far] * 2,
        [near] * 5,
        [wide_shape, row_shape, jax.ShapeDtypeStruct((2, 8, 128), jnp.int32), used_shape, used_shape],
        [
            held, held, env, env, pltpu.VMEM((nblk * EXTRA, 128), F32),
            dma(n), dma(n), dma(steps), dma(steps),
        ],
    )(offsets, mine, dims, *vrows, *[rows for rows, _, _ in rpieces], in_hbm(lenv), in_hbm(renv))

    sent_two = onward(sent_two)
    parts = lax.all_gather(sums, "blk", axis=0)
    most_needed = sums[4, 0].astype(jnp.int32)
    table, table_before = tables[0], tables[1]

    most = count * n_late * width + SLACK
    out_shape = jax.ShapeDtypeStruct(by_group.shape, BF16)
    per = step_of(count, PACK_STEP)

    def finish(rows):
        def branch(parts, hzero, gone, vsrc, wsrc, sent_one, sent_two, table, table_before):
            passed, coefs = call(
                functools.partial(ritz_kernel, count, cells),
                "ritz",
                [scalars] + [near] * 3,
                [near] * 2,
                [jax.ShapeDtypeStruct((body, width), BF16), row_shape],
            )(ranks, parts, vsrc, wsrc)
            passed = onward(passed)
            packed = call(
                functools.partial(pack_kernel, count, late, used),
                "pack_update",
                [scalars] + [near] * 3 + [far],
                near,
                jax.ShapeDtypeStruct((rows, width), BF16),
                [
                    pltpu.VMEM((n_late, count, width, width), BF16),
                    pltpu.VMEM((per, n_late + 2, width, width), F32),
                    dma(len(late), count // per),
                ],
                moved=20 * 1024 * 1024,
            )(table, coefs, vsrc, wsrc, in_hbm(by_group))
            packed, passed = lax.optimization_barrier((packed, passed))
            arrived = onward(packed)
            kpieces = gathered(passed)
            rows_two, coefs = lax.optimization_barrier((kpieces[2][0], coefs))
            kpieces[2] = (rows_two, *kpieces[2][1:])
            from_v, from_w, ritz = coefs[0, 0], coefs[1, 0], coefs[2, 0]
            state_new = (from_v * vsrc[0].astype(F32) + from_w * wsrc[0].astype(F32)).astype(BF16)
            hstate_new = (from_v * hzero + from_w * gone).astype(BF16)
            so_far = call(
                functools.partial(early_kernel, places, count, early),
                "early_update",
                [scalars] * 3 + [anywhere] * n + [far] * 3,
                far,
                out_shape,
                [
                    held,
                    pltpu.VMEM((n_early, count, width, width), BF16),
                    pltpu.VMEM((n_early, count, width, width), BF16),
                    dma(n),
                    dma(2),
                    dma(len(early) * count),
                ],
            )(table_before, mine, first_sec, *[r for r, _, _ in kpieces], in_hbm(sent_one), in_hbm(sent_two), in_hbm(by_group))
            next_left = call(
                functools.partial(unpack_kernel, count, late),
                "unpack_update",
                [scalars] * 2 + [near] + [far] * 2,
                far,
                out_shape,
                [pltpu.VMEM((n_late, count, width, width), BF16), dma(len(late) * count)],
                {4: 0},
            )(table_before, first_sec, arrived, in_hbm(by_group), in_hbm(so_far))
            return state_new, hstate_new, ritz, next_left

        return branch

    sizes = [most * part // 64 // 16 * 16 for part in (28, 32)] + [most]
    tier = sum((most_needed + SLACK > size).astype(jnp.int32) for size in sizes[:-1])
    state_new, hstate_new, ritz, next_left = lax.switch(
        tier, [finish(size) for size in sizes], parts, hzero, gone, vsrc, wsrc, sent_one, sent_two, table, table_before
    )
    next_left = next_left.reshape((channels, count, width, width))
    return (state_new[None], hstate_new[None], jnp.reshape(ritz, (1,)), next_left[None])


def solution(mesh):
    placed = (
        P("sec", "blk", None, None),
        P("sec", None, "blk", None, None),
        P("sec", None, "blk", None, None),
        P("sec", None),
        P("sec", "blk", None),
        P("sec", "blk"),
    )
    return jax.shard_map(
        shards,
        mesh=mesh,
        in_specs=placed,
        out_specs=(
            P("sec", "blk", None, None),
            P("sec", "blk", None, None),
            P("sec"),
            P("sec", None, "blk", None, None),
        ),
        check_vma=False,
    )
```

```python
import functools

import jax
import jax.numpy as jnp
from jax import lax
from jax.experimental import pallas as pl
from jax.experimental.pallas import tpu as pltpu
from jax.sharding import PartitionSpec as P

GROUPS = 5
EXTRA = 16
SLACK = 128
HAM_STEP = 6
PACK_STEP = 2
UNPACK_STEP = 2
EARLY_STEP = 1
VMEM = 40 * 1024 * 1024
F32 = jnp.float32
BF16 = jnp.bfloat16


def params():
    return pltpu.CompilerParams(vmem_limit_bytes=VMEM)


def shares(kinds):
    first = tuple((c, 0, 1) for c in range(GROUPS))
    then = ((0, 1, kinds),)
    return first, then, ((1, 1, kinds), (2, 1, kinds), (3, 1, kinds), (4, 1, kinds))


def exchange(value, bit):
    length = lax.axis_size("blk")
    return lax.ppermute(value, "blk", [(i, i ^ bit) for i in range(length)])


def onward(value):
    length = lax.axis_size("sec")
    return lax.ppermute(value, "sec", [(i, i + 1) for i in range(length - 1)])


def in_hbm(value):
    return pltpu.with_memory_space_constraint(value, pltpu.HBM)


def gathered(value):
    nblk = lax.axis_size("blk")
    if nblk == 8:
        rows = value.shape[0]
        half = rows // 2 // 16 * 16
        four, two, one = exchange(value, 4), exchange(value, 2), exchange(value, 1)
        six_a, six_b = exchange(two[:half], 4), exchange(four[half:], 2)
        three, five = exchange(two, 1), exchange(four, 1)
        seven_a, seven_b = exchange(six_a, 1), exchange(six_b, 1)
        return [
            (value, 0, 0), (one, 1, 0), (two, 2, 0), (three, 3, 0), (four, 4, 0), (five, 5, 0),
            (six_a, 6, 0), (six_b, 6, half), (seven_a, 7, 0), (seven_b, 7, half),
        ]
    held = {0: value}
    bit = 1
    while bit < nblk:
        held.update({place | bit: exchange(rows, bit) for place, rows in list(held.items())})
        bit *= 2
    return [(held[place], place, 0) for place in range(nblk)]


def start_pieces(places, refs, scratch, sem):
    copies = []
    for (place, first), ref in zip(places, refs):
        copies.append(
            pltpu.make_async_copy(ref, scratch.at[place, pl.ds(first, ref.shape[0])], sem.at[len(copies)])
        )
        copies[-1].start()
    return copies


def source_of(c, t, offsets, device, count, nblk):
    mine = device[0]
    down = (mine - offsets(t)) & (nblk - 1)
    if c == 0:
        return 0, t, None
    if c in (1, 2):
        slot = jnp.maximum(t - 1, 0) if c == 1 else jnp.minimum(t + 1, count - 1)
        holder = (down + offsets(slot)) & (nblk - 1)
        return holder ^ mine, slot, (t >= 1) if c == 1 else (t <= count - 2)
    if c == 3:
        return ((mine - 1) & (nblk - 1)) ^ mine, t, down >= 1
    return ((mine + 1) & (nblk - 1)) ^ mine, t, down <= nblk - 2


def block_of(scratch, place, slot, width):
    return scratch[place, pl.ds(pl.multiple_of(slot * width, width), width), :]


def only(on, block):
    return block if on is None else jnp.where(on, block, jnp.zeros_like(block))


def ham_sum(x, t, lref, rref):
    kinds = lref.shape[0] // GROUPS
    zero = jnp.zeros_like(x[0])
    width = zero.shape[0]
    inner = [None] * lref.shape[0]
    for c0, c1 in ((0, 1), (2, 3)):
        both = jnp.concatenate(
            [jnp.concatenate([x[c0], zero], 1), jnp.concatenate([zero, x[c1]], 1)], 0
        )
        left = jnp.concatenate(
            [
                jnp.concatenate([lref[GROUPS * k + c0, t], lref[GROUPS * k + c1, t]], 1)
                for k in range(kinds)
            ],
            0,
        )
        pair = jnp.dot(left, both, preferred_element_type=F32).astype(BF16)
        for k in range(kinds):
            inner[GROUPS * k + c0] = pair[width * k : width * (k + 1), :width]
            inner[GROUPS * k + c1] = pair[width * k : width * (k + 1), width:]
    left = jnp.concatenate([lref[GROUPS * k + 4, t] for k in range(kinds)], 0)
    last = jnp.dot(left, x[4], preferred_element_type=F32).astype(BF16)
    for k in range(kinds):
        inner[GROUPS * k + 4] = last[width * k : width * (k + 1)]
    right = jnp.concatenate([rref[w, t] for w in range(lref.shape[0])], 1)
    return lax.dot_general(
        jnp.concatenate(inner, 1), right, (((1,), (1,)), ((), ())), preferred_element_type=F32
    )


def step_of(count, most):
    return max(p for p in range(1, most + 1) if count % p == 0)


def over_slots(count, body, most, before=None, after=None):
    per = step_of(count, most)

    def step(i, carry):
        if before is not None:
            before(i)
        for p in range(per):
            body(i * per + p)
        if after is not None:
            after(i)
        return carry

    lax.fori_loop(0, count // per, step, 0)


def env_copies(envs, count, i):
    per = step_of(count, HAM_STEP)
    span = pl.ds(i * per, per)
    return [pltpu.make_async_copy(far.at[:, span], near.at[:, span], sem.at[i]) for far, near, sem in envs]


def bring_in(envs, count, copies):
    for copy in env_copies(envs, count, 0):
        copy.start()
    for copy in copies:
        copy.wait()
    for i in range(1, count // step_of(count, HAM_STEP)):
        for copy in env_copies(envs, count, i):
            copy.start()


def arrival(envs, count):
    def before(i):
        for copy in env_copies(envs, count, i):
            copy.wait()

    return before


def inside(rows, cols, shape):
    row = lax.broadcasted_iota(jnp.int32, shape, 0)
    col = lax.broadcasted_iota(jnp.int32, shape, 1)
    return (row < rows) & (col < cols)


def total_of(value):
    return jnp.sum(jnp.sum(value, axis=0, keepdims=True), axis=1, keepdims=True)


def first_kernel(places, count, then, offsets, device, dims, table, *refs):
    pieces = refs[: len(places)]
    lfar, rfar, href, payload, sent, held, lref, rref, ext, sem, lsem, rsem, out_sem = refs[len(places) :]
    width = href.shape[1]
    nblk = held.shape[0]
    envs = ((lfar, lref, lsem), (rfar, rref, rsem))
    channels = [GROUPS * k + c for c, low, end in then for k in range(low, end)]
    outgoing = [pltpu.make_async_copy(lref.at[w], sent.at[i], out_sem.at[i]) for i, w in enumerate(channels)]
    ext[...] = jnp.zeros_like(ext)
    bring_in(envs, count, start_pieces(places, pieces, held, sem))
    row = lax.broadcasted_iota(jnp.int32, ext.shape, 0)
    lane = lax.broadcasted_iota(jnp.int32, ext.shape, 1)

    def slot(t):
        x = []
        for c in range(GROUPS):
            place, at, on = source_of(c, t, lambda i: offsets[i], device, count, nblk)
            x.append(only(on, block_of(held, place, at, width)))
        h = jnp.where(inside(dims[t, 0], dims[t, 1], (width, width)), ham_sum(x, t, lref, rref), 0.0)
        href[t] = h
        v = x[0].astype(F32)
        norm, num = total_of(v * v), total_of(v * h)
        alpha = jnp.where(norm > 1e-30, num / jnp.maximum(norm, 1e-30), 0.0).astype(BF16).astype(F32)
        payload[pl.ds(pl.multiple_of(t * width, width), width), :] = (h - alpha * v).astype(BF16)
        now = jnp.where(row == t, alpha, ext[...])
        now = now + jnp.where(row == count, norm, 0.0) + jnp.where(row == count + 1, num, 0.0)
        top = jnp.max(jnp.max(jnp.abs(h), axis=0, keepdims=True), axis=1, keepdims=True)
        ext[...] = jnp.where(row == count + 2, jnp.maximum(now, top), now)

    def before(i):
        arrival(envs, count)(i)

        @pl.when(i == count // step_of(count, HAM_STEP) - 1)
        def _():
            for copy in outgoing:
                copy.start()

    over_slots(count, slot, HAM_STEP, before)
    now = ext[...]
    high = now.astype(BF16).astype(F32)
    rest = now - high
    mid = rest.astype(BF16).astype(F32)
    low = rest - mid
    split = jnp.where(lane == 0, high, jnp.where(lane == 1, mid, jnp.where(lane == 2, low, 0.0)))
    split = jnp.where((row == count) & (lane == 3), now[count + 2 : count + 3], split)
    extra = jnp.where(row < count, now, split)
    extra = jnp.where(row == count + 2, table[0:1, :], jnp.where(row == count + 3, table[1:2, :], extra))
    payload[pl.ds(count * width, EXTRA), :] = extra.astype(BF16)
    for copy in outgoing:
        copy.wait()


def layout_of(caps, offsets, device, sec, count, secs, late):
    nblk = caps.shape[0]
    row = lax.broadcasted_iota(jnp.int32, caps.shape, 0)
    lane = lax.broadcasted_iota(jnp.int32, caps.shape, 1)
    sec_of = sum((lane >= count * k).astype(jnp.int32) for k in range(1, secs))
    up = lane - count * sec_of
    down = ((row ^ device) - offsets) & (nblk - 1)

    def by_sector(value):
        rows = [jnp.sum(jnp.where(down == e, value, 0.0), axis=0, keepdims=True) for e in range(nblk)]
        return jnp.concatenate(rows, 0)

    def by_place(value):
        return sum(jnp.where(down == e, value[e : e + 1], 0.0) for e in range(nblk))

    own = by_sector(caps)
    none = jnp.zeros_like(own[:1])
    groups = [
        own,
        jnp.where(up >= 1, pltpu.roll(own, 1, 1), 0.0),
        jnp.where(up <= count - 2, pltpu.roll(own, 127, 1), 0.0),
        jnp.concatenate([none, own[:-1]], 0),
        jnp.concatenate([own[1:], none], 0),
    ]
    wide = sum((end - low) * groups[c] for c, low, end in late)
    used = jnp.floor((own + 15.0) / 16.0) * 16.0 * jnp.floor((wide + 127.0) / 128.0)
    groups = [by_place(value) for value in groups]
    used = by_place(used)
    most = jnp.zeros((1, 1), F32)
    for s in range(secs - 1):
        rows = jnp.sum(jnp.where(sec_of == s, used, 0.0), axis=1, keepdims=True)
        most = jnp.maximum(most, jnp.max(rows, axis=0, keepdims=True))
    line = lax.broadcasted_iota(jnp.int32, (8, 128), 0)
    place = lax.broadcasted_iota(jnp.int32, (8, 128), 1)
    tables = []
    for s in (sec, jnp.maximum(sec - 1, 0)):

        def mine(value, s=s):
            value = jnp.broadcast_to(value[:1], (8, 128))
            return jnp.where(place < count, pltpu.roll(value, (128 - count * s) & 127, 1), 0.0)

        rows = mine(used)
        ends = rows
        for shift in (1, 2, 4, 8):
            ends = ends + jnp.where(place >= shift, pltpu.roll(ends, shift, 1), 0.0)
        lines = [groups[0], *groups, offsets.astype(F32)]
        table = ends - rows
        for i, value in enumerate(lines):
            table = jnp.where(line == i, mine(value), table)
        tables.append(table.astype(jnp.int32))
    return most, tables


def second_kernel(places, count, cells, secs, late, used, offsets, device, dims, *refs):
    n = len(places)
    vpieces, rpieces = refs[:n], refs[n : 2 * n]
    lfar, rfar, gref, sums, tables, vsrc, wsrc, vheld, rheld, lref, rref, ext, vsem, hsem, lsem, rsem = refs[2 * n :]
    width = gref.shape[1]
    nblk = vheld.shape[0]
    srow = lax.broadcasted_iota(jnp.int32, sums.shape, 0)
    envs = ((lfar, lref, lsem), (rfar, rref, rsem))
    copies = start_pieces(places, rpieces, rheld, hsem) + start_pieces(places, vpieces, vheld, vsem)
    bring_in(envs, count, copies)
    both = jnp.zeros((EXTRA, 128), F32)
    caps, tops = [], []
    for place in range(nblk):
        part = rheld[place, pl.ds(count * width, EXTRA), :].astype(F32)
        ext[pl.ds(place * EXTRA, EXTRA), :] = part
        caps.append(part[count + 2 : count + 3])
        tops.append(part[count : count + 1])
        both = both + part
    turns = part[count + 3 : count + 4].astype(jnp.int32)
    most, (table, table_before) = layout_of(
        jnp.concatenate(caps, 0), turns, device[0], device[1], count, secs, late
    )
    tables[0], tables[1] = table, table_before
    lane = lax.broadcasted_iota(jnp.int32, (1, 128), 1)
    top = jnp.where(lane == 3, functools.reduce(jnp.maximum, tops), 0.0)
    top = jnp.max(top, axis=1, keepdims=True)
    top = jnp.where(top > 0.0, top, 1.0)
    both = jnp.sum(jnp.where(lane < 3, both, 0.0), axis=1, keepdims=True)
    norm, num = both[count : count + 1], both[count + 1 : count + 2]
    firsts = jnp.where(srow == 2, num / norm, jnp.where(srow == 3, jnp.sqrt(cells / norm), 0.0))
    firsts = jnp.where(srow == 5, jnp.sqrt(cells / norm) * top, firsts)
    sums[...] = jnp.where(srow == 4, most, firsts)
    a_zero, scale = sums[2:3, :], 1.0 / top

    def slot(t):
        x = []
        squares = None
        for c in range(GROUPS):
            place, at, on = source_of(c, t, lambda i: offsets[i], device, count, nblk)
            v = only(on, block_of(vheld, place, at, width))
            r = block_of(rheld, place, at, width).astype(F32)
            alpha = ext[pl.ds(place * EXTRA + at, 1), :]
            w = scale * (r + (alpha - a_zero) * v.astype(F32))
            if c == 0:
                squares = total_of(w * w)
            w = only(on, w).astype(BF16)
            x.append(w)
            if c in used:
                vsrc[used.index(c), t] = v
                wsrc[used.index(c), t] = w
        g = jnp.where(inside(dims[t, 0], dims[t, 1], (width, width)), ham_sum(x, t, lref, rref), 0.0)
        gref[t] = g
        num = total_of(x[0].astype(F32) * g)
        sums[...] += jnp.where(srow == 0, squares, jnp.where(srow == 1, num, 0.0))

    over_slots(count, slot, HAM_STEP, arrival(envs, count))


def ritz_kernel(count, cells, ranks, parts, vsrc, wsrc, passed, coefs):
    width = vsrc.shape[2]
    both = parts[0]
    for i in range(1, parts.shape[0]):
        both = both + parts[i]
    squares, num = both[0:1, :] / cells, both[1:2, :] / cells
    a_zero, scale = parts[0, 2:3, :], parts[0, 3:4, :]
    unit = parts[0, 5:6, :]
    size = unit * jnp.sqrt(squares)
    beta = jnp.sqrt(size * size + 1e-06)
    in_units = beta / unit
    a_one = num / (in_units * in_units)
    half_gap = (a_zero - a_one) / 2.0
    ritz = (a_zero + a_one) / 2.0 - jnp.sqrt(half_gap * half_gap + beta * beta)
    gap_val = ritz - a_zero
    length = jnp.sqrt(beta * beta + gap_val * gap_val)
    from_v, from_w = beta / length * scale, gap_val / length / in_units
    row = lax.broadcasted_iota(jnp.int32, coefs.shape, 0)
    coefs[...] = jnp.where(row == 0, from_v, jnp.where(row == 1, from_w, ritz))
    lane = lax.broadcasted_iota(jnp.int32, (width, width), 1)

    def slot(t):
        state = from_v * vsrc[0, t].astype(F32) + from_w * wsrc[0, t].astype(F32)
        kept = jnp.where(lane < ranks[t], state, 0.0).astype(BF16)
        passed[pl.ds(pl.multiple_of(t * width, width), width), :] = kept

    over_slots(count, slot, 2)


def stacked(blocks):
    width = blocks.shape[1]
    return jnp.concatenate([blocks[width * k : width * (k + 1)] for k in range(blocks.shape[0] // width)], 1)


def pack_kernel(count, late, used, table, coefs, vsrc, wsrc, far, out, lref, accs, sem):
    width = vsrc.shape[2]
    per = accs.shape[0]
    lane = lax.broadcasted_iota(jnp.int32, (width, width), 1)
    from_v, from_w = coefs[0:1, :], coefs[1:2, :]

    def envs(g):
        span, first, copies = pl.ds(g * per, per), 0, []
        for i, (c, low, end) in enumerate(late):
            copies.append(
                pltpu.make_async_copy(
                    far.at[pl.ds(low, end - low), c, span], lref.at[pl.ds(first, end - low), span], sem.at[i, g]
                )
            )
            first += end - low
        return copies

    for g in range(count // per):
        for copy in envs(g):
            copy.start()

    def kept_block(c, t, cap):
        i = used.index(c)
        state = from_v * vsrc[i, t].astype(F32) + from_w * wsrc[i, t].astype(F32)
        return jnp.where(lane < cap, state, 0.0)

    def slot(t, acc):
        own = kept_block(0, t, table[0, t]).T.astype(BF16)
        at, first = jnp.int32(0), 0
        for c, low, end in late:
            cap = table[1 + c, t]
            left = jnp.concatenate([lref[first + k, t] for k in range(end - low)], 0)
            inner = jnp.dot(left, kept_block(c, t, cap).astype(BF16), preferred_element_type=F32).astype(BF16)
            update = jnp.dot(own, stacked(inner), preferred_element_type=F32)
            for k in range(end - low):
                tile = at // width
                lead = at - tile * width
                turned = pltpu.roll(update[:, width * k : width * (k + 1)], lead, 1)
                acc[tile] = jnp.where(lane >= lead, turned, acc[tile])
                acc[tile + 1] = turned
                at = at + cap
            first += end - low
        return (at + width - 1) // width

    def step(g, carry):
        for copy in envs(g):
            copy.wait()
        tiles = [slot(g * per + p, accs.at[p]) for p in range(per)]
        for p in range(per):
            t = g * per + p
            high = (table[0, t] + 15) // 16 * 16

            def flush(tile, c, t=t, p=p, high=high):
                first = jnp.minimum(table[7, t] + tile * high, out.shape[0] - width)
                out[pl.ds(pl.multiple_of(first, 16), width), :] = accs[p, tile].astype(BF16)
                return c

            lax.fori_loop(0, tiles[p], flush, 0)
        return carry

    lax.fori_loop(0, count // per, step, 0)


def made_copies(share, out, made, sem, span, at):
    copies, first = [], 0
    for i, (c, low, end) in enumerate(share):
        copies.append(
            (made.at[pl.ds(first, end - low), span], out.at[pl.ds(low, end - low), c, span], sem.at[len(share) * at + i])
        )
        first += end - low
    return copies


def own_left(share, lenv, out, made, sem, count):
    every = pl.ds(0, count)
    into = [pltpu.make_async_copy(b, a, s) for a, b, s in made_copies(share, lenv, made, sem, every, 0)]
    for copy in into:
        copy.start()
    for copy in into:
        copy.wait()
    back = [pltpu.make_async_copy(a, b, s) for a, b, s in made_copies(share, out, made, sem, every, 0)]
    for copy in back:
        copy.start()
    for copy in back:
        copy.wait()


def send_out(share, out, made, sem, per):
    def after(g):
        for a, b, s in made_copies(share, out, made, sem, pl.ds(g * per, per), g):
            pltpu.make_async_copy(a, b, s).start()

    return after


def wait_out(share, out, made, sem, count, per):
    def wait(g, carry):
        for a, b, s in made_copies(share, out, made, sem, pl.ds(g * per, per), g):
            pltpu.make_async_copy(a, b, s).wait()
        return carry

    lax.fori_loop(0, count // per, wait, 0)


def unpack_kernel(count, late, table, first_sec, packed, lenv, so_far, out, made, sem):
    del so_far
    width = packed.shape[1]

    @pl.when(first_sec[0] == 1)
    def _():
        own_left(late, lenv, out, made, sem, count)

    @pl.when(first_sec[0] == 0)
    def _():
        lane = lax.broadcasted_iota(jnp.int32, (width, width), 1)

        def slot(t):
            high = (table[0, t] + 15) // 16 * 16
            at, first = jnp.int32(0), 0
            for c, low, end in late:
                mine = table[1 + c, t]
                valid = inside(table[0, t], mine, (width, width))
                for k in range(end - low):
                    tile = jnp.where(mine > 0, at // width, 0)
                    lead = at - at // width * width
                    near = packed[pl.ds(pl.multiple_of(table[7, t] + tile * high, 16), width), :]
                    next_one = packed[pl.ds(pl.multiple_of(table[7, t] + (tile + 1) * high, 16), width), :]
                    both = jnp.where(lane >= lead, near.astype(F32), next_one.astype(F32))
                    both = pltpu.roll(both, width - lead, 1)
                    made[first + k, t] = jnp.where(valid, both, 0.0).astype(BF16)
                    at = at + mine
                first += end - low

        per = step_of(count, UNPACK_STEP)
        over_slots(count, slot, UNPACK_STEP, None, send_out(late, out, made, sem, per))
        wait_out(late, out, made, sem, count, per)


def early_kernel(places, count, early, table, device, first_sec, *refs):
    pieces = refs[: len(places)]
    one, two, lenv, out, held, sent, made, sem, far_sem, out_sem = refs[len(places) :]
    width = made.shape[2]
    nblk = held.shape[0]

    @pl.when(first_sec[0] == 1)
    def _():
        own_left(early, lenv, out, made, out_sem, count)

    @pl.when(first_sec[0] == 0)
    def _():
        copies = start_pieces(places, pieces, held, sem)
        m = one.shape[0]
        copies.append(pltpu.make_async_copy(one, sent.at[pl.ds(0, m)], far_sem.at[0]))
        copies.append(pltpu.make_async_copy(two, sent.at[pl.ds(m, two.shape[0])], far_sem.at[1]))
        for copy in copies[-2:]:
            copy.start()
        for copy in copies:
            copy.wait()

        def slot(t):
            own = block_of(held, 0, t, width).astype(F32).T.astype(BF16)
            first = 0
            for c, low, end in early:
                place, at, on = source_of(c, t, lambda i: table[6, i], device, count, nblk)
                kept = only(on, block_of(held, place, at, width))
                left = jnp.concatenate([sent[first + k, t] for k in range(end - low)], 0)
                inner = jnp.dot(left, kept, preferred_element_type=F32).astype(BF16)
                update = jnp.dot(own, stacked(inner), preferred_element_type=F32).astype(BF16)
                for k in range(end - low):
                    made[first + k, t] = update[:, width * k : width * (k + 1)]
                first += end - low

        per = step_of(count, EARLY_STEP)
        over_slots(count, slot, EARLY_STEP, None, send_out(early, out, made, out_sem, per))
        wait_out(early, out, made, out_sem, count, per)


def shards(wavefunction, left_env, right_env, row_offset, sector_dims, trunc_ranks):
    start, lenv, renv = wavefunction[0], left_env[0], right_env[0]
    offsets, dims, ranks = row_offset[0], sector_dims[0], trunc_ranks[0]
    count, width = start.shape[0], start.shape[1]
    channels = lenv.shape[0]
    kinds = channels // GROUPS
    nblk, device = lax.axis_size("blk"), lax.axis_index("blk")
    body = count * width
    cells = float(count * nblk * width * width)
    lines = jnp.arange(width, dtype=jnp.int32)
    first_sec = jnp.reshape((lax.axis_index("sec") == 0).astype(jnp.int32), (1,))
    sec, secs = lax.axis_index("sec"), lax.axis_size("sec")
    mine = jnp.stack([device, sec]).astype(jnp.int32)
    by_group = lenv.reshape((kinds, GROUPS, count, width, width))
    at_once, then, late = shares(kinds)
    early = at_once + then
    used = (0,) + tuple(c for c, _, _ in late if c)
    n_then, n_late = (sum(end - low for _, low, end in share) for share in (then, late))
    n_early = channels - n_late

    mask_on = (lines[None, :, None] < dims[:, 0][:, None, None]) & (
        lines[None, None, :] < dims[:, 1][:, None, None]
    )
    vzero = jnp.where(mask_on, start, jnp.zeros_like(start))
    both = jnp.stack([jnp.minimum(dims[:, 1], ranks), offsets]).astype(F32)
    zero = jnp.zeros((), jnp.int32)
    own_lanes = lax.dynamic_update_slice(jnp.zeros((8, 128), F32), both, (zero, (count * sec).astype(jnp.int32)))
    vpieces = gathered(vzero.reshape((body, width)))
    own_lanes, one = lax.optimization_barrier((own_lanes, vpieces[1][0]))
    vpieces[1] = (one, *vpieces[1][1:])
    table = own_lanes
    for shift in range(1, secs):
        table = table + lax.ppermute(own_lanes, "sec", [(i, (i + shift) % secs) for i in range(secs)])
    sent_one, table = lax.optimization_barrier((lenv[: len(at_once)], table))
    sent_one = onward(sent_one)
    places = tuple((place, first) for _, place, first in vpieces)
    n = len(places)
    vrows = [in_hbm(rows) for rows, _, _ in vpieces]
    anywhere = pl.BlockSpec(memory_space=pl.ANY)
    far = pl.BlockSpec(memory_space=pltpu.HBM)
    near = pl.BlockSpec(memory_space=pltpu.VMEM)
    scalars = pl.BlockSpec(memory_space=pltpu.SMEM)
    held = pltpu.VMEM((nblk, body + EXTRA, width), BF16)
    env = pltpu.VMEM(lenv.shape, BF16)
    wide_shape = jax.ShapeDtypeStruct((count, width, width), F32)
    pay_shape = jax.ShapeDtypeStruct((body + EXTRA, width), BF16)
    row_shape = jax.ShapeDtypeStruct((8, 128), F32)
    used_shape = jax.ShapeDtypeStruct((len(used), count, width, width), BF16)
    steps = count // step_of(count, HAM_STEP)

    def dma(*shape):
        return pltpu.SemaphoreType.DMA(shape)

    def call(kernel, name, in_specs, out_specs, out_shape, scratch=(), aliases=None, moved=1):
        return pl.pallas_call(
            kernel,
            in_specs=in_specs,
            out_specs=out_specs,
            out_shape=out_shape,
            scratch_shapes=list(scratch),
            input_output_aliases=aliases or {},
            compiler_params=params(),
            cost_estimate=pl.CostEstimate(flops=1, bytes_accessed=moved, transcendentals=0),
            name=name,
        )

    hzero, rpay, sent_two = call(
        functools.partial(first_kernel, places, count, then),
        "ham_first",
        [scalars] * 3 + [near] + [anywhere] * n + [far] * 2,
        [near, near, far],
        [wide_shape, pay_shape, jax.ShapeDtypeStruct((n_then, count, width, width), BF16)],
        [held, env, env, pltpu.VMEM((EXTRA, 128), F32), dma(n), dma(steps), dma(steps), dma(n_then)],
    )(offsets, mine, dims, table, *vrows, in_hbm(lenv), in_hbm(renv))

    rpieces = gathered(rpay)
    gone, sums, tables, vsrc, wsrc = call(
        functools.partial(second_kernel, places, count, cells, secs, late, used),
        "ham_second",
        [scalars] * 3 + [anywhere] * (2 * n) + [far] * 2,
        [near] * 5,
        [wide_shape, row_shape, jax.ShapeDtypeStruct((2, 8, 128), jnp.int32), used_shape, used_shape],
        [
            held, held, env, env, pltpu.VMEM((nblk * EXTRA, 128), F32),
            dma(n), dma(n), dma(steps), dma(steps),
        ],
    )(offsets, mine, dims, *vrows, *[rows for rows, _, _ in rpieces], in_hbm(lenv), in_hbm(renv))

    sent_two = onward(sent_two)
    parts = lax.all_gather(sums, "blk", axis=0)
    most_needed = sums[4, 0].astype(jnp.int32)
    table, table_before = tables[0], tables[1]

    most = count * n_late * width + SLACK
    out_shape = jax.ShapeDtypeStruct(by_group.shape, BF16)
    per = step_of(count, PACK_STEP)

    def finish(rows):
        def branch(parts, hzero, gone, vsrc, wsrc, sent_one, sent_two, table, table_before):
            passed, coefs = call(
                functools.partial(ritz_kernel, count, cells),
                "ritz",
                [scalars] + [near] * 3,
                [near] * 2,
                [jax.ShapeDtypeStruct((body, width), BF16), row_shape],
            )(ranks, parts, vsrc, wsrc)
            passed = onward(passed)
            packed = call(
                functools.partial(pack_kernel, count, late, used),
                "pack_update",
                [scalars] + [near] * 3 + [far],
                near,
                jax.ShapeDtypeStruct((rows, width), BF16),
                [
                    pltpu.VMEM((n_late, count, width, width), BF16),
                    pltpu.VMEM((per, n_late + 2, width, width), F32),
                    dma(len(late), count // per),
                ],
                moved=20 * 1024 * 1024,
            )(table, coefs, vsrc, wsrc, in_hbm(by_group))
            packed, passed = lax.optimization_barrier((packed, passed))
            arrived = onward(packed)
            kpieces = gathered(passed)
            rows_two, coefs = lax.optimization_barrier((kpieces[2][0], coefs))
            kpieces[2] = (rows_two, *kpieces[2][1:])
            from_v, from_w, ritz = coefs[0, 0], coefs[1, 0], coefs[2, 0]
            state_new = (from_v * vsrc[0].astype(F32) + from_w * wsrc[0].astype(F32)).astype(BF16)
            hstate_new = (from_v * hzero + from_w * gone).astype(BF16)
            so_far = call(
                functools.partial(early_kernel, places, count, early),
                "early_update",
                [scalars] * 3 + [anywhere] * n + [far] * 3,
                far,
                out_shape,
                [
                    held,
                    pltpu.VMEM((n_early, count, width, width), BF16),
                    pltpu.VMEM((n_early, count, width, width), BF16),
                    dma(n),
                    dma(2),
                    dma(len(early) * count),
                ],
            )(table_before, mine, first_sec, *[r for r, _, _ in kpieces], in_hbm(sent_one), in_hbm(sent_two), in_hbm(by_group))
            next_left = call(
                functools.partial(unpack_kernel, count, late),
                "unpack_update",
                [scalars] * 2 + [near] + [far] * 2,
                far,
                out_shape,
                [pltpu.VMEM((n_late, count, width, width), BF16), dma(len(late) * count)],
                {4: 0},
            )(table_before, first_sec, arrived, in_hbm(by_group), in_hbm(so_far))
            return state_new, hstate_new, ritz, next_left

        return branch

    sizes = [most * part // 64 // 16 * 16 for part in (28, 32)] + [most]
    tier = sum((most_needed + SLACK > size).astype(jnp.int32) for size in sizes[:-1])
    state_new, hstate_new, ritz, next_left = lax.switch(
        tier, [finish(size) for size in sizes], parts, hzero, gone, vsrc, wsrc, sent_one, sent_two, table, table_before
    )
    next_left = next_left.reshape((channels, count, width, width))
    return (state_new[None], hstate_new[None], jnp.reshape(ritz, (1,)), next_left[None])


def solution(mesh):
    placed = (
        P("sec", "blk", None, None),
        P("sec", None, "blk", None, None),
        P("sec", None, "blk", None, None),
        P("sec", None),
        P("sec", "blk", None),
        P("sec", "blk"),
    )
    return jax.shard_map(
        shards,
        mesh=mesh,
        in_specs=placed,
        out_specs=(
            P("sec", "blk", None, None),
            P("sec", "blk", None, None),
            P("sec"),
            P("sec", None, "blk", None, None),
        ),
        check_vma=False,
    )
```

```python
import functools

import jax
import jax.numpy as jnp
from jax import lax
from jax.experimental import pallas as pl
from jax.experimental.pallas import tpu as pltpu
from jax.sharding import PartitionSpec as P

GROUPS = 5
EXTRA = 16
SLACK = 128
HAM_STEP = 6
PACK_STEP = 2
UNPACK_STEP = 2
EARLY_STEP = 1
VMEM = 40 * 1024 * 1024
F32 = jnp.float32
BF16 = jnp.bfloat16


def params():
    return pltpu.CompilerParams(vmem_limit_bytes=VMEM)


def shares(kinds):
    first = tuple((c, 0, 1) for c in range(GROUPS))
    then = ((0, 1, kinds),)
    return first, then, ((1, 1, kinds), (2, 1, kinds), (3, 1, kinds), (4, 1, kinds))


def exchange(value, bit):
    length = lax.axis_size("blk")
    return lax.ppermute(value, "blk", [(i, i ^ bit) for i in range(length)])


def onward(value):
    length = lax.axis_size("sec")
    return lax.ppermute(value, "sec", [(i, i + 1) for i in range(length - 1)])


def in_hbm(value):
    return pltpu.with_memory_space_constraint(value, pltpu.HBM)


def gathered(value):
    nblk = lax.axis_size("blk")
    if nblk == 8:
        rows = value.shape[0]
        half = rows // 2 // 16 * 16
        four, two, one = exchange(value, 4), exchange(value, 2), exchange(value, 1)
        six_a, six_b = exchange(two[:half], 4), exchange(four[half:], 2)
        three, five = exchange(two, 1), exchange(four, 1)
        seven_a, seven_b = exchange(six_a, 1), exchange(six_b, 1)
        return [
            (value, 0, 0), (one, 1, 0), (two, 2, 0), (three, 3, 0), (four, 4, 0), (five, 5, 0),
            (six_a, 6, 0), (six_b, 6, half), (seven_a, 7, 0), (seven_b, 7, half),
        ]
    held = {0: value}
    bit = 1
    while bit < nblk:
        held.update({place | bit: exchange(rows, bit) for place, rows in list(held.items())})
        bit *= 2
    return [(held[place], place, 0) for place in range(nblk)]


def start_pieces(places, refs, scratch, sem):
    copies = []
    for (place, first), ref in zip(places, refs):
        copies.append(
            pltpu.make_async_copy(ref, scratch.at[place, pl.ds(first, ref.shape[0])], sem.at[len(copies)])
        )
        copies[-1].start()
    return copies


def source_of(c, t, offsets, device, count, nblk):
    mine = device[0]
    down = (mine - offsets(t)) & (nblk - 1)
    if c == 0:
        return 0, t, None
    if c in (1, 2):
        slot = jnp.maximum(t - 1, 0) if c == 1 else jnp.minimum(t + 1, count - 1)
        holder = (down + offsets(slot)) & (nblk - 1)
        return holder ^ mine, slot, (t >= 1) if c == 1 else (t <= count - 2)
    if c == 3:
        return ((mine - 1) & (nblk - 1)) ^ mine, t, down >= 1
    return ((mine + 1) & (nblk - 1)) ^ mine, t, down <= nblk - 2


def block_of(scratch, place, slot, width):
    return scratch[place, pl.ds(pl.multiple_of(slot * width, width), width), :]


def only(on, block):
    return block if on is None else jnp.where(on, block, jnp.zeros_like(block))


def ham_sum(x, t, lref, rref):
    kinds = lref.shape[0] // GROUPS
    zero = jnp.zeros_like(x[0])
    width = zero.shape[0]
    inner = [None] * lref.shape[0]
    for c0, c1 in ((0, 1), (2, 3)):
        both = jnp.concatenate(
            [jnp.concatenate([x[c0], zero], 1), jnp.concatenate([zero, x[c1]], 1)], 0
        )
        left = jnp.concatenate(
            [
                jnp.concatenate([lref[GROUPS * k + c0, t], lref[GROUPS * k + c1, t]], 1)
                for k in range(kinds)
            ],
            0,
        )
        pair = jnp.dot(left, both, preferred_element_type=F32).astype(BF16)
        for k in range(kinds):
            inner[GROUPS * k + c0] = pair[width * k : width * (k + 1), :width]
            inner[GROUPS * k + c1] = pair[width * k : width * (k + 1), width:]
    left = jnp.concatenate([lref[GROUPS * k + 4, t] for k in range(kinds)], 0)
    last = jnp.dot(left, x[4], preferred_element_type=F32).astype(BF16)
    for k in range(kinds):
        inner[GROUPS * k + 4] = last[width * k : width * (k + 1)]
    right = jnp.concatenate([rref[w, t] for w in range(lref.shape[0])], 1)
    return lax.dot_general(
        jnp.concatenate(inner, 1), right, (((1,), (1,)), ((), ())), preferred_element_type=F32
    )


def step_of(count, most):
    return max(p for p in range(1, most + 1) if count % p == 0)


def over_slots(count, body, most, before=None, after=None):
    per = step_of(count, most)

    def step(i, carry):
        if before is not None:
            before(i)
        for p in range(per):
            body(i * per + p)
        if after is not None:
            after(i)
        return carry

    lax.fori_loop(0, count // per, step, 0)


def env_copies(envs, count, i):
    per = step_of(count, HAM_STEP)
    span = pl.ds(i * per, per)
    return [pltpu.make_async_copy(far.at[:, span], near.at[:, span], sem.at[i]) for far, near, sem in envs]


def bring_in(envs, count, copies):
    for copy in env_copies(envs, count, 0):
        copy.start()
    for copy in copies:
        copy.wait()
    for i in range(1, count // step_of(count, HAM_STEP)):
        for copy in env_copies(envs, count, i):
            copy.start()


def arrival(envs, count):
    def before(i):
        for copy in env_copies(envs, count, i):
            copy.wait()

    return before


def inside(rows, cols, shape):
    row = lax.broadcasted_iota(jnp.int32, shape, 0)
    col = lax.broadcasted_iota(jnp.int32, shape, 1)
    return (row < rows) & (col < cols)


def total_of(value):
    return jnp.sum(jnp.sum(value, axis=0, keepdims=True), axis=1, keepdims=True)


def first_kernel(places, count, then, offsets, device, dims, table, *refs):
    pieces = refs[: len(places)]
    lfar, rfar, href, payload, sent, held, lref, rref, ext, sem, lsem, rsem, out_sem = refs[len(places) :]
    width = href.shape[1]
    nblk = held.shape[0]
    envs = ((lfar, lref, lsem), (rfar, rref, rsem))
    channels = [GROUPS * k + c for c, low, end in then for k in range(low, end)]
    outgoing = [pltpu.make_async_copy(lref.at[w], sent.at[i], out_sem.at[i]) for i, w in enumerate(channels)]
    ext[...] = jnp.zeros_like(ext)
    bring_in(envs, count, start_pieces(places, pieces, held, sem))
    row = lax.broadcasted_iota(jnp.int32, ext.shape, 0)
    lane = lax.broadcasted_iota(jnp.int32, ext.shape, 1)

    def slot(t):
        x = []
        for c in range(GROUPS):
            place, at, on = source_of(c, t, lambda i: offsets[i], device, count, nblk)
            x.append(only(on, block_of(held, place, at, width)))
        h = jnp.where(inside(dims[t, 0], dims[t, 1], (width, width)), ham_sum(x, t, lref, rref), 0.0)
        href[t] = h
        v = x[0].astype(F32)
        norm, num = total_of(v * v), total_of(v * h)
        alpha = jnp.where(norm > 1e-30, num / jnp.maximum(norm, 1e-30), 0.0).astype(BF16).astype(F32)
        payload[pl.ds(pl.multiple_of(t * width, width), width), :] = (h - alpha * v).astype(BF16)
        now = jnp.where(row == t, alpha, ext[...])
        now = now + jnp.where(row == count, norm, 0.0) + jnp.where(row == count + 1, num, 0.0)
        top = jnp.max(jnp.max(jnp.abs(h), axis=0, keepdims=True), axis=1, keepdims=True)
        ext[...] = jnp.where(row == count + 2, jnp.maximum(now, top), now)

    def before(i):
        arrival(envs, count)(i)

        @pl.when(i == count // step_of(count, HAM_STEP) - 1)
        def _():
            for copy in outgoing:
                copy.start()

    over_slots(count, slot, HAM_STEP, before)
    now = ext[...]
    high = now.astype(BF16).astype(F32)
    rest = now - high
    mid = rest.astype(BF16).astype(F32)
    low = rest - mid
    split = jnp.where(lane == 0, high, jnp.where(lane == 1, mid, jnp.where(lane == 2, low, 0.0)))
    split = jnp.where((row == count) & (lane == 3), now[count + 2 : count + 3], split)
    extra = jnp.where(row < count, now, split)
    extra = jnp.where(row == count + 2, table[0:1, :], jnp.where(row == count + 3, table[1:2, :], extra))
    payload[pl.ds(count * width, EXTRA), :] = extra.astype(BF16)
    for copy in outgoing:
        copy.wait()


def layout_of(caps, offsets, device, sec, count, secs, late):
    nblk = caps.shape[0]
    row = lax.broadcasted_iota(jnp.int32, caps.shape, 0)
    lane = lax.broadcasted_iota(jnp.int32, caps.shape, 1)
    sec_of = sum((lane >= count * k).astype(jnp.int32) for k in range(1, secs))
    up = lane - count * sec_of
    down = ((row ^ device) - offsets) & (nblk - 1)

    def by_sector(value):
        rows = [jnp.sum(jnp.where(down == e, value, 0.0), axis=0, keepdims=True) for e in range(nblk)]
        return jnp.concatenate(rows, 0)

    def by_place(value):
        return sum(jnp.where(down == e, value[e : e + 1], 0.0) for e in range(nblk))

    own = by_sector(caps)
    none = jnp.zeros_like(own[:1])
    groups = [
        own,
        jnp.where(up >= 1, pltpu.roll(own, 1, 1), 0.0),
        jnp.where(up <= count - 2, pltpu.roll(own, 127, 1), 0.0),
        jnp.concatenate([none, own[:-1]], 0),
        jnp.concatenate([own[1:], none], 0),
    ]
    wide = sum((end - low) * groups[c] for c, low, end in late)
    used = jnp.floor((own + 15.0) / 16.0) * 16.0 * jnp.floor((wide + 127.0) / 128.0)
    groups = [by_place(value) for value in groups]
    used = by_place(used)
    most = jnp.zeros((1, 1), F32)
    for s in range(secs - 1):
        rows = jnp.sum(jnp.where(sec_of == s, used, 0.0), axis=1, keepdims=True)
        most = jnp.maximum(most, jnp.max(rows, axis=0, keepdims=True))
    line = lax.broadcasted_iota(jnp.int32, (8, 128), 0)
    place = lax.broadcasted_iota(jnp.int32, (8, 128), 1)
    tables = []
    for s in (sec, jnp.maximum(sec - 1, 0)):

        def mine(value, s=s):
            value = jnp.broadcast_to(value[:1], (8, 128))
            return jnp.where(place < count, pltpu.roll(value, (128 - count * s) & 127, 1), 0.0)

        rows = mine(used)
        ends = rows
        for shift in (1, 2, 4, 8):
            ends = ends + jnp.where(place >= shift, pltpu.roll(ends, shift, 1), 0.0)
        lines = [groups[0], *groups, offsets.astype(F32)]
        table = ends - rows
        for i, value in enumerate(lines):
            table = jnp.where(line == i, mine(value), table)
        tables.append(table.astype(jnp.int32))
    return most, tables


def second_kernel(places, count, cells, secs, late, used, offsets, device, dims, *refs):
    n = len(places)
    vpieces, rpieces = refs[:n], refs[n : 2 * n]
    lfar, rfar, gref, sums, tables, vsrc, wsrc, vheld, rheld, lref, rref, ext, vsem, hsem, lsem, rsem = refs[2 * n :]
    width = gref.shape[1]
    nblk = vheld.shape[0]
    srow = lax.broadcasted_iota(jnp.int32, sums.shape, 0)
    envs = ((lfar, lref, lsem), (rfar, rref, rsem))
    copies = start_pieces(places, rpieces, rheld, hsem) + start_pieces(places, vpieces, vheld, vsem)
    bring_in(envs, count, copies)
    both = jnp.zeros((EXTRA, 128), F32)
    caps, tops = [], []
    for place in range(nblk):
        part = rheld[place, pl.ds(count * width, EXTRA), :].astype(F32)
        ext[pl.ds(place * EXTRA, EXTRA), :] = part
        caps.append(part[count + 2 : count + 3])
        tops.append(part[count : count + 1])
        both = both + part
    turns = part[count + 3 : count + 4].astype(jnp.int32)
    most, (table, table_before) = layout_of(
        jnp.concatenate(caps, 0), turns, device[0], device[1], count, secs, late
    )
    tables[0], tables[1] = table, table_before
    lane = lax.broadcasted_iota(jnp.int32, (1, 128), 1)
    top = jnp.where(lane == 3, functools.reduce(jnp.maximum, tops), 0.0)
    top = jnp.max(top, axis=1, keepdims=True)
    top = jnp.where(top > 0.0, top, 1.0)
    both = jnp.sum(jnp.where(lane < 3, both, 0.0), axis=1, keepdims=True)
    norm, num = both[count : count + 1], both[count + 1 : count + 2]
    firsts = jnp.where(srow == 2, num / norm, jnp.where(srow == 3, jnp.sqrt(cells / norm), 0.0))
    firsts = jnp.where(srow == 5, jnp.sqrt(cells / norm) * top, firsts)
    sums[...] = jnp.where(srow == 4, most, firsts)
    a_zero, scale = sums[2:3, :], 1.0 / top

    def slot(t):
        x = []
        squares = None
        for c in range(GROUPS):
            place, at, on = source_of(c, t, lambda i: offsets[i], device, count, nblk)
            v = only(on, block_of(vheld, place, at, width))
            r = block_of(rheld, place, at, width).astype(F32)
            alpha = ext[pl.ds(place * EXTRA + at, 1), :]
            w = scale * (r + (alpha - a_zero) * v.astype(F32))
            if c == 0:
                squares = total_of(w * w)
            w = only(on, w).astype(BF16)
            x.append(w)
            if c in used:
                vsrc[used.index(c), t] = v
                wsrc[used.index(c), t] = w
        g = jnp.where(inside(dims[t, 0], dims[t, 1], (width, width)), ham_sum(x, t, lref, rref), 0.0)
        gref[t] = g
        num = total_of(x[0].astype(F32) * g)
        sums[...] += jnp.where(srow == 0, squares, jnp.where(srow == 1, num, 0.0))

    over_slots(count, slot, HAM_STEP, arrival(envs, count))


def ritz_kernel(count, cells, ranks, parts, vsrc, wsrc, passed, coefs):
    width = vsrc.shape[2]
    both = parts[0]
    for i in range(1, parts.shape[0]):
        both = both + parts[i]
    squares, num = both[0:1, :] / cells, both[1:2, :] / cells
    a_zero, scale = parts[0, 2:3, :], parts[0, 3:4, :]
    unit = parts[0, 5:6, :]
    size = unit * jnp.sqrt(squares)
    beta = jnp.sqrt(size * size + 1e-06)
    in_units = beta / unit
    a_one = num / (in_units * in_units)
    half_gap = (a_zero - a_one) / 2.0
    ritz = (a_zero + a_one) / 2.0 - jnp.sqrt(half_gap * half_gap + beta * beta)
    gap_val = ritz - a_zero
    length = jnp.sqrt(beta * beta + gap_val * gap_val)
    from_v, from_w = beta / length * scale, gap_val / length / in_units
    row = lax.broadcasted_iota(jnp.int32, coefs.shape, 0)
    coefs[...] = jnp.where(row == 0, from_v, jnp.where(row == 1, from_w, ritz))
    lane = lax.broadcasted_iota(jnp.int32, (width, width), 1)

    def slot(t):
        state = from_v * vsrc[0, t].astype(F32) + from_w * wsrc[0, t].astype(F32)
        kept = jnp.where(lane < ranks[t], state, 0.0).astype(BF16)
        passed[pl.ds(pl.multiple_of(t * width, width), width), :] = kept

    over_slots(count, slot, 2)


def stacked(blocks):
    width = blocks.shape[1]
    return jnp.concatenate([blocks[width * k : width * (k + 1)] for k in range(blocks.shape[0] // width)], 1)


def pack_kernel(count, late, used, table, coefs, vsrc, wsrc, far, out, lref, accs, sem):
    width = vsrc.shape[2]
    per = accs.shape[0]
    lane = lax.broadcasted_iota(jnp.int32, (width, width), 1)
    from_v, from_w = coefs[0:1, :], coefs[1:2, :]

    def envs(g):
        span, first, copies = pl.ds(g * per, per), 0, []
        for i, (c, low, end) in enumerate(late):
            copies.append(
                pltpu.make_async_copy(
                    far.at[pl.ds(low, end - low), c, span], lref.at[pl.ds(first, end - low), span], sem.at[i, g]
                )
            )
            first += end - low
        return copies

    for g in range(count // per):
        for copy in envs(g):
            copy.start()

    def kept_block(c, t, cap):
        i = used.index(c)
        state = from_v * vsrc[i, t].astype(F32) + from_w * wsrc[i, t].astype(F32)
        return jnp.where(lane < cap, state, 0.0)

    def slot(t, acc):
        own = kept_block(0, t, table[0, t]).T.astype(BF16)
        at, first = jnp.int32(0), 0
        for c, low, end in late:
            cap = table[1 + c, t]
            left = jnp.concatenate([lref[first + k, t] for k in range(end - low)], 0)
            inner = jnp.dot(left, kept_block(c, t, cap).astype(BF16), preferred_element_type=F32).astype(BF16)
            update = jnp.dot(own, stacked(inner), preferred_element_type=F32)
            for k in range(end - low):
                tile = at // width
                lead = at - tile * width
                turned = pltpu.roll(update[:, width * k : width * (k + 1)], lead, 1)
                acc[tile] = jnp.where(lane >= lead, turned, acc[tile])
                acc[tile + 1] = turned
                at = at + cap
            first += end - low
        return (at + width - 1) // width

    def step(g, carry):
        for copy in envs(g):
            copy.wait()
        tiles = [slot(g * per + p, accs.at[p]) for p in range(per)]
        for p in range(per):
            t = g * per + p
            high = (table[0, t] + 15) // 16 * 16

            def flush(tile, c, t=t, p=p, high=high):
                first = jnp.minimum(table[7, t] + tile * high, out.shape[0] - width)
                out[pl.ds(pl.multiple_of(first, 16), width), :] = accs[p, tile].astype(BF16)
                return c

            lax.fori_loop(0, tiles[p], flush, 0)
        return carry

    lax.fori_loop(0, count // per, step, 0)


def made_copies(share, out, made, sem, span, at):
    copies, first = [], 0
    for i, (c, low, end) in enumerate(share):
        copies.append(
            (made.at[pl.ds(first, end - low), span], out.at[pl.ds(low, end - low), c, span], sem.at[len(share) * at + i])
        )
        first += end - low
    return copies


def own_left(share, lenv, out, made, sem, count):
    every = pl.ds(0, count)
    into = [pltpu.make_async_copy(b, a, s) for a, b, s in made_copies(share, lenv, made, sem, every, 0)]
    for copy in into:
        copy.start()
    for copy in into:
        copy.wait()
    back = [pltpu.make_async_copy(a, b, s) for a, b, s in made_copies(share, out, made, sem, every, 0)]
    for copy in back:
        copy.start()
    for copy in back:
        copy.wait()


def send_out(share, out, made, sem, per):
    def after(g):
        for a, b, s in made_copies(share, out, made, sem, pl.ds(g * per, per), g):
            pltpu.make_async_copy(a, b, s).start()

    return after


def wait_out(share, out, made, sem, count, per):
    def wait(g, carry):
        for a, b, s in made_copies(share, out, made, sem, pl.ds(g * per, per), g):
            pltpu.make_async_copy(a, b, s).wait()
        return carry

    lax.fori_loop(0, count // per, wait, 0)


def unpack_kernel(count, late, table, first_sec, packed, lenv, so_far, out, made, sem):
    del so_far
    width = packed.shape[1]

    @pl.when(first_sec[0] == 1)
    def _():
        own_left(late, lenv, out, made, sem, count)

    @pl.when(first_sec[0] == 0)
    def _():
        lane = lax.broadcasted_iota(jnp.int32, (width, width), 1)

        def slot(t):
            high = (table[0, t] + 15) // 16 * 16
            at, first = jnp.int32(0), 0
            for c, low, end in late:
                mine = table[1 + c, t]
                valid = inside(table[0, t], mine, (width, width))
                for k in range(end - low):
                    tile = jnp.where(mine > 0, at // width, 0)
                    lead = at - at // width * width
                    near = packed[pl.ds(pl.multiple_of(table[7, t] + tile * high, 16), width), :]
                    next_one = packed[pl.ds(pl.multiple_of(table[7, t] + (tile + 1) * high, 16), width), :]
                    both = jnp.where(lane >= lead, near.astype(F32), next_one.astype(F32))
                    both = pltpu.roll(both, width - lead, 1)
                    made[first + k, t] = jnp.where(valid, both, 0.0).astype(BF16)
                    at = at + mine
                first += end - low

        per = step_of(count, UNPACK_STEP)
        over_slots(count, slot, UNPACK_STEP, None, send_out(late, out, made, sem, per))
        wait_out(late, out, made, sem, count, per)


def early_kernel(places, count, early, table, device, first_sec, *refs):
    pieces = refs[: len(places)]
    one, two, lenv, out, held, sent, made, sem, far_sem, out_sem = refs[len(places) :]
    width = made.shape[2]
    nblk = held.shape[0]

    @pl.when(first_sec[0] == 1)
    def _():
        own_left(early, lenv, out, made, out_sem, count)

    @pl.when(first_sec[0] == 0)
    def _():
        copies = start_pieces(places, pieces, held, sem)
        m = one.shape[0]
        copies.append(pltpu.make_async_copy(one, sent.at[pl.ds(0, m)], far_sem.at[0]))
        copies.append(pltpu.make_async_copy(two, sent.at[pl.ds(m, two.shape[0])], far_sem.at[1]))
        for copy in copies[-2:]:
            copy.start()
        for copy in copies:
            copy.wait()

        def slot(t):
            own = block_of(held, 0, t, width).astype(F32).T.astype(BF16)
            first = 0
            for c, low, end in early:
                place, at, on = source_of(c, t, lambda i: table[6, i], device, count, nblk)
                kept = only(on, block_of(held, place, at, width))
                left = jnp.concatenate([sent[first + k, t] for k in range(end - low)], 0)
                inner = jnp.dot(left, kept, preferred_element_type=F32).astype(BF16)
                update = jnp.dot(own, stacked(inner), preferred_element_type=F32).astype(BF16)
                for k in range(end - low):
                    made[first + k, t] = update[:, width * k : width * (k + 1)]
                first += end - low

        per = step_of(count, EARLY_STEP)
        over_slots(count, slot, EARLY_STEP, None, send_out(early, out, made, out_sem, per))
        wait_out(early, out, made, out_sem, count, per)


def shards(wavefunction, left_env, right_env, row_offset, sector_dims, trunc_ranks):
    start, lenv, renv = wavefunction[0], left_env[0], right_env[0]
    offsets, dims, ranks = row_offset[0], sector_dims[0], trunc_ranks[0]
    count, width = start.shape[0], start.shape[1]
    channels = lenv.shape[0]
    kinds = channels // GROUPS
    nblk, device = lax.axis_size("blk"), lax.axis_index("blk")
    body = count * width
    cells = float(count * nblk * width * width)
    lines = jnp.arange(width, dtype=jnp.int32)
    first_sec = jnp.reshape((lax.axis_index("sec") == 0).astype(jnp.int32), (1,))
    sec, secs = lax.axis_index("sec"), lax.axis_size("sec")
    mine = jnp.stack([device, sec]).astype(jnp.int32)
    by_group = lenv.reshape((kinds, GROUPS, count, width, width))
    at_once, then, late = shares(kinds)
    early = at_once + then
    used = (0,) + tuple(c for c, _, _ in late if c)
    n_then, n_late = (sum(end - low for _, low, end in share) for share in (then, late))
    n_early = channels - n_late

    mask_on = (lines[None, :, None] < dims[:, 0][:, None, None]) & (
        lines[None, None, :] < dims[:, 1][:, None, None]
    )
    vzero = jnp.where(mask_on, start, jnp.zeros_like(start))
    both = jnp.stack([jnp.minimum(dims[:, 1], ranks), offsets]).astype(F32)
    zero = jnp.zeros((), jnp.int32)
    own_lanes = lax.dynamic_update_slice(jnp.zeros((8, 128), F32), both, (zero, (count * sec).astype(jnp.int32)))
    vpieces = gathered(vzero.reshape((body, width)))
    own_lanes, one = lax.optimization_barrier((own_lanes, vpieces[1][0]))
    vpieces[1] = (one, *vpieces[1][1:])
    table = own_lanes
    for shift in range(1, secs):
        table = table + lax.ppermute(own_lanes, "sec", [(i, (i + shift) % secs) for i in range(secs)])
    sent_one, table = lax.optimization_barrier((lenv[: len(at_once)], table))
    sent_one = onward(sent_one)
    places = tuple((place, first) for _, place, first in vpieces)
    n = len(places)
    vrows = [in_hbm(rows) for rows, _, _ in vpieces]
    anywhere = pl.BlockSpec(memory_space=pl.ANY)
    far = pl.BlockSpec(memory_space=pltpu.HBM)
    near = pl.BlockSpec(memory_space=pltpu.VMEM)
    scalars = pl.BlockSpec(memory_space=pltpu.SMEM)
    held = pltpu.VMEM((nblk, body + EXTRA, width), BF16)
    env = pltpu.VMEM(lenv.shape, BF16)
    wide_shape = jax.ShapeDtypeStruct((count, width, width), F32)
    pay_shape = jax.ShapeDtypeStruct((body + EXTRA, width), BF16)
    row_shape = jax.ShapeDtypeStruct((8, 128), F32)
    used_shape = jax.ShapeDtypeStruct((len(used), count, width, width), BF16)
    steps = count // step_of(count, HAM_STEP)

    def dma(*shape):
        return pltpu.SemaphoreType.DMA(shape)

    def call(kernel, name, in_specs, out_specs, out_shape, scratch=(), aliases=None, moved=1):
        return pl.pallas_call(
            kernel,
            in_specs=in_specs,
            out_specs=out_specs,
            out_shape=out_shape,
            scratch_shapes=list(scratch),
            input_output_aliases=aliases or {},
            compiler_params=params(),
            cost_estimate=pl.CostEstimate(flops=1, bytes_accessed=moved, transcendentals=0),
            name=name,
        )

    hzero, rpay, sent_two = call(
        functools.partial(first_kernel, places, count, then),
        "ham_first",
        [scalars] * 3 + [near] + [anywhere] * n + [far] * 2,
        [near, near, far],
        [wide_shape, pay_shape, jax.ShapeDtypeStruct((n_then, count, width, width), BF16)],
        [held, env, env, pltpu.VMEM((EXTRA, 128), F32), dma(n), dma(steps), dma(steps), dma(n_then)],
    )(offsets, mine, dims, table, *vrows, in_hbm(lenv), in_hbm(renv))

    rpieces = gathered(rpay)
    gone, sums, tables, vsrc, wsrc = call(
        functools.partial(second_kernel, places, count, cells, secs, late, used),
        "ham_second",
        [scalars] * 3 + [anywhere] * (2 * n) + [far] * 2,
        [near] * 5,
        [wide_shape, row_shape, jax.ShapeDtypeStruct((2, 8, 128), jnp.int32), used_shape, used_shape],
        [
            held, held, env, env, pltpu.VMEM((nblk * EXTRA, 128), F32),
            dma(n), dma(n), dma(steps), dma(steps),
        ],
    )(offsets, mine, dims, *vrows, *[rows for rows, _, _ in rpieces], in_hbm(lenv), in_hbm(renv))

    sent_two = onward(sent_two)
    parts = lax.all_gather(sums, "blk", axis=0)
    most_needed = sums[4, 0].astype(jnp.int32)
    table, table_before = tables[0], tables[1]

    most = count * n_late * width + SLACK
    out_shape = jax.ShapeDtypeStruct(by_group.shape, BF16)
    per = step_of(count, PACK_STEP)

    def finish(rows):
        def branch(parts, hzero, gone, vsrc, wsrc, sent_one, sent_two, table, table_before):
            passed, coefs = call(
                functools.partial(ritz_kernel, count, cells),
                "ritz",
                [scalars] + [near] * 3,
                [near] * 2,
                [jax.ShapeDtypeStruct((body, width), BF16), row_shape],
            )(ranks, parts, vsrc, wsrc)
            passed = onward(passed)
            packed = call(
                functools.partial(pack_kernel, count, late, used),
                "pack_update",
                [scalars] + [near] * 3 + [far],
                near,
                jax.ShapeDtypeStruct((rows, width), BF16),
                [
                    pltpu.VMEM((n_late, count, width, width), BF16),
                    pltpu.VMEM((per, n_late + 2, width, width), F32),
                    dma(len(late), count // per),
                ],
                moved=400 * 1024 * 1024,
            )(table, coefs, vsrc, wsrc, in_hbm(by_group))
            arrived = onward(packed)
            kpieces = gathered(passed)
            rows_two, coefs = lax.optimization_barrier((kpieces[2][0], coefs))
            kpieces[2] = (rows_two, *kpieces[2][1:])
            from_v, from_w, ritz = coefs[0, 0], coefs[1, 0], coefs[2, 0]
            state_new = (from_v * vsrc[0].astype(F32) + from_w * wsrc[0].astype(F32)).astype(BF16)
            hstate_new = (from_v * hzero + from_w * gone).astype(BF16)
            so_far = call(
                functools.partial(early_kernel, places, count, early),
                "early_update",
                [scalars] * 3 + [anywhere] * n + [far] * 3,
                far,
                out_shape,
                [
                    held,
                    pltpu.VMEM((n_early, count, width, width), BF16),
                    pltpu.VMEM((n_early, count, width, width), BF16),
                    dma(n),
                    dma(2),
                    dma(len(early) * count),
                ],
            )(table_before, mine, first_sec, *[r for r, _, _ in kpieces], in_hbm(sent_one), in_hbm(sent_two), in_hbm(by_group))
            next_left = call(
                functools.partial(unpack_kernel, count, late),
                "unpack_update",
                [scalars] * 2 + [near] + [far] * 2,
                far,
                out_shape,
                [pltpu.VMEM((n_late, count, width, width), BF16), dma(len(late) * count)],
                {4: 0},
            )(table_before, first_sec, arrived, in_hbm(by_group), in_hbm(so_far))
            return state_new, hstate_new, ritz, next_left

        return branch

    sizes = [most * part // 64 // 16 * 16 for part in (28, 32)] + [most]
    tier = sum((most_needed + SLACK > size).astype(jnp.int32) for size in sizes[:-1])
    state_new, hstate_new, ritz, next_left = lax.switch(
        tier, [finish(size) for size in sizes], parts, hzero, gone, vsrc, wsrc, sent_one, sent_two, table, table_before
    )
    next_left = next_left.reshape((channels, count, width, width))
    return (state_new[None], hstate_new[None], jnp.reshape(ritz, (1,)), next_left[None])


def solution(mesh):
    placed = (
        P("sec", "blk", None, None),
        P("sec", None, "blk", None, None),
        P("sec", None, "blk", None, None),
        P("sec", None),
        P("sec", "blk", None),
        P("sec", "blk"),
    )
    return jax.shard_map(
        shards,
        mesh=mesh,
        in_specs=placed,
        out_specs=(
            P("sec", "blk", None, None),
            P("sec", "blk", None, None),
            P("sec"),
            P("sec", None, "blk", None, None),
        ),
        check_vma=False,
    )
```
